128 devices in a mesh: gx: 4 (over x), gy: 32 (over z, y, core).
Axes of the slice: x: 4, y: 4, z: 4, core: 2. Of those that a mesh axis runs over, the one named last changes fastest.
Arguments:
- fine_pop: float32 [512, 19, 4096], P(('gx', 'gy')), may hold values from 0 to 1, as said below
- coarse_pop: float32 [256, 19, 4096], P(('gx', 'gy')), may hold values from 0 to 1, as said below
- fine_nbr: int32 [512, 4], P(('gx', 'gy')), may hold values from -1 to 511, as said below
- coarse_nbr: int32 [256, 6], P(('gx', 'gy')), may hold values from -1 to 255, as said below
- parent: int32 [512, 2], P(('gx', 'gy')), may hold values from 0 to 255, as said below
- children: int32 [256, 4], P(('gx', 'gy')), may hold values from -1 to 511, as said below
- solid: int32 [512, 4096], P(('gx', 'gy')), may hold values from 0 to 1, as said below
Outputs:
- fine_out: float32 [512, 19, 4096], P(('gx', 'gy'))
- coarse_out: float32 [256, 19, 4096], P(('gx', 'gy'))
The draws below stay inside these ranges and needn't reach their ends.
Inputs may be any that keep to these rules, and one draw needn't show every extreme that they name: `fine_pop`: positive populations. `coarse_pop`: positive populations. `fine_nbr`: -1 where the neighbouring position holds no fine block. A neighbour is held by the same device as the block or by the device just before or after it along gx+gy. The fine blocks form one layer along z. `coarse_nbr`: -1 where the neighbouring position holds no coarse block. A neighbour is held by the same device as the block or by the device just before or after it along gx+gy. Column 0 is the parent's coarse block, column 1 the quadrant 2 qy + qx; every child lies in the lower half of its parent along z. A fine block and its parent are held by devices of the same aligned group of four consecutive devices along gx+gy. children[c,q] = f exactly when parent[f] = (c, q), else -1. `solid`: the outermost layer of cells of every block is 0.
All inputs are finite; a program needn't handle non-finite values.
Results may differ from the reference program's by a relative error of at most 0.0001.
Values sent between devices are 32-bit elements; how exact they have to be, the bound alone decides.
No kernel may reach another device: no remote copies, remote signals or barrier semaphores. Data moves between devices by JAX's collectives and lax.ppermute only.
A program may use at most 128 MiB of HBM per device.

```python
import jax
import jax.numpy as jnp
from jax import lax

S = 16
FB = 4
NF = 512
NC = 256


WEIGHTS = (1.0 / 3.0,) + (1.0 / 18.0,) * 6 + (1.0 / 36.0,) * 12


def lookup(table, position, allowed):
    safe = jnp.clip(position, 0, table.shape[0] - 1)
    return jnp.where(allowed, table[safe], -1).astype(jnp.int32)


def lattice(key):
    groups = NF // (4 * FB)
    wide_fine = FB // 2
    wide_coarse = FB // 4
    fine_keys = jax.random.split(jax.random.fold_in(key, 101), groups)
    coarse_keys = jax.random.split(jax.random.fold_in(key, 202), groups)
    fine_perm = jax.vmap(lambda k: jax.random.permutation(k, 5 * FB))(fine_keys)
    fine_occ = (fine_perm >= FB).reshape(-1).astype(jnp.int32)
    upper_perm = jax.vmap(lambda k: jax.random.permutation(k, 5 * wide_coarse))(coarse_keys)
    upper = (upper_perm >= FB // 2).reshape((groups, 5, 1, wide_coarse)).astype(jnp.int32)
    lower = jnp.ones((groups, 5, 1, wide_coarse), jnp.int32)
    coarse_occ = jnp.concatenate([lower, upper], axis=2).reshape(-1)
    fine_slot = jnp.where(fine_occ > 0, jnp.cumsum(fine_occ) - 1, -1).astype(jnp.int32)
    coarse_slot = jnp.where(coarse_occ > 0, jnp.cumsum(coarse_occ) - 1, -1).astype(jnp.int32)
    fine_len = fine_occ.shape[0]
    coarse_len = coarse_occ.shape[0]
    fine_pos = jnp.argsort((1 - fine_occ) * fine_len + jnp.arange(fine_len))[:NF].astype(jnp.int32)
    coarse_pos = jnp.argsort((1 - coarse_occ) * coarse_len + jnp.arange(coarse_len))[:NC].astype(jnp.int32)
    rows_fine = 10 * groups
    rows_coarse = 5 * groups
    fine_row = fine_pos // wide_fine
    fine_col = fine_pos % wide_fine
    fine_nbr = jnp.stack([lookup(fine_slot, fine_pos - 1, fine_col > 0), lookup(fine_slot, fine_pos + 1, fine_col < wide_fine - 1), lookup(fine_slot, fine_pos - wide_fine, fine_row > 0), lookup(fine_slot, fine_pos + wide_fine, fine_row < rows_fine - 1)], axis=1)
    parent_pos = fine_row // 2 * 2 * wide_coarse + fine_col // 2
    parent = jnp.stack([coarse_slot[parent_pos], fine_row % 2 * 2 + fine_col % 2], axis=1).astype(jnp.int32)
    coarse_col = coarse_pos % wide_coarse
    coarse_lay = coarse_pos // wide_coarse % 2
    coarse_row = coarse_pos // (2 * wide_coarse)
    coarse_nbr = jnp.stack([lookup(coarse_slot, coarse_pos - 1, coarse_col > 0), lookup(coarse_slot, coarse_pos + 1, coarse_col < wide_coarse - 1), lookup(coarse_slot, coarse_pos - 2 * wide_coarse, coarse_row > 0), lookup(coarse_slot, coarse_pos + 2 * wide_coarse, coarse_row < rows_coarse - 1), lookup(coarse_slot, coarse_pos - wide_coarse, coarse_lay == 1), lookup(coarse_slot, coarse_pos + wide_coarse, coarse_lay == 0)], axis=1)
    child_cols = []
    for row_half in range(2):
        for col_half in range(2):
            spot = (2 * coarse_row + row_half) * wide_fine + 2 * coarse_col + col_half
            child_cols.append(lookup(fine_slot, spot, coarse_lay == 0))
    children = jnp.stack(child_cols, axis=1)
    return (fine_nbr, coarse_nbr, parent, children)


def draw_fine_nbr(key, part):
    shared = lattice(key)
    return shared[0]


def draw_coarse_nbr(key, part):
    shared = lattice(key)
    return shared[1]


def draw_parent(key, part):
    shared = lattice(key)
    return shared[2]


def draw_children(key, part):
    shared = lattice(key)
    return shared[3]


def draw_solid(key, part):
    key = jax.random.fold_in(key, 5)
    heights = jax.random.randint(key, (NF, 1, S, S), 1, S // 2 + 1)
    depth = jnp.arange(S).reshape((1, S, 1, 1))
    across = jnp.arange(S)
    inner_y = ((across >= 1) & (across <= S - 2)).reshape((1, 1, S, 1))
    inner_x = ((across >= 1) & (across <= S - 2)).reshape((1, 1, 1, S))
    solid = (depth >= 1) & (depth < heights) & inner_y & inner_x
    return solid.reshape((NF, S ** 3)).astype(jnp.int32)


def draw_fine_pop(key, part):
    key = jax.random.fold_in(key, 7)
    weight = jnp.array(WEIGHTS, jnp.float32).reshape((1, 19, 1))
    noise = 0.25 * jax.random.truncated_normal(key, -3.0, 3.0, (NF, 19, S ** 3), jnp.float32)
    return (weight * (1.0 + noise)).astype(jnp.float32)


def draw_coarse_pop(key, part):
    key = jax.random.fold_in(key, 9)
    weight = jnp.array(WEIGHTS, jnp.float32).reshape((1, 19, 1))
    noise = 0.25 * jax.random.truncated_normal(key, -3.0, 3.0, (NC, 19, S ** 3), jnp.float32)
    return (weight * (1.0 + noise)).astype(jnp.float32)


def setup_inputs(seed: int = 0) -> dict:
    key_list = jax.random.split(jax.random.key(seed), 8)
    return {
        "fine_pop": draw_fine_pop(jax.random.fold_in(key_list[7], 71), 0),
        "coarse_pop": draw_coarse_pop(jax.random.fold_in(key_list[7], 71), 0),
        "fine_nbr": draw_fine_nbr(jax.random.fold_in(key_list[7], 71), 0),
        "coarse_nbr": draw_coarse_nbr(jax.random.fold_in(key_list[7], 71), 0),
        "parent": draw_parent(jax.random.fold_in(key_list[7], 71), 0),
        "children": draw_children(jax.random.fold_in(key_list[7], 71), 0),
        "solid": draw_solid(jax.random.fold_in(key_list[7], 71), 0),
    }


VELOCITIES = ((0, 0, 0), (1, 0, 0), (-1, 0, 0), (0, 1, 0), (0, -1, 0), (0, 0, 1), (0, 0, -1),
              (1, 1, 0), (-1, -1, 0), (1, -1, 0), (-1, 1, 0), (1, 0, 1), (-1, 0, -1), (1, 0, -1),
              (-1, 0, 1), (0, 1, 1), (0, -1, -1), (0, 1, -1), (0, -1, 1))
WEIGHTS = (1.0 / 3.0,) + (1.0 / 18.0,) * 6 + (1.0 / 36.0,) * 12
OPPOSITE = (0, 2, 1, 4, 3, 6, 5, 8, 7, 10, 9, 12, 11, 14, 13, 16, 15, 18, 17)
OMEGA_COARSE = 1.6
OMEGA_FINE = 1.0 / (2.0 * (1.0 / 1.6 - 0.5) + 0.5)


def collide(populations, relax_rate):
    kind = populations.dtype
    comp_x = jnp.array([v[0] for v in VELOCITIES], kind)[None, :, None]
    comp_y = jnp.array([v[1] for v in VELOCITIES], kind)[None, :, None]
    comp_z = jnp.array([v[2] for v in VELOCITIES], kind)[None, :, None]
    weight = jnp.array(WEIGHTS, kind)[None, :, None]
    density = jnp.sum(populations, axis=1, keepdims=True)
    vel_x = jnp.sum(populations * comp_x, axis=1, keepdims=True) / density
    vel_y = jnp.sum(populations * comp_y, axis=1, keepdims=True) / density
    vel_z = jnp.sum(populations * comp_z, axis=1, keepdims=True) / density
    square = vel_x * vel_x + vel_y * vel_y + vel_z * vel_z
    projection = comp_x * vel_x + comp_y * vel_y + comp_z * vel_z
    equilibrium = weight * density * (1.0 + 3.0 * projection + 4.5 * projection * projection - 1.5 * square)
    return populations - relax_rate * (populations - equilibrium)


def to_cube(populations):
    return populations.reshape((populations.shape[0], 19, S, S, S))


def clamp_ends(field, axis_dim):
    edge_size = field.shape[axis_dim]
    return jnp.concatenate([lax.slice_in_dim(field, 0, 1, axis=axis_dim), field,
                            lax.slice_in_dim(field, edge_size - 1, edge_size, axis=axis_dim)], axis=axis_dim)


def extend(block_field, low_index, high_index, outer_field, axis_dim):
    edge_size = block_field.shape[axis_dim]
    first_layer = lax.slice_in_dim(block_field, 0, 1, axis=axis_dim)
    last_layer = lax.slice_in_dim(block_field, edge_size - 1, edge_size, axis=axis_dim)
    low_rows = jnp.take(last_layer, jnp.maximum(low_index, 0), axis=0)
    high_rows = jnp.take(first_layer, jnp.maximum(high_index, 0), axis=0)
    mask_shape = (-1,) + (1,) * (block_field.ndim - 1)
    low_side = jnp.where((low_index >= 0).reshape(mask_shape), low_rows,
                         lax.slice_in_dim(outer_field, 0, 1, axis=axis_dim))
    high_side = jnp.where((high_index >= 0).reshape(mask_shape), high_rows,
                          lax.slice_in_dim(outer_field, edge_size - 1, edge_size, axis=axis_dim))
    return jnp.concatenate([low_side, block_field, high_side], axis=axis_dim)


def stream(widened):
    pieces = []
    for i in range(19):
        step_x, step_y, step_z = VELOCITIES[i]
        pieces.append(widened[:, i, 1 - step_z:1 - step_z + S, 1 - step_y:1 - step_y + S, 1 - step_x:1 - step_x + S])
    return jnp.stack(pieces, axis=1)


def bounce(passed, collided, previous, solid_cube):
    wall_cells = jnp.pad(solid_cube, ((0, 0), (1, 1), (1, 1), (1, 1)))
    pieces = []
    for i in range(19):
        step_x, step_y, step_z = VELOCITIES[i]
        from_wall = wall_cells[:, 1 - step_z:1 - step_z + S, 1 - step_y:1 - step_y + S, 1 - step_x:1 - step_x + S]
        pieces.append(jnp.where(from_wall, collided[:, OPPOSITE[i]], passed[:, i]))
    result = jnp.stack(pieces, axis=1)
    return jnp.where(solid_cube[:, None], previous, result)


def upsample(field):
    for axis_dim in (2, 3, 4):
        field = jnp.repeat(field, 2, axis=axis_dim)
    return field


def explode(coarse_pop, parent):
    half_edge = S // 2
    coarse_cube = to_cube(coarse_pop)
    octants = jnp.stack([coarse_cube[:, :, 0:half_edge, row_half * half_edge:(row_half + 1) * half_edge,
                                     col_half * half_edge:(col_half + 1) * half_edge]
                         for row_half in range(2) for col_half in range(2)], axis=1)
    octants = octants.reshape((-1, 19, half_edge, half_edge, half_edge))
    picked = jnp.take(octants, parent[:, 0] * 4 + parent[:, 1], axis=0)
    return upsample(picked)


def fine_step(populations, explode_cube, fine_nbr, solid_mask):
    block_count = populations.shape[0]
    solid_cube = solid_mask.reshape((block_count, S, S, S))
    collided = jnp.where(solid_mask[:, None, :], populations, collide(populations, OMEGA_FINE))
    post_cube = to_cube(collided)
    widened = extend(post_cube, fine_nbr[:, 0], fine_nbr[:, 1], explode_cube, 4)
    outer_field = clamp_ends(explode_cube, 4)
    widened = extend(widened, fine_nbr[:, 2], fine_nbr[:, 3], outer_field, 3)
    outer_field = clamp_ends(outer_field, 3)
    widened = jnp.concatenate([outer_field[:, :, :1], widened, outer_field[:, :, -1:]], axis=2)
    result = bounce(stream(widened), post_cube, to_cube(populations), solid_cube)
    return result.reshape(populations.shape)


def coarse_step(coarse_pop, coarse_nbr):
    post_cube = to_cube(collide(coarse_pop, OMEGA_COARSE))
    widened = extend(post_cube, coarse_nbr[:, 0], coarse_nbr[:, 1], post_cube, 4)
    widened = extend(widened, coarse_nbr[:, 2], coarse_nbr[:, 3], widened, 3)
    widened = extend(widened, coarse_nbr[:, 4], coarse_nbr[:, 5], widened, 2)
    return stream(widened)


def coalesce(passed, fine_final, children):
    half_edge = S // 2
    fine_cube = to_cube(fine_final)
    child_means = fine_cube.reshape((fine_cube.shape[0], 19, half_edge, 2, half_edge, 2, half_edge, 2))
    child_means = child_means.sum(axis=(3, 5, 7)) * 0.125
    for q in range(4):
        row_half, col_half = q // 2, q % 2
        child_slot = children[:, q]
        values = jnp.take(child_means, jnp.maximum(child_slot, 0), axis=0)
        region = passed[:, :, 0:half_edge, row_half * half_edge:(row_half + 1) * half_edge,
                          col_half * half_edge:(col_half + 1) * half_edge]
        merged = jnp.where((child_slot >= 0)[:, None, None, None, None], values, region)
        passed = passed.at[:, :, 0:half_edge, row_half * half_edge:(row_half + 1) * half_edge,
                               col_half * half_edge:(col_half + 1) * half_edge].set(merged)
    return passed


def reference(fine_pop, coarse_pop, fine_nbr, coarse_nbr, parent, children, solid):
    explode_cube = explode(coarse_pop, parent)
    solid_mask = solid > 0
    populations = fine_pop
    for substep in range(2):
        populations = fine_step(populations, explode_cube, fine_nbr, solid_mask)
    passed = coarse_step(coarse_pop, coarse_nbr)
    coarse_new = coalesce(passed, populations, children)
    return populations, coarse_new.reshape(coarse_pop.shape)
```

```python
import functools

import jax
import jax.numpy as jnp
from jax import lax
from jax.experimental import pallas as pl
from jax.experimental.pallas import tpu as pltpu
from jax.sharding import PartitionSpec as P

AXES = ("gx", "gy")
VELOCITIES = (
    (0, 0, 0),
    (1, 0, 0),
    (-1, 0, 0),
    (0, 1, 0),
    (0, -1, 0),
    (0, 0, 1),
    (0, 0, -1),
    (1, 1, 0),
    (-1, -1, 0),
    (1, -1, 0),
    (-1, 1, 0),
    (1, 0, 1),
    (-1, 0, -1),
    (1, 0, -1),
    (-1, 0, 1),
    (0, 1, 1),
    (0, -1, -1),
    (0, 1, -1),
    (0, -1, 1),
)
WEIGHTS = (1.0 / 3.0,) + (1.0 / 18.0,) * 6 + (1.0 / 36.0,) * 12
OPPOSITE = (0, 2, 1, 4, 3, 6, 5, 8, 7, 10, 9, 12, 11, 14, 13, 16, 15, 18, 17)
OMEGA_COARSE = 1.6
OMEGA_FINE = 1.0 / (2.0 * (1.0 / 1.6 - 0.5) + 0.5)

XP = (1, 7, 9, 11, 13)
XM = (2, 8, 10, 12, 14)
YP = (3, 7, 10, 15, 17)
YM = (4, 8, 9, 16, 18)
ZP = (5, 11, 14, 15, 18)
ZM = (6, 12, 13, 16, 17)
YP1, YM1 = (3, 15, 17), (4, 16, 18)
YP2, YM2 = (7, 10), (8, 9)
ZP2, ZM2 = (11, 14, 15, 18), (12, 13, 16, 17)

R = 32
BLOCK = 19 * R
FB, CB = 4, 2
EDGES = FB * 64
META = EDGES + R
F_ROWS = META + 8
E_BLOCK = 96
EC_AT = CB * E_BLOCK
E_ROWS = EC_AT + 8
C1_BLOCK = 72
C1_ROWS = CB * C1_BLOCK
C2_BLOCK = 64
C2_ROWS = CB * C2_BLOCK
K_ROWS = 2 * 19 * 8
EZ_BLOCK = 80
HALO = 3 * (META) + FB * 64


def iotas(rows=R):
    row = lax.broadcasted_iota(jnp.int32, (rows, 128), 0)
    lane = lax.broadcasted_iota(jnp.int32, (rows, 128), 1)
    return row, lane


def roll(a, shift, axis):
    if isinstance(shift, int):
        shift = shift % a.shape[axis]
        if shift == 0:
            return a
    return pltpu.roll(a, shift, axis)


def at(ref, start, size=R):
    if not isinstance(start, int):
        start = pl.multiple_of(start, 8)
    return ref[pl.ds(start, size), :]


def put(ref, start, value):
    if not isinstance(start, int):
        start = pl.multiple_of(start, 8)
    ref[pl.ds(start, value.shape[0]), :] = value


def rows_in(src, dst, blocks):
    def body(b, carry):
        for t, n in ((0, 8), (1, 8), (2, 3)):
            for r in range(R):
                dst[pl.ds(b * BLOCK + t * 8 * R + r, n, stride=R), :] = src[
                    b, 8 * t : 8 * t + n, 128 * r : 128 * r + 128
                ]
        return carry

    lax.fori_loop(0, blocks, body, 0)


def rows_out(src, dst, blocks):
    def body(b, carry):
        for t, n in ((0, 8), (1, 8), (2, 3)):
            for r in range(R):
                dst[b, 8 * t : 8 * t + n, 128 * r : 128 * r + 128] = src[
                    pl.ds(b * BLOCK + t * 8 * R + r, n, stride=R), :
                ]
        return carry

    lax.fori_loop(0, blocks, body, 0)


def collide(f, rate):
    rho = functools.reduce(lambda a, b: a + b, f)
    mom = []
    for axis in range(3):
        plus = [f[i] for i in range(19) if VELOCITIES[i][axis] == 1]
        minus = [f[i] for i in range(19) if VELOCITIES[i][axis] == -1]
        mom.append(sum(plus[1:], plus[0]) - sum(minus[1:], minus[0]))
    inv = 1.0 / rho
    u = [m * inv for m in mom]
    base = 1.0 - 1.5 * (u[0] * u[0] + u[1] * u[1] + u[2] * u[2])
    scaled = {w: (rate * w) * rho for w in sorted(set(WEIGHTS))}
    keep = 1.0 - rate
    out = [None] * 19
    out[0] = keep * f[0] + scaled[WEIGHTS[0]] * base
    for i in range(1, 19, 2):
        proj = None
        for axis in range(3):
            c = VELOCITIES[i][axis]
            if c:
                term = u[axis]
                if proj is None:
                    proj = term if c > 0 else -term
                else:
                    proj = proj + term if c > 0 else proj - term
        even = base + 4.5 * (proj * proj)
        odd = 3.0 * proj
        w = scaled[WEIGHTS[i]]
        out[i] = keep * f[i] + w * (even + odd)
        out[i + 1] = keep * f[i + 1] + w * (even - odd)
    return out


def collide_rows(src, src_base, dst, dst_base, rate, mask, mask_base):
    def body(v, carry):
        f = [at(src, src_base + i * R + v * 8, 8) for i in range(19)]
        post = collide(f, rate)
        if mask is not None:
            solid = (at(mask, mask_base + v * 8, 8) & 1) > 0
            post = [jnp.where(solid, f[i], post[i]) for i in range(19)]
        for i in range(19):
            put(dst, dst_base + i * R + v * 8, post[i])
        return carry

    lax.fori_loop(0, 4, body, 0)


def pack_x(get):
    _, lane = iotas()
    x = lane & 15
    packed = jnp.zeros((R, 128), jnp.float32)
    for j in range(5):
        packed = jnp.where(x == j, roll(get(XP[j]), j - 15, 1), packed)
        packed = jnp.where(x == 5 + j, roll(get(XM[j]), 5 + j, 1), packed)
    return packed


def swap_rows(a):
    row, _ = iotas()
    return jnp.where((row & 1) == 0, roll(a, -1, 0), roll(a, 1, 0))


def pack_y(get, plus, minus):
    row, lane = iotas()
    upper = (row & 1) == 1
    packed = jnp.zeros((R, 128), jnp.float32)
    for p in range(len(plus)):
        one = jnp.where(upper, roll(get(plus[p]), 16 * p - 112, 1), roll(get(minus[p]), 16 * p, 1))
        packed = jnp.where((lane >> 4) == p, one, packed)
    return swap_rows(packed)


def pack_edges(get):
    row, lane = iotas()
    upper = (row & 1) == 1
    first = jnp.where(upper, roll(get(7), -127, 1), get(8))
    second = jnp.where(upper, roll(get(10), 1 - 112, 1), roll(get(9), 1 - 15, 1))
    return swap_rows(jnp.where(lane == 0, first, second))


def move_x(a, cx, halo):
    _, lane = iotas()
    x = lane & 15
    if cx == 1:
        return jnp.where(x == 0, halo, roll(a, 1, 1))
    return jnp.where(x == 15, halo, roll(a, -1, 1))


def move_y(a, cy, halo):
    row, lane = iotas()
    upper = (row & 1) == 1
    if cy == 1:
        near = roll(a, 16, 1)
        return jnp.where(lane < 16, jnp.where(upper, roll(near, 1, 0), halo), near)
    near = roll(a, -16, 1)
    return jnp.where(lane >= 112, jnp.where(upper, halo, roll(near, -1, 0)), near)


def move_z(a, cz, halo8):
    row, _ = iotas(8)
    if cz == 1:
        near = roll(a, 2, 0)
        return jnp.concatenate([jnp.where(row < 2, halo8, near[:8]), near[8:]], axis=0)
    near = roll(a, -2, 0)
    return jnp.concatenate([near[:24], jnp.where(row >= 6, halo8, near[24:])], axis=0)


def send_faces(get, out, b):
    put(out, b * 64, pack_x(get))
    put(out, b * 64 + R, pack_y(get, YP, YM))
    _, lane = iotas()
    edges = roll(pack_edges(get), 2 * b, 1)
    put(out, EDGES, jnp.where((lane >> 1) == b, edges, at(out, EDGES)))


def place():
    device = lax.axis_index("gx") * lax.axis_size("gy") + lax.axis_index("gy")
    sign = 1 - 2 * (device & 1)
    return device, sign


def coarse_first_kernel(pop, post, e_out, c_out, raw):
    rows_in(pop, raw, CB)
    _, lane = iotas(16)
    _, lane8 = iotas(8)
    x16 = lane & 15
    corner = jnp.zeros((8, 128), jnp.float32)
    for c in range(CB):
        base = c * BLOCK
        half = lambda i: at(raw, base + i * R, 16)
        for qx in range(2):
            packed = jnp.zeros((16, 128), jnp.float32)
            for j in range(5):
                packed = jnp.where(x16 == j, roll(half(XP[j]), j - 8 * qx, 1), packed)
                packed = jnp.where(x16 == 5 + j, roll(half(XM[j]), 5 + j - 8 * qx - 7, 1), packed)
            put(e_out, c * E_BLOCK + qx * 16, packed)
        low = jnp.zeros((16, 128), jnp.float32)
        high = jnp.zeros((16, 128), jnp.float32)
        for p in range(5):
            low = jnp.where((lane >> 4) == p, roll(half(YP[p]), 16 * p, 1), low)
            high = jnp.where((lane >> 4) == p, roll(half(YM[p]), 16 * p - 112, 1), high)
        put(e_out, c * E_BLOCK + 32, low)
        put(e_out, c * E_BLOCK + 48, high)
        put(e_out, c * E_BLOCK + 64, jnp.zeros((R, 128), jnp.float32))
        for k in range(5):
            e_out[pl.ds(c * E_BLOCK + 64 + 2 * k, 2), :] = raw[pl.ds(base + ZP[k] * R, 2), :]
            e_out[pl.ds(c * E_BLOCK + 74 + 2 * k, 2), :] = raw[pl.ds(base + ZM[k] * R + 14, 2), :]
        for q in range(4):
            for e, (i, yq, xq) in enumerate(((7, 7, 0), (10, 7, 7), (9, 0, 0), (8, 0, 7))):
                to = (c * 4 + q) * 4 + e
                rows = raw[pl.ds(base + i * R + q // 2, 8, stride=2), :]
                rows = roll(rows, to - (yq * 16 + 8 * (q % 2) + xq), 1)
                corner = jnp.where(lane8 == to, rows, corner)
    put(e_out, EC_AT, corner)
    row8, _ = iotas(8)
    for c in range(CB):
        base = c * BLOCK
        collide_rows(raw, base, post, base, OMEGA_COARSE, None, 0)
        get = lambda i: at(post, base + i * R)
        put(c_out, c * C1_BLOCK, pack_x(get))
        put(c_out, c * C1_BLOCK + R, pack_y(get, YP1, YM1))
        top = roll(at(post, base + 5 * R + 24, 8), 2, 0)
        bottom = roll(at(post, base + 6 * R, 8), 6, 0)
        put(c_out, c * C1_BLOCK + 2 * R, jnp.where(row8 < 2, top, bottom))


def fine_first_kernel(nbr, parent, pop, solid, post, mask, f_out, raw, sol):
    rows_in(pop, raw, FB)
    for r in range(R):
        sol[pl.ds(r, FB, stride=R), :] = solid[:, 128 * r : 128 * r + 128]
    put(f_out, EDGES, jnp.zeros((R, 128), jnp.float32))

    def body(b, carry):
        s = jnp.where(at(sol, b * R) > 0, 1, 0)
        bits = s
        for i in range(1, 19):
            cx, cy, cz = VELOCITIES[i]
            m = s
            if cx:
                m = roll(m, cx, 1)
            if cy:
                m = move_y(m, cy, jnp.zeros_like(m))
            if cz:
                m = roll(m, 2 * cz, 0)
            bits = bits | (m << i)
        put(mask, b * R, bits)
        base = b * BLOCK
        collide_rows(raw, base, post, base, OMEGA_FINE, mask, b * R)
        send_faces(lambda i: at(post, base + i * R), f_out, b)
        return carry

    lax.fori_loop(0, FB, body, 0)
    row, lane = iotas(8)
    meta = jnp.zeros((8, 128), jnp.float32)
    for b in range(FB):
        for k in range(4):
            meta = jnp.where((row == b) & (lane == k), nbr[b, k].astype(jnp.float32), meta)
        for k in range(2):
            meta = jnp.where((row == b) & (lane == 4 + k), parent[b, k].astype(jnp.float32), meta)
    put(f_out, META, meta)


def onehot(rows, cols, source):
    row = lax.broadcasted_iota(jnp.int32, (rows, cols), 0)
    col = lax.broadcasted_iota(jnp.int32, (rows, cols), 1)
    return jnp.where(row == source(col), 1.0, 0.0).astype(jnp.float32)


def exact_dot(a, b):
    return jnp.dot(a, b, preferred_element_type=jnp.float32, precision=lax.Precision.HIGHEST)


def expand(parent, device, gathered, halo, ez):
    _, lane = iotas(16)
    row, _ = iotas(16)
    x = lane & 15
    spread_x = onehot(
        128, 256, lambda m: ((m >> 7) * 4 + ((m & 127) >> 5)) * 16 + (m & 15)
    )

    def body(b, carry):
        p, q = parent[b, 0], parent[b, 1]
        qy, qx = q >> 1, q & 1
        base = ((p >> 1) ^ device) * E_ROWS + (p & 1) * E_BLOCK
        home = 3 * META + b * 64
        ex = exact_dot(gathered[pl.ds(base + qx * 16 + qy, 8, stride=2), :], spread_x)
        spread_y = onehot(128, 128, lambda m: (m >> 4) * 16 + 8 * qx + ((m & 15) >> 1))
        ey0 = exact_dot(gathered[pl.ds(base + 32 + qy, 8, stride=2), :], spread_y)
        ey1 = exact_dot(gathered[pl.ds(base + 48 + qy, 8, stride=2), :], spread_y)
        for k in range(2):
            halo[pl.ds(home + 2 * k, 8, stride=4), :] = ex[:, :128]
            halo[pl.ds(home + 2 * k + 1, 8, stride=4), :] = ex[:, 128:]
            halo[pl.ds(home + R + 2 * k, 8, stride=4), :] = ey0
            halo[pl.ds(home + R + 2 * k + 1, 8, stride=4), :] = ey1
        spread_z = onehot(
            128,
            256,
            lambda m: ((m >> 7) * 4 + ((m & 127) >> 5)) * 16 + 8 * qx + ((m & 15) >> 1),
        )
        ezs = exact_dot(gathered[pl.ds(base + 64 + qy, 16, stride=2), :], spread_z)
        a0, a1 = ezs[:, :128], ezs[:, 128:]
        moves = {}
        moves[0, 0] = (a0, a1)
        moves[1, 0] = tuple(jnp.where(x == 0, a, roll(a, 1, 1)) for a in (a0, a1))
        moves[-1, 0] = tuple(jnp.where(x == 15, a, roll(a, -1, 1)) for a in (a0, a1))
        moves[0, 1] = (
            jnp.where(lane < 16, a0, roll(a0, 16, 1)),
            jnp.where(lane < 16, roll(a0, 16, 1), roll(a1, 16, 1)),
        )
        moves[0, -1] = (
            jnp.where(lane >= 112, roll(a1, -16, 1), roll(a0, -16, 1)),
            jnp.where(lane >= 112, a1, roll(a1, -16, 1)),
        )
        out = [a0, a1]
        for k, i in enumerate(ZP + ZM):
            moved = moves[VELOCITIES[i][:2]]
            out = [jnp.where(row == k, moved[h], out[h]) for h in range(2)]
        for h in range(2):
            for k in range(5):
                ez[pl.ds(b * EZ_BLOCK + 8 * k + h, 1), :] = out[h][k : k + 1]
                ez[pl.ds(b * EZ_BLOCK + 40 + 8 * k + 6 + h, 1), :] = out[h][5 + k : 6 + k]
        return carry

    lax.fori_loop(0, FB, body, 0)


def gather_halo(own, x_in, n_in, x_late, relayed, halo, edges):
    for k, ref in enumerate((n_in, own, x_in)):
        put(halo, k * META, ref[0:META, :])
        put(edges, (k + 1) * R, ref[EDGES : EDGES + R, :])
    put(edges, 0, n_in[pl.ds(relayed, R), :])
    put(edges, 4 * R, x_late[...])


def corners(nbr, meta_n, meta_own, meta_x, device, sign, halo, edges, fixed, b):
    row, lane = iotas()
    upper = (row & 1) == 1
    result = jnp.zeros((R, 128), jnp.float32)
    for side in range(2):
        n = nbr[b, 2 + side]
        safe = jnp.maximum(n, 0)
        which = ((safe >> 2) - device) * sign + 1
        which = jnp.clip(which, 0, 2)
        row_n = safe & 3
        for end in range(2):
            i = ((7, 10), (9, 8))[side][end]
            p = (YP, YM)[side].index(i)
            edge_col = ((0, 1), (1, 0))[side][end]
            to = 112 * side + 15 * end
            m = jnp.where(
                which == 0,
                meta_n[row_n, end],
                jnp.where(which == 1, meta_own[row_n, end], meta_x[row_n, end]),
            ).astype(jnp.int32)
            m_safe = jnp.maximum(m, 0)
            slot = jnp.clip(((m_safe >> 2) - device) * sign + 2, 0, 4)
            shift = (to - (2 * (m_safe & 3) + edge_col)) & 127
            sent = roll(at(edges, slot * R), shift, 1)
            own = roll(at(halo, 3 * META + b * 64 + R), to - (16 * p + 15 * end), 1)
            value = jnp.where(n < 0, own, jnp.where(m >= 0, sent, at(fixed, b * R)))
            here = (lane == to) & (upper if side else jnp.logical_not(upper))
            result = jnp.where(here, value, result)
    return result


def fixed_corners(nbr, meta_n, meta_own, meta_x, device, sign, group, from_n, fixed, spare):
    _, lane = iotas()
    npart = device - sign

    def body(b, carry):
        result = jnp.zeros((R, 128), jnp.float32)
        for side in range(2):
            safe = jnp.maximum(nbr[b, 2 + side], 0)
            which = jnp.clip(((safe >> 2) - device) * sign + 1, 0, 2)
            row_n = safe & 3
            pq = [
                jnp.where(
                    which == 0,
                    meta_n[row_n, 4 + k],
                    jnp.where(which == 1, meta_own[row_n, 4 + k], meta_x[row_n, 4 + k]),
                ).astype(jnp.int32)
                for k in range(2)
            ]
            p, q = pq
            near = ((p >> 1) ^ device) & 3
            far = ((p >> 1) ^ npart) & 3
            quad = jnp.where(
                which == 0, at(from_n, far * 8, 8), at(group, near * E_ROWS + EC_AT, 8)
            )
            for k in range(4):
                spare[pl.ds(k, 8, stride=4), :] = quad
            rows = spare[...]
            for end in range(2):
                to = 112 * side + 15 * end
                source = ((p & 1) * 4 + q) * 4 + 2 * side + end
                result = jnp.where(lane == to, roll(rows, (to - source) & 127, 1), result)
        put(fixed, b * R, result)
        return carry

    lax.fori_loop(0, FB, body, 0)


def stream_fine(nbr, device, sign, post, mask, halo, ez, corner, dst, dst_base, b):
    base = b * BLOCK
    bits = at(mask, b * R)
    faces = []
    for k in range(4):
        n = nbr[b, k]
        safe = jnp.maximum(n, 0)
        which = jnp.clip(((safe >> 2) - device) * sign + 1, 0, 2)
        start = jnp.where(n >= 0, which * META + (safe & 3) * 64, 3 * META + b * 64)
        faces.append(at(halo, start + (R if k >= 2 else 0)))
    row, lane = iotas()
    solid = (bits & 1) > 0
    for i in range(19):
        cx, cy, cz = VELOCITIES[i]
        a = at(post, base + i * R)
        if i == 0:
            put(dst, dst_base, a)
            continue
        g = a
        if cx == 1:
            g = move_x(g, 1, roll(faces[0], -XP.index(i), 1))
        elif cx == -1:
            g = move_x(g, -1, roll(faces[1], 10 - XM.index(i), 1))
        if cy:
            first = 112 * (cy == -1)
            p = (YP if cy == 1 else YM).index(i)
            side = roll(faces[2 if cy == 1 else 3], first - 16 * p + cx, 1)
            if cx:
                side = jnp.where(lane == first + (0 if cx == 1 else 15), corner, side)
            g = move_y(g, cy, side)
        if cz:
            k = ZP.index(i) if cz == 1 else 5 + ZM.index(i)
            g = move_z(g, cz, at(ez, b * EZ_BLOCK + 8 * k, 8))
        from_wall = (bits & (1 << i)) > 0
        g = jnp.where(from_wall, at(post, base + OPPOSITE[i] * R), g)
        put(dst, dst_base + i * R, jnp.where(solid, a, g))


def fetch_meta(pairs, sem):
    copies = [
        pltpu.make_async_copy(ref.at[pl.ds(META, 8)], dst, sem.at[k])
        for k, (ref, dst) in enumerate(pairs)
    ]
    for c in copies:
        c.start()
    return copies


X_E = F_ROWS
X_E2 = X_E + E_ROWS
X_C = X_E2 + E_ROWS
X_ROWS = X_C + C1_ROWS
N_EDGE = F_ROWS
N_EC = N_EDGE + R
N_C = N_EC + 4 * 8
N_ROWS = N_C + C1_ROWS


def coarse_source(index, device, sign):
    safe = jnp.maximum(index, 0)
    which = jnp.clip(((safe >> 1) - device) * sign + 1, 0, 2)
    return which, safe & 1


def middle_kernel(
    nbr,
    parent,
    cnbr,
    post,
    mask,
    f_own,
    e_own,
    e_two,
    x_in,
    n_in,
    x_late,
    cpost,
    c_own,
    post2,
    f_out,
    e_halo,
    ez,
    fixed,
    cmid,
    c_out,
    gathered,
    halo,
    edges,
    spare,
    new,
    chalo,
    meta_n,
    meta_own,
    meta_x,
    sem,
):
    device, sign = place()
    copies = fetch_meta(((n_in, meta_n), (f_own, meta_own), (x_in, meta_x)), sem)
    put(gathered, 0, e_own[...])
    put(gathered, E_ROWS, x_in[X_E : X_E + E_ROWS, :])
    put(gathered, 2 * E_ROWS, e_two[...])
    put(gathered, 3 * E_ROWS, x_in[X_E2 : X_E2 + E_ROWS, :])
    expand(parent, device, gathered, halo, ez)
    put(e_halo, 0, halo[3 * META : HALO, :])
    gather_halo(f_own, x_in, n_in, x_late, N_EDGE, halo, edges)
    for c in copies:
        c.wait()
    fixed_corners(
        nbr,
        meta_n,
        meta_own,
        meta_x,
        device,
        sign,
        gathered,
        n_in.at[pl.ds(N_EC, 32)],
        fixed,
        spare,
    )
    put(f_out, EDGES, jnp.zeros((R, 128), jnp.float32))
    put(f_out, META, jnp.zeros((8, 128), jnp.float32))

    def body(b, carry):
        corner = corners(nbr, meta_n, meta_own, meta_x, device, sign, halo, edges, fixed, b)
        stream_fine(nbr, device, sign, post, mask, halo, ez, corner, new, 0, b)
        base = b * BLOCK
        collide_rows(new, 0, post2, base, OMEGA_FINE, mask, b * R)
        send_faces(lambda i: at(post2, base + i * R), f_out, b)
        return carry

    lax.fori_loop(0, FB, body, 0)

    put(chalo, 0, n_in[N_C : N_C + C1_ROWS, :])
    put(chalo, C1_ROWS, c_own[...])
    put(chalo, 2 * C1_ROWS, x_in[X_C : X_C + C1_ROWS, :])
    row8, _ = iotas(8)

    def coarse_body(c, carry):
        base = c * BLOCK
        has, sources = [], []
        for k in range(6):
            which, slot = coarse_source(cnbr[c, k], device, sign)
            has.append(cnbr[c, k] >= 0)
            sources.append(which * C1_ROWS + slot * C1_BLOCK)
        faces = [at(chalo, sources[k] + (0 if k < 2 else R)) for k in range(4)]
        zs = [at(chalo, sources[k] + 2 * R, 8) for k in (4, 5)]
        put(cmid, base, at(cpost, base))
        for i in range(1, 19):
            cx, cy, cz = VELOCITIES[i]
            a = at(cpost, base + i * R)
            if cx == 1:
                g = move_x(a, 1, jnp.where(has[0], roll(faces[0], -XP.index(i), 1), a))
            elif cx == -1:
                g = move_x(a, -1, jnp.where(has[1], roll(faces[1], 10 - XM.index(i), 1), a))
            elif cy == 1:
                side = roll(faces[2], -16 * YP1.index(i), 1)
                g = move_y(a, 1, jnp.where(has[2], side, a))
            elif cy == -1:
                side = roll(faces[3], 112 - 16 * YM1.index(i), 1)
                g = move_y(a, -1, jnp.where(has[3], side, a))
            elif cz == 1:
                g = move_z(a, 1, jnp.where(has[4], zs[0], a[:8]))
            else:
                g = move_z(a, -1, jnp.where(has[5], zs[1], a[24:]))
            put(cmid, base + i * R, g)
        get = lambda i: at(cmid, base + i * R)
        put(c_out, c * C2_BLOCK, pack_y(get, YP2, YM2))
        for k in range(4):
            top = roll(at(cmid, base + ZP2[k] * R + 24, 8), 2, 0)
            bottom = roll(at(cmid, base + ZM2[k] * R, 8), 6, 0)
            put(c_out, c * C2_BLOCK + R + 8 * k, jnp.where(row8 < 2, top, bottom))
        return carry

    lax.fori_loop(0, CB, coarse_body, 0)


X2_C = F_ROWS
N2_EDGE = F_ROWS
N2_C = N2_EDGE + R


def fine_last_kernel(
    nbr,
    cnbr,
    post,
    mask,
    f_own,
    x_in,
    n_in,
    x_late,
    e_halo,
    ez,
    fixed,
    f_first,
    x_first,
    n_first,
    cmid,
    c_own,
    fine_out,
    means,
    cpassed,
    halo,
    edges,
    new,
    summed,
    chalo,
    meta_n,
    meta_own,
    meta_x,
    sem,
):
    device, sign = place()
    copies = fetch_meta(((n_first, meta_n), (f_first, meta_own), (x_first, meta_x)), sem)
    gather_halo(f_own, x_in, n_in, x_late, N2_EDGE, halo, edges)
    put(halo, 3 * META, e_halo[...])
    for c in copies:
        c.wait()

    def body(b, carry):
        corner = corners(nbr, meta_n, meta_own, meta_x, device, sign, halo, edges, fixed, b)
        stream_fine(nbr, device, sign, post, mask, halo, ez, corner, new, b * BLOCK, b)
        return carry

    lax.fori_loop(0, FB, body, 0)
    rows_out(new, fine_out, FB)

    row = lax.broadcasted_iota(jnp.int32, (128, 128), 0)
    col = lax.broadcasted_iota(jnp.int32, (128, 128), 1)
    target = lambda yh, h: (yh * 4 + (row >> 5)) * 16 + ((row & 15) >> 1) + 8 * h
    mats = [
        [jnp.where(col == target(yh, h), 0.125, 0.0).astype(jnp.float32) for yh in range(2)]
        for h in range(2)
    ]
    rows = 19 * 8
    for pair in range(2):
        total = None
        for h in range(2):
            b = 2 * pair + h
            for yh in range(2):
                z0 = new[pl.ds(b * BLOCK + yh, rows, stride=4), :]
                z1 = new[pl.ds(b * BLOCK + 2 + yh, rows, stride=4), :]
                part = exact_dot(z0 + z1, mats[h][yh])
                total = part if total is None else total + part
        put(means, pair * rows, total)

    put(chalo, 0, n_in[N2_C : N2_C + C2_ROWS, :])
    put(chalo, C2_ROWS, c_own[...])
    put(chalo, 2 * C2_ROWS, x_in[X2_C : X2_C + C2_ROWS, :])

    def coarse_body(c, carry):
        base = c * BLOCK
        has, sources = [], []
        for k in range(6):
            which, slot = coarse_source(cnbr[c, k], device, sign)
            has.append(cnbr[c, k] >= 0)
            sources.append(which * C2_ROWS + slot * C2_BLOCK)
        faces = [at(chalo, sources[k]) for k in (2, 3)]
        for i in range(19):
            a = at(cmid, base + i * R)
            g = a
            if i in YP2:
                g = move_y(a, 1, jnp.where(has[2], roll(faces[0], -16 * YP2.index(i), 1), a))
            elif i in YM2:
                side = roll(faces[1], 112 - 16 * YM2.index(i), 1)
                g = move_y(a, -1, jnp.where(has[3], side, a))
            elif i in ZP2:
                side = at(chalo, sources[4] + R + 8 * ZP2.index(i), 8)
                g = move_z(a, 1, jnp.where(has[4], side, a[:8]))
            elif i in ZM2:
                side = at(chalo, sources[5] + R + 8 * ZM2.index(i), 8)
                g = move_z(a, -1, jnp.where(has[5], side, a[24:]))
            put(cpassed, base + i * R, g)
        return carry

    lax.fori_loop(0, CB, coarse_body, 0)


def coarse_last_kernel(children, cpassed, own, two, x_in, coarse_out, merged, gathered):
    device, _ = place()
    put(gathered, 0, own[...])
    put(gathered, K_ROWS, x_in[0:K_ROWS, :])
    put(gathered, 2 * K_ROWS, two[...])
    put(gathered, 3 * K_ROWS, x_in[K_ROWS : 2 * K_ROWS, :])
    merged[...] = cpassed[...]
    _, lane = iotas(8)
    x_half = (lane >> 3) & 1

    def body(step, carry):
        c, q = step >> 2, step & 3
        qy, qx = q >> 1, q & 1
        child = children[c, q]

        @pl.when(child >= 0)
        def _():
            slot = ((child >> 2) ^ device) & 3
            start = slot * K_ROWS + ((child & 3) >> 1) * (19 * 8)
            shift = (8 * (qx - (child & 1))) & 127
            mine = x_half == qx
            for i in range(19):
                value = roll(at(gathered, start + 8 * i, 8), shift, 1)
                rows = pl.ds(c * BLOCK + i * R + qy, 8, stride=2)
                merged[rows, :] = jnp.where(mine, value, merged[rows, :])

        return carry

    lax.fori_loop(0, CB * 4, body, 0)
    rows_out(merged, coarse_out, CB)


VMEM = pl.BlockSpec(memory_space=pltpu.VMEM)
SMEM = pl.BlockSpec(memory_space=pltpu.SMEM)


def rows_of(n, dtype=jnp.float32):
    return jax.ShapeDtypeStruct((n, 128), dtype)


def scratch(n, dtype=jnp.float32):
    return pltpu.VMEM((n, 128), dtype)


def call(kernel, name, specs, outs, scratches):
    return pl.pallas_call(
        kernel,
        name=name,
        in_specs=specs,
        out_specs=[VMEM] * len(outs),
        out_shape=outs,
        scratch_shapes=scratches,
        compiler_params=pltpu.CompilerParams(vmem_limit_bytes=32 * 1024 * 1024),
    )


def meta_scratch():
    return [pltpu.SMEM((8, 128), jnp.float32)] * 3 + [pltpu.SemaphoreType.DMA((3,))]


def exchange(rows, devices, partner):
    return lax.ppermute(rows, AXES, [(i, partner(i)) for i in range(devices)])


def on_device(fine_pop, coarse_pop, fine_nbr, coarse_nbr, parent, children, solid):
    devices = lax.axis_size(AXES)
    by_one = lambda a: exchange(a, devices, lambda i: i ^ 1)
    by_two = lambda a: exchange(a, devices, lambda i: i ^ 2)
    odd_even = lambda a: exchange(a, devices, lambda i: (((i + 1) ^ 1) - 1) % devices)

    cpost, e_own, c_own = call(
        coarse_first_kernel,
        "coarse_first",
        [VMEM],
        [rows_of(CB * BLOCK), rows_of(E_ROWS), rows_of(C1_ROWS)],
        [scratch(CB * BLOCK)],
    )(coarse_pop)
    e_two = by_two(e_own)
    post, mask, f_own = call(
        fine_first_kernel,
        "fine_first",
        [SMEM, SMEM, VMEM, VMEM],
        [rows_of(FB * BLOCK), rows_of(FB * R, jnp.int32), rows_of(F_ROWS)],
        [scratch(FB * BLOCK), scratch(FB * R, jnp.int32)],
    )(fine_nbr, parent, fine_pop, solid)

    x_in = by_one(jnp.concatenate([f_own, e_own, e_two, c_own]))
    n_in = odd_even(
        jnp.concatenate(
            [
                f_own,
                x_in[EDGES:META],
                e_own[EC_AT:],
                x_in[X_E + EC_AT : X_E2],
                e_two[EC_AT:],
                x_in[X_E2 + EC_AT : X_C],
                c_own,
            ]
        )
    )
    x_late = by_one(n_in[EDGES:META])
    post2, f2_own, e_halo, ez, fixed, cmid, c2_own = call(
        middle_kernel,
        "middle",
        [SMEM] * 3 + [VMEM] * 10,
        [
            rows_of(FB * BLOCK),
            rows_of(F_ROWS),
            rows_of(FB * 64),
            rows_of(FB * EZ_BLOCK),
            rows_of(FB * R),
            rows_of(CB * BLOCK),
            rows_of(C2_ROWS),
        ],
        [
            scratch(4 * E_ROWS),
            scratch(HALO),
            scratch(5 * R),
            scratch(R),
            scratch(BLOCK),
            scratch(3 * C1_ROWS),
        ]
        + meta_scratch(),
    )(
        fine_nbr,
        parent,
        coarse_nbr,
        post,
        mask,
        f_own,
        e_own,
        e_two,
        x_in,
        n_in,
        x_late,
        cpost,
        c_own,
    )

    x2_in = by_one(jnp.concatenate([f2_own, c2_own]))
    n2_in = odd_even(jnp.concatenate([f2_own, x2_in[EDGES:META], c2_own]))
    x2_late = by_one(n2_in[EDGES:META])
    fine_out, means, cpassed = call(
        fine_last_kernel,
        "fine_last",
        [SMEM] * 2 + [VMEM] * 14,
        [
            jax.ShapeDtypeStruct(fine_pop.shape, jnp.float32),
            rows_of(K_ROWS),
            rows_of(CB * BLOCK),
        ],
        [
            scratch(HALO),
            scratch(5 * R),
            scratch(FB * BLOCK),
            scratch(8),
            scratch(3 * C2_ROWS),
        ]
        + meta_scratch(),
    )(
        fine_nbr,
        coarse_nbr,
        post2,
        mask,
        f2_own,
        x2_in,
        n2_in,
        x2_late,
        e_halo,
        ez,
        fixed,
        f_own,
        x_in,
        n_in,
        cmid,
        c2_own,
    )

    k_two = by_two(means)
    k_one = by_one(jnp.concatenate([means, k_two]))
    (coarse_out,) = call(
        coarse_last_kernel,
        "coarse_last",
        [SMEM] + [VMEM] * 4,
        [jax.ShapeDtypeStruct(coarse_pop.shape, jnp.float32)],
        [scratch(CB * BLOCK), scratch(4 * K_ROWS)],
    )(children, cpassed, means, k_two, k_one)
    return fine_out, coarse_out


def solution(mesh):
    rows = P(AXES, None)
    blocks = P(AXES, None, None)
    return jax.shard_map(
        on_device,
        mesh=mesh,
        in_specs=(blocks, blocks, rows, rows, rows, rows, rows),
        out_specs=(blocks, blocks),
        check_vma=False,
    )
```

```python
import jax
import jax.numpy as jnp
from jax import lax
from jax.experimental import pallas as pl
from jax.experimental.pallas import tpu as pltpu
from jax.sharding import PartitionSpec as P

AXES = ("gx", "gy")
VELOCITIES = (
    (0, 0, 0),
    (1, 0, 0),
    (-1, 0, 0),
    (0, 1, 0),
    (0, -1, 0),
    (0, 0, 1),
    (0, 0, -1),
    (1, 1, 0),
    (-1, -1, 0),
    (1, -1, 0),
    (-1, 1, 0),
    (1, 0, 1),
    (-1, 0, -1),
    (1, 0, -1),
    (-1, 0, 1),
    (0, 1, 1),
    (0, -1, -1),
    (0, 1, -1),
    (0, -1, 1),
)
WEIGHTS = (1.0 / 3.0,) + (1.0 / 18.0,) * 6 + (1.0 / 36.0,) * 12
OPPOSITE = (0, 2, 1, 4, 3, 6, 5, 8, 7, 10, 9, 12, 11, 14, 13, 16, 15, 18, 17)
OMEGA_COARSE = 1.6
OMEGA_FINE = 1.0 / (2.0 * (1.0 / 1.6 - 0.5) + 0.5)

XP = (1, 7, 9, 11, 13)
XM = (2, 8, 10, 12, 14)
YP = (3, 7, 10, 15, 17)
YM = (4, 8, 9, 16, 18)
ZP = (5, 11, 14, 15, 18)
ZM = (6, 12, 13, 16, 17)
YP1, YM1 = (3, 15, 17), (4, 16, 18)
YP2, YM2 = (7, 10), (8, 9)
ZP2, ZM2 = (11, 14, 15, 18), (12, 13, 16, 17)

R = 32
BLOCK = 19 * R
FB, CB = 4, 2
ZS = FB * 64
EDGES = ZS + R
META = EDGES + R
F_ROWS = META + 8
F2_ROWS = META
E_BLOCK = 96
EC_AT = CB * E_BLOCK
E_ROWS = EC_AT + 8
C_ROWS = FB * 64 + 16
K_ROWS = 2 * 19 * 8
EZ_BLOCK = 80
HALO = 3 * EDGES + FB * 64
X_E = F_ROWS
X_E2 = X_E + E_ROWS
N_EDGE = F_ROWS
N_EC = N_EDGE + R
M_PARENT, M_CNBR, M_CHILD = 4, 8, 16


def iotas(rows=R):
    row = lax.broadcasted_iota(jnp.int32, (rows, 128), 0)
    lane = lax.broadcasted_iota(jnp.int32, (rows, 128), 1)
    return row, lane


def roll(a, shift, axis):
    if isinstance(shift, int):
        shift = shift % a.shape[axis]
        if shift == 0:
            return a
    return pltpu.roll(a, shift, axis)


def at(ref, start, size=R):
    if not isinstance(start, int):
        start = pl.multiple_of(start, 8)
    return ref[pl.ds(start, size), :]


def put(ref, start, value):
    if not isinstance(start, int):
        start = pl.multiple_of(start, 8)
    ref[pl.ds(start, value.shape[0]), :] = value


def rows_in(src, dst, blocks):
    def body(i, carry):
        for r in range(R):
            dst[pl.ds(i * R + r, blocks, stride=BLOCK), :] = src[i, :, 128 * r : 128 * r + 128]
        return carry

    lax.fori_loop(0, 19, body, 0)


def rows_out(src, dst, blocks):
    def body(i, carry):
        for r in range(R):
            dst[i, :, 128 * r : 128 * r + 128] = src[pl.ds(i * R + r, blocks, stride=BLOCK), :]
        return carry

    lax.fori_loop(0, 19, body, 0)


def total(terms):
    while len(terms) > 1:
        pairs = [terms[k] + terms[k + 1] for k in range(0, len(terms) - 1, 2)]
        terms = pairs + terms[len(terms) - len(terms) % 2 :]
    return terms[0]


def collide(f, rate):
    rho = total(f)
    mom = []
    for axis in range(3):
        plus = [f[i] for i in range(19) if VELOCITIES[i][axis] == 1]
        minus = [f[i] for i in range(19) if VELOCITIES[i][axis] == -1]
        mom.append(total(plus) - total(minus))
    inv = 1.0 / rho
    u = [m * inv for m in mom]
    base = 1.0 - 1.5 * (u[0] * u[0] + u[1] * u[1] + u[2] * u[2])
    scaled = {w: (rate * w) * rho for w in sorted(set(WEIGHTS))}
    keep = 1.0 - rate
    out = [None] * 19
    out[0] = keep * f[0] + scaled[WEIGHTS[0]] * base
    for i in range(1, 19, 2):
        proj = None
        for axis in range(3):
            c = VELOCITIES[i][axis]
            if c:
                term = u[axis]
                if proj is None:
                    proj = term if c > 0 else -term
                else:
                    proj = proj + term if c > 0 else proj - term
        even = base + 4.5 * (proj * proj)
        odd = 3.0 * proj
        w = scaled[WEIGHTS[i]]
        out[i] = keep * f[i] + w * (even + odd)
        out[i + 1] = keep * f[i + 1] + w * (even - odd)
    return out


def collide_rows(src, src_base, dst, dst_base, rate, mask, mask_base, corner=None):
    def body(v, carry):
        f = [at(src, src_base + i * R + v * 16, 16) for i in range(19)]
        if corner is not None:
            edge = at(corner, v * 16, 16)
            f = [with_corners(f[i], i, edge) for i in range(19)]
        post = collide(f, rate)
        if mask is not None:
            solid = (at(mask, mask_base + v * 16, 16) & 1) > 0
            post = [jnp.where(solid, f[i], post[i]) for i in range(19)]
        for i in range(19):
            put(dst, dst_base + i * R + v * 16, post[i])
        return carry

    lax.fori_loop(0, 2, body, 0)


def pack_x(get, packed):
    _, lane = iotas()
    x = lane & 15
    for j in range(5):
        packed = jnp.where(x == j, roll(get(XP[j]), j - 15, 1), packed)
        packed = jnp.where(x == 5 + j, roll(get(XM[j]), 5 + j, 1), packed)
    return packed


def swap_rows(a):
    row, _ = iotas()
    return jnp.where((row & 1) == 0, roll(a, -1, 0), roll(a, 1, 0))


def pack_y(get, plus, minus, first, rest):
    row, lane = iotas()
    upper = (row & 1) == 1
    packed = jnp.zeros((R, 128), jnp.float32)
    for k in range(len(plus)):
        p = first + k
        one = jnp.where(upper, roll(get(plus[k]), 16 * p - 112, 1), roll(get(minus[k]), 16 * p, 1))
        packed = jnp.where((lane >> 4) == p, one, packed)
    packed = swap_rows(packed)
    if rest is None:
        return packed
    group = lane >> 4
    return jnp.where((group >= first) & (group < first + len(plus)), packed, rest)


def pack_edges(get):
    row, lane = iotas()
    upper = (row & 1) == 1
    first = jnp.where(upper, roll(get(7), -127, 1), get(8))
    second = jnp.where(upper, roll(get(10), 1 - 112, 1), roll(get(9), 1 - 15, 1))
    return swap_rows(jnp.where(lane == 0, first, second))


def move_x(a, cx, halo):
    _, lane = iotas()
    x = lane & 15
    if cx == 1:
        return jnp.where(x == 0, halo, roll(a, 1, 1))
    return jnp.where(x == 15, halo, roll(a, -1, 1))


def move_y(a, cy, halo):
    row, lane = iotas()
    upper = (row & 1) == 1
    if cy == 1:
        near = roll(a, 16, 1)
        return jnp.where(lane < 16, jnp.where(upper, roll(near, 1, 0), halo), near)
    near = roll(a, -16, 1)
    return jnp.where(lane >= 112, jnp.where(upper, halo, roll(near, -1, 0)), near)


def move_z(a, cz, halo8):
    row, _ = iotas(8)
    if cz == 1:
        near = roll(a, 2, 0)
        return jnp.concatenate([jnp.where(row < 2, halo8, near[:8]), near[8:]], axis=0)
    near = roll(a, -2, 0)
    return jnp.concatenate([near[:24], jnp.where(row >= 6, halo8, near[24:])], axis=0)


def send_faces(get, out, coarse, b):
    put(out, b * 64, pack_x(get, at(coarse, b * 64)))
    put(out, b * 64 + R, pack_y(get, YP, YM, 0, at(coarse, b * 64 + R)))
    _, lane = iotas()
    edges = roll(pack_edges(get), 2 * b, 1)
    put(out, EDGES, jnp.where((lane >> 1) == b, edges, at(out, EDGES)))


def place():
    device = lax.axis_index("gx") * lax.axis_size("gy") + lax.axis_index("gy")
    sign = 1 - 2 * (device & 1)
    return device, sign


def coarse_first_kernel(
    pop_hbm,
    fine_hbm,
    solid_hbm,
    nbr_hbm,
    parent_hbm,
    cnbr_hbm,
    children_hbm,
    post,
    e_out,
    c_out,
    fine_out,
    solid_out,
    meta_out,
    pop,
    nbr,
    parent,
    cnbr,
    children,
    raw,
    sem,
):
    copies = [
        pltpu.make_async_copy(src, dst, sem.at[k])
        for k, (src, dst) in enumerate(
            (
                (pop_hbm, pop),
                (nbr_hbm, nbr),
                (parent_hbm, parent),
                (cnbr_hbm, cnbr),
                (children_hbm, children),
                (fine_hbm, fine_out),
                (solid_hbm, solid_out),
            )
        )
    ]
    for c in copies:
        c.start()
    copies[0].wait()
    rows_in(pop, raw, CB)
    _, lane = iotas(16)
    _, lane8 = iotas(8)
    x16 = lane & 15
    corner = jnp.zeros((8, 128), jnp.float32)
    for c in range(CB):
        base = c * BLOCK
        half = lambda i: at(raw, base + i * R, 16)
        for qx in range(2):
            packed = jnp.zeros((16, 128), jnp.float32)
            for j in range(5):
                packed = jnp.where(x16 == j, roll(half(XP[j]), j - 8 * qx, 1), packed)
                packed = jnp.where(x16 == 5 + j, roll(half(XM[j]), 5 + j - 8 * qx - 7, 1), packed)
            put(e_out, c * E_BLOCK + qx * 16, packed)
        low = jnp.zeros((16, 128), jnp.float32)
        high = jnp.zeros((16, 128), jnp.float32)
        for p in range(5):
            low = jnp.where((lane >> 4) == p, roll(half(YP[p]), 16 * p, 1), low)
            high = jnp.where((lane >> 4) == p, roll(half(YM[p]), 16 * p - 112, 1), high)
        put(e_out, c * E_BLOCK + 32, low)
        put(e_out, c * E_BLOCK + 48, high)
        put(e_out, c * E_BLOCK + 64, jnp.zeros((R, 128), jnp.float32))
        for k in range(5):
            e_out[pl.ds(c * E_BLOCK + 64 + 2 * k, 2), :] = raw[pl.ds(base + ZP[k] * R, 2), :]
            e_out[pl.ds(c * E_BLOCK + 74 + 2 * k, 2), :] = raw[pl.ds(base + ZM[k] * R + 14, 2), :]
        for q in range(4):
            for e, (i, yq, xq) in enumerate(((7, 7, 0), (10, 7, 7), (9, 0, 0), (8, 0, 7))):
                to = (c * 4 + q) * 4 + e
                rows = raw[pl.ds(base + i * R + q // 2, 8, stride=2), :]
                rows = roll(rows, to - (yq * 16 + 8 * (q % 2) + xq), 1)
                corner = jnp.where(lane8 == to, rows, corner)
    put(e_out, EC_AT, corner)
    row8, _ = iotas(8)
    for c in range(CB):
        base = c * BLOCK
        collide_rows(raw, base, post, base, OMEGA_COARSE, None, 0)
        get = lambda i: at(post, base + i * R)
        x_wide = lax.broadcasted_iota(jnp.int32, (R, 128), 1) & 15
        ahead = jnp.zeros((R, 128), jnp.float32)
        back = jnp.zeros((R, 128), jnp.float32)
        for j in range(5):
            ahead = jnp.where(x_wide == 10 + j, roll(get(XP[j]), 10 + j - 15, 1), ahead)
            back = jnp.where(x_wide == 10 + j, roll(get(XM[j]), 10 + j, 1), back)
        put(c_out, c * 128, ahead)
        put(c_out, c * 128 + 64, back)
        put(c_out, c * 64 + R, pack_y(get, YP1, YM1, 5, None))
        put(c_out, (c + 2) * 64 + R, jnp.zeros((R, 128), jnp.float32))
        top = roll(at(post, base + 5 * R + 24, 8), 2, 0)
        bottom = roll(at(post, base + 6 * R, 8), 6, 0)
        put(c_out, FB * 64 + 8 * c, jnp.where(row8 < 2, top, bottom))
    for c in copies[1:]:
        c.wait()
    meta = jnp.zeros((8, 128), jnp.float32)
    entries = []
    for b in range(FB):
        entries += [(b, k, nbr[b, k]) for k in range(4)]
        entries += [(b, 4 + k, parent[k, b]) for k in range(2)]
    for c in range(CB):
        entries += [(c, M_CNBR + k, cnbr[c, k]) for k in range(6)]
        entries += [(c, M_CHILD + k, children[c, k]) for k in range(4)]
    for b, k, value in entries:
        meta = jnp.where((row8 == b) & (lane8 == k), value.astype(jnp.float32), meta)
    put(meta_out, 0, meta)


def fine_first_kernel(meta, pop, solid, coarse, post, mask, f_out, raw, sol):
    rows_in(pop, raw, FB)
    for r in range(R):
        sol[pl.ds(r, FB, stride=R), :] = solid[:, 128 * r : 128 * r + 128]
    put(f_out, EDGES, jnp.zeros((R, 128), jnp.float32))
    put(f_out, ZS, coarse[pl.ds(FB * 64, 16), :])
    put(f_out, ZS + 16, jnp.zeros((16, 128), jnp.float32))

    def body(b, carry):
        s = jnp.where(at(sol, b * R) > 0, 1, 0)
        bits = s
        for i in range(1, 19):
            cx, cy, cz = VELOCITIES[i]
            m = s
            if cx:
                m = roll(m, cx, 1)
            if cy:
                m = move_y(m, cy, jnp.zeros_like(m))
            if cz:
                m = roll(m, 2 * cz, 0)
            bits = bits | (m << i)
        put(mask, b * R, bits)
        base = b * BLOCK
        collide_rows(raw, base, post, base, OMEGA_FINE, mask, b * R)
        send_faces(lambda i: at(post, base + i * R), f_out, coarse, b)
        return carry

    lax.fori_loop(0, FB, body, 0)
    put(f_out, META, meta[...])


def number(meta, row, column):
    return meta[row, column].astype(jnp.int32)


def onehot(rows, cols, source):
    row = lax.broadcasted_iota(jnp.int32, (rows, cols), 0)
    col = lax.broadcasted_iota(jnp.int32, (rows, cols), 1)
    return jnp.where(row == source(col), 1.0, 0.0).astype(jnp.float32)


def exact_dot(a, b):
    return jnp.dot(a, b, preferred_element_type=jnp.float32, precision=lax.Precision.HIGHEST)


def expand(meta, device, gathered, halo, ez):
    _, lane = iotas(16)
    row, _ = iotas(16)
    x = lane & 15
    spread_x = onehot(
        128, 256, lambda m: ((m >> 7) * 4 + ((m & 127) >> 5)) * 16 + (m & 15)
    )

    def body(b, carry):
        p, q = number(meta, b, M_PARENT), number(meta, b, M_PARENT + 1)
        qy, qx = q >> 1, q & 1
        base = ((p >> 1) ^ device) * E_ROWS + (p & 1) * E_BLOCK
        home = b * 64
        ex = exact_dot(gathered[pl.ds(base + qx * 16 + qy, 8, stride=2), :], spread_x)
        spread_y = onehot(128, 128, lambda m: (m >> 4) * 16 + 8 * qx + ((m & 15) >> 1))
        ey0 = exact_dot(gathered[pl.ds(base + 32 + qy, 8, stride=2), :], spread_y)
        ey1 = exact_dot(gathered[pl.ds(base + 48 + qy, 8, stride=2), :], spread_y)
        for k in range(2):
            halo[pl.ds(home + 2 * k, 8, stride=4), :] = ex[:, :128]
            halo[pl.ds(home + 2 * k + 1, 8, stride=4), :] = ex[:, 128:]
            halo[pl.ds(home + R + 2 * k, 8, stride=4), :] = ey0
            halo[pl.ds(home + R + 2 * k + 1, 8, stride=4), :] = ey1
        spread_z = onehot(
            128,
            256,
            lambda m: ((m >> 7) * 4 + ((m & 127) >> 5)) * 16 + 8 * qx + ((m & 15) >> 1),
        )
        ezs = exact_dot(gathered[pl.ds(base + 64 + qy, 16, stride=2), :], spread_z)
        a0, a1 = ezs[:, :128], ezs[:, 128:]
        moves = {}
        moves[0, 0] = (a0, a1)
        moves[1, 0] = tuple(jnp.where(x == 0, a, roll(a, 1, 1)) for a in (a0, a1))
        moves[-1, 0] = tuple(jnp.where(x == 15, a, roll(a, -1, 1)) for a in (a0, a1))
        moves[0, 1] = (
            jnp.where(lane < 16, a0, roll(a0, 16, 1)),
            jnp.where(lane < 16, roll(a0, 16, 1), roll(a1, 16, 1)),
        )
        moves[0, -1] = (
            jnp.where(lane >= 112, roll(a1, -16, 1), roll(a0, -16, 1)),
            jnp.where(lane >= 112, a1, roll(a1, -16, 1)),
        )
        out = [a0, a1]
        for k, i in enumerate(ZP + ZM):
            moved = moves[VELOCITIES[i][:2]]
            out = [jnp.where(row == k, moved[h], out[h]) for h in range(2)]
        for h in range(2):
            for k in range(5):
                ez[pl.ds(b * EZ_BLOCK + 8 * k + h, 1), :] = out[h][k : k + 1]
                ez[pl.ds(b * EZ_BLOCK + 40 + 8 * k + 6 + h, 1), :] = out[h][5 + k : 6 + k]
        return carry

    lax.fori_loop(0, FB, body, 0)


def gather_halo(own, x_in, n_in, e_halo, halo):
    put(halo, 3 * EDGES, e_halo[...])
    for k, ref in enumerate((n_in, own, x_in)):
        put(halo, k * EDGES, ref[0:EDGES, :])


def gather_edges(own, x_in, n_in, x_late, relayed, edges):
    for k, ref in enumerate((n_in, own, x_in)):
        put(edges, (k + 1) * R, ref[EDGES : EDGES + R, :])
    put(edges, 0, n_in[pl.ds(relayed, R), :])
    put(edges, 4 * R, x_late[...])


def corners(meta_n, meta_own, meta_x, device, sign, e_halo, edges, fixed, b):
    row, lane = iotas()
    upper = (row & 1) == 1
    result = jnp.zeros((R, 128), jnp.float32)
    for side in range(2):
        n = number(meta_own, b, 2 + side)
        safe = jnp.maximum(n, 0)
        which = ((safe >> 2) - device) * sign + 1
        which = jnp.clip(which, 0, 2)
        row_n = safe & 3
        for end in range(2):
            i = ((7, 10), (9, 8))[side][end]
            p = (YP, YM)[side].index(i)
            edge_col = ((0, 1), (1, 0))[side][end]
            to = 112 * side + 15 * end
            m = jnp.where(
                which == 0,
                meta_n[row_n, end],
                jnp.where(which == 1, meta_own[row_n, end], meta_x[row_n, end]),
            ).astype(jnp.int32)
            m_safe = jnp.maximum(m, 0)
            slot = jnp.clip(((m_safe >> 2) - device) * sign + 2, 0, 4)
            shift = (to - (2 * (m_safe & 3) + edge_col)) & 127
            sent = roll(at(edges, slot * R), shift, 1)
            own = roll(at(e_halo, b * 64 + R), to - (16 * p + 15 * end), 1)
            value = jnp.where(n < 0, own, jnp.where(m >= 0, sent, at(fixed, b * R)))
            here = (lane == to) & (upper if side else jnp.logical_not(upper))
            result = jnp.where(here, value, result)
    return result


def fixed_corners(meta_n, meta_own, meta_x, device, sign, group, from_n, fixed, spare):
    _, lane = iotas()
    npart = device - sign

    def body(b, carry):
        result = jnp.zeros((R, 128), jnp.float32)
        for side in range(2):
            safe = jnp.maximum(number(meta_own, b, 2 + side), 0)
            which = jnp.clip(((safe >> 2) - device) * sign + 1, 0, 2)
            row_n = safe & 3
            pq = [
                jnp.where(
                    which == 0,
                    meta_n[row_n, 4 + k],
                    jnp.where(which == 1, meta_own[row_n, 4 + k], meta_x[row_n, 4 + k]),
                ).astype(jnp.int32)
                for k in range(2)
            ]
            p, q = pq
            near = ((p >> 1) ^ device) & 3
            far = ((p >> 1) ^ npart) & 3
            quad = jnp.where(
                which == 0, at(from_n, far * 8, 8), at(group, near * 8, 8)
            )
            for k in range(4):
                spare[pl.ds(k, 8, stride=4), :] = quad
            rows = spare[...]
            for end in range(2):
                to = 112 * side + 15 * end
                source = ((p & 1) * 4 + q) * 4 + 2 * side + end
                result = jnp.where(lane == to, roll(rows, (to - source) & 127, 1), result)
        put(fixed, b * R, result)
        return carry

    lax.fori_loop(0, FB, body, 0)


def stream_fine(meta, device, sign, post, mask, halo, ez, dst, dst_base, b):
    base = b * BLOCK
    bits = at(mask, b * R)
    faces = []
    for k in range(4):
        n = number(meta, b, k)
        safe = jnp.maximum(n, 0)
        which = jnp.clip(((safe >> 2) - device) * sign + 1, 0, 2)
        start = jnp.where(n >= 0, which * EDGES + (safe & 3) * 64, 3 * EDGES + b * 64)
        faces.append(at(halo, start + (R if k >= 2 else 0)))
    solid = (bits & 1) > 0
    for i in range(19):
        cx, cy, cz = VELOCITIES[i]
        a = at(post, base + i * R)
        if i == 0:
            put(dst, dst_base, a)
            continue
        g = a
        if cx == 1:
            g = move_x(g, 1, roll(faces[0], -XP.index(i), 1))
        elif cx == -1:
            g = move_x(g, -1, roll(faces[1], 10 - XM.index(i), 1))
        if cy:
            first = 112 * (cy == -1)
            p = (YP if cy == 1 else YM).index(i)
            side = roll(faces[2 if cy == 1 else 3], first - 16 * p + cx, 1)
            g = move_y(g, cy, side)
        if cz:
            k = ZP.index(i) if cz == 1 else 5 + ZM.index(i)
            g = move_z(g, cz, at(ez, b * EZ_BLOCK + 8 * k, 8))
        from_wall = (bits & (1 << i)) > 0
        g = jnp.where(from_wall, at(post, base + OPPOSITE[i] * R), g)
        put(dst, dst_base + i * R, jnp.where(solid, a, g))


def with_corners(cells, i, corner):
    if i not in (7, 8, 9, 10):
        return cells
    row, lane = iotas(cells.shape[0])
    column, upper = {7: (0, 0), 10: (15, 0), 9: (112, 1), 8: (127, 1)}[i]
    return jnp.where((lane == column) & ((row & 1) == upper), corner, cells)


def fetch_meta(pairs, sem):
    copies = [
        pltpu.make_async_copy(ref.at[pl.ds(META, 8)], dst, sem.at[k])
        for k, (ref, dst) in enumerate(pairs)
    ]
    for c in copies:
        c.start()
    return copies


def expand_kernel(f_own, e_own, e_two, x_in, e_halo, ez, gathered, meta, sem):
    device, _ = place()
    (fetch,) = fetch_meta(((f_own, meta),), sem)
    put(gathered, 0, e_own[...])
    put(gathered, E_ROWS, x_in[X_E : X_E + E_ROWS, :])
    put(gathered, 2 * E_ROWS, e_two[...])
    put(gathered, 3 * E_ROWS, x_in[X_E2 : X_E2 + E_ROWS, :])
    fetch.wait()
    expand(meta, device, gathered, e_halo, ez)


def coarse_source(index, device, sign):
    safe = jnp.maximum(index, 0)
    which = jnp.clip(((safe >> 1) - device) * sign + 1, 0, 2)
    return which, safe & 1


def first_stream_kernel(
    post,
    mask,
    f_own,
    e_own,
    e_two,
    x_in,
    n_in,
    cpost,
    e_halo,
    ez,
    new,
    fixed,
    cmid,
    c_out,
    group,
    halo,
    spare,
    meta_n,
    meta_own,
    meta_x,
    sem,
):
    device, sign = place()
    copies = fetch_meta(((n_in, meta_n), (f_own, meta_own), (x_in, meta_x)), sem)
    put(group, 0, e_own[EC_AT:E_ROWS, :])
    put(group, 8, x_in[X_E + EC_AT : X_E + E_ROWS, :])
    put(group, 16, e_two[EC_AT:E_ROWS, :])
    put(group, 24, x_in[X_E2 + EC_AT : X_E2 + E_ROWS, :])
    gather_halo(f_own, x_in, n_in, e_halo, halo)
    for k in range(FB):
        put(c_out, k * 64, jnp.zeros((64, 128), jnp.float32))
    for c in copies:
        c.wait()

    row8, _ = iotas(8)

    def coarse_body(c, carry):
        base = c * BLOCK
        has, which, slot = [], [], []
        for k in range(6):
            neighbour = number(meta_own, c, M_CNBR + k)
            w, s = coarse_source(neighbour, device, sign)
            has.append(neighbour >= 0)
            which.append(w * EDGES)
            slot.append(s)
        faces = [at(halo, which[k] + slot[k] * 128 + 64 * k) for k in range(2)]
        faces += [at(halo, which[k] + slot[k] * 64 + R) for k in (2, 3)]
        zs = [at(halo, which[k] + ZS + slot[k] * 8, 8) for k in (4, 5)]
        put(cmid, base, at(cpost, base))
        for i in range(1, 19):
            cx, cy, cz = VELOCITIES[i]
            a = at(cpost, base + i * R)
            if cx == 1:
                g = move_x(a, 1, jnp.where(has[0], roll(faces[0], -10 - XP.index(i), 1), a))
            elif cx == -1:
                g = move_x(a, -1, jnp.where(has[1], roll(faces[1], 5 - XM.index(i), 1), a))
            elif cy == 1:
                side = roll(faces[2], -16 * (5 + YP1.index(i)), 1)
                g = move_y(a, 1, jnp.where(has[2], side, a))
            elif cy == -1:
                side = roll(faces[3], 112 - 16 * (5 + YM1.index(i)), 1)
                g = move_y(a, -1, jnp.where(has[3], side, a))
            elif cz == 1:
                g = move_z(a, 1, jnp.where(has[4], zs[0], a[:8]))
            else:
                g = move_z(a, -1, jnp.where(has[5], zs[1], a[24:]))
            put(cmid, base + i * R, g)
        get = lambda i: at(cmid, base + i * R)
        put(c_out, c * 64 + R, pack_y(get, YP2, YM2, 5, None))
        for k in (0, 2):
            layers = None
            for h in range(2):
                top = roll(at(cmid, base + ZP2[k + h] * R + 24, 8), 2 + 2 * h, 0)
                bottom = roll(at(cmid, base + ZM2[k + h] * R, 8), 6 - 2 * h, 0)
                both = jnp.where(row8 < 4, top, bottom)
                layers = both if h == 0 else jnp.where((row8 < 2) | (row8 >= 6), layers, both)
            put(c_out, FB * 64 + c * 16 + 4 * k, layers)
        return carry

    lax.fori_loop(0, CB, coarse_body, 0)
    fixed_corners(
        meta_n,
        meta_own,
        meta_x,
        device,
        sign,
        group,
        n_in.at[pl.ds(N_EC, 32)],
        fixed,
        spare,
    )

    def body(b, carry):
        stream_fine(meta_own, device, sign, post, mask, halo, ez, new, b * BLOCK, b)
        return carry

    lax.fori_loop(0, FB, body, 0)


def second_collision_kernel(
    new,
    mask,
    f_own,
    x_in,
    n_in,
    x_late,
    e_halo,
    fixed,
    coarse,
    post,
    f_out,
    spot,
    edges,
    meta_n,
    meta_own,
    meta_x,
    sem,
):
    device, sign = place()
    copies = fetch_meta(((n_in, meta_n), (f_own, meta_own), (x_in, meta_x)), sem)
    gather_edges(f_own, x_in, n_in, x_late, N_EDGE, edges)
    put(f_out, EDGES, jnp.zeros((R, 128), jnp.float32))
    put(f_out, ZS, coarse[pl.ds(FB * 64, R), :])
    for c in copies:
        c.wait()

    def body(b, carry):
        base = b * BLOCK
        spot[...] = corners(meta_n, meta_own, meta_x, device, sign, e_halo, edges, fixed, b)
        collide_rows(new, base, post, base, OMEGA_FINE, mask, b * R, spot)
        send_faces(lambda i: at(post, base + i * R), f_out, coarse, b)
        return carry

    lax.fori_loop(0, FB, body, 0)


def second_stream_kernel(
    post, mask, f_own, x_in, n_in, e_halo, ez, f_first, new, halo, meta, sem
):
    device, sign = place()
    (fetch,) = fetch_meta(((f_first, meta),), sem)
    gather_halo(f_own, x_in, n_in, e_halo, halo)
    fetch.wait()

    def body(b, carry):
        stream_fine(meta, device, sign, post, mask, halo, ez, new, b * BLOCK, b)
        return carry

    lax.fori_loop(0, FB, body, 0)


def coarsen_kernel(
    new_in,
    f_own,
    x_in,
    n_in,
    x_late,
    e_halo,
    fixed,
    f_first,
    x_first,
    n_first,
    new,
    means,
    edges,
    meta_n,
    meta_own,
    meta_x,
    sem,
):
    device, sign = place()
    copies = fetch_meta(((n_first, meta_n), (f_first, meta_own), (x_first, meta_x)), sem)
    gather_edges(f_own, x_in, n_in, x_late, F2_ROWS, edges)
    for c in copies:
        c.wait()

    def body(b, carry):
        corner = corners(meta_n, meta_own, meta_x, device, sign, e_halo, edges, fixed, b)
        for i in range(19):
            start = b * BLOCK + i * R
            put(new, start, with_corners(at(new_in, start), i, corner))
        return carry

    lax.fori_loop(0, FB, body, 0)

    row = lax.broadcasted_iota(jnp.int32, (128, 128), 0)
    col = lax.broadcasted_iota(jnp.int32, (128, 128), 1)
    target = lambda yh, h: (yh * 4 + (row >> 5)) * 16 + ((row & 15) >> 1) + 8 * h
    mats = [
        [jnp.where(col == target(yh, h), 0.125, 0.0).astype(jnp.float32) for yh in range(2)]
        for h in range(2)
    ]
    rows = 19 * 8
    for pair in range(2):
        total = None
        for h in range(2):
            b = 2 * pair + h
            for yh in range(2):
                z0 = new[pl.ds(b * BLOCK + yh, rows, stride=4), :]
                z1 = new[pl.ds(b * BLOCK + 2 + yh, rows, stride=4), :]
                part = exact_dot(z0 + z1, mats[h][yh])
                total = part if total is None else total + part
        put(means, pair * rows, total)


def tail_kernel(
    f_first, new, f_own, x_in, n_in, cmid, fine_out, cpassed, halo, meta_own, sem
):
    device, sign = place()
    (fetch,) = fetch_meta(((f_first, meta_own),), sem)
    rows_out(new, fine_out, FB)
    for k, ref in enumerate((n_in, f_own, x_in)):
        put(halo, k * EDGES, ref[0:EDGES, :])
    fetch.wait()

    def coarse_body(c, carry):
        base = c * BLOCK
        has, which, slot = [], [], []
        for k in range(6):
            neighbour = number(meta_own, c, M_CNBR + k)
            w, s = coarse_source(neighbour, device, sign)
            has.append(neighbour >= 0)
            which.append(w * EDGES)
            slot.append(s)
        faces = [at(halo, which[k] + slot[k] * 64 + R) for k in (2, 3)]

        def layer(k, n, back):
            side = at(halo, which[k] + ZS + slot[k] * 16 + 8 * (n // 2), 8)
            return roll(side, (2 if back else -2) * (n & 1), 0)

        for i in range(19):
            a = at(cmid, base + i * R)
            g = a
            if i in YP2:
                side = roll(faces[0], -16 * (5 + YP2.index(i)), 1)
                g = move_y(a, 1, jnp.where(has[2], side, a))
            elif i in YM2:
                side = roll(faces[1], 112 - 16 * (5 + YM2.index(i)), 1)
                g = move_y(a, -1, jnp.where(has[3], side, a))
            elif i in ZP2:
                g = move_z(a, 1, jnp.where(has[4], layer(4, ZP2.index(i), False), a[:8]))
            elif i in ZM2:
                g = move_z(a, -1, jnp.where(has[5], layer(5, ZM2.index(i), True), a[24:]))
            put(cpassed, base + i * R, g)
        return carry

    lax.fori_loop(0, CB, coarse_body, 0)


def coarse_last_kernel(
    f_first, cpassed, own, two, x_in, coarse_out, merged, gathered, meta, sem
):
    device, _ = place()
    (fetch,) = fetch_meta(((f_first, meta),), sem)
    put(gathered, 0, own[...])
    put(gathered, K_ROWS, x_in[0:K_ROWS, :])
    put(gathered, 2 * K_ROWS, two[...])
    put(gathered, 3 * K_ROWS, x_in[K_ROWS : 2 * K_ROWS, :])
    merged[...] = cpassed[...]
    fetch.wait()
    _, lane = iotas(8)
    x_half = (lane >> 3) & 1

    def body(step, carry):
        c, q = step >> 2, step & 3
        qy, qx = q >> 1, q & 1
        child = number(meta, c, M_CHILD + q)

        @pl.when(child >= 0)
        def _():
            slot = ((child >> 2) ^ device) & 3
            start = slot * K_ROWS + ((child & 3) >> 1) * (19 * 8)
            shift = (8 * (qx - (child & 1))) & 127
            mine = x_half == qx
            for i in range(19):
                value = roll(at(gathered, start + 8 * i, 8), shift, 1)
                rows = pl.ds(c * BLOCK + i * R + qy, 8, stride=2)
                merged[rows, :] = jnp.where(mine, value, merged[rows, :])

        return carry

    lax.fori_loop(0, CB * 4, body, 0)
    rows_out(merged, coarse_out, CB)


VMEM = pl.BlockSpec(memory_space=pltpu.VMEM)
HBM = pl.BlockSpec(memory_space=pltpu.HBM)


def rows_of(n, dtype=jnp.float32):
    return jax.ShapeDtypeStruct((n, 128), dtype)


def scratch(n, dtype=jnp.float32):
    return pltpu.VMEM((n, 128), dtype)


def call(kernel, name, specs, outs, scratches, flops=1 << 20):
    return pl.pallas_call(
        kernel,
        name=name,
        in_specs=specs,
        out_specs=[VMEM] * len(outs),
        out_shape=outs,
        scratch_shapes=scratches,
        cost_estimate=pl.CostEstimate(flops=flops, bytes_accessed=4 << 20, transcendentals=0),
        compiler_params=pltpu.CompilerParams(vmem_limit_bytes=32 * 1024 * 1024),
    )


def meta_scratch(n=3):
    return [pltpu.SMEM((8, 128), jnp.float32)] * n + [pltpu.SemaphoreType.DMA((n,))]


def exchange(rows, devices, partner):
    return lax.ppermute(rows, AXES, [(i, partner(i)) for i in range(devices)])


def on_device(fine_pop, coarse_pop, fine_nbr, coarse_nbr, parent, children, solid):
    devices = lax.axis_size(AXES)
    by_one = lambda a: exchange(a, devices, lambda i: i ^ 1)
    by_two = lambda a: exchange(a, devices, lambda i: i ^ 2)
    odd_even = lambda a: exchange(a, devices, lambda i: (((i + 1) ^ 1) - 1) % devices)
    by_direction = lambda a: jnp.transpose(a, (1, 0, 2))
    parent = parent.T
    fine_cells, coarse_cells = by_direction(fine_pop), by_direction(coarse_pop)
    small = lambda a: pltpu.SMEM(a.shape, jnp.int32)

    cpost, e_own, c_own, fine_raw, solid_raw, meta = call(
        coarse_first_kernel,
        "coarse_first",
        [HBM] * 7,
        [
            rows_of(CB * BLOCK),
            rows_of(E_ROWS),
            rows_of(C_ROWS),
            jax.ShapeDtypeStruct(fine_cells.shape, jnp.float32),
            jax.ShapeDtypeStruct(solid.shape, jnp.int32),
            rows_of(8),
        ],
        [
            pltpu.VMEM(coarse_cells.shape, jnp.float32),
            small(fine_nbr),
            small(parent),
            small(coarse_nbr),
            small(children),
            scratch(CB * BLOCK),
            pltpu.SemaphoreType.DMA((7,)),
        ],
    )(
        *(
            pltpu.with_memory_space_constraint(a, pltpu.HBM)
            for a in (coarse_cells, fine_cells, solid, fine_nbr, parent, coarse_nbr, children)
        )
    )
    e_two = by_two(e_own)
    post, mask, f_own = call(
        fine_first_kernel,
        "fine_first",
        [VMEM] * 4,
        [rows_of(FB * BLOCK), rows_of(FB * R, jnp.int32), rows_of(F_ROWS)],
        [scratch(FB * BLOCK), scratch(FB * R, jnp.int32)],
    )(meta, fine_raw, solid_raw, c_own)

    x_in = by_one(jnp.concatenate([f_own, e_own, e_two]))
    n_in = odd_even(
        jnp.concatenate(
            [
                f_own,
                x_in[EDGES:META],
                e_own[EC_AT:],
                x_in[X_E + EC_AT : X_E2],
                e_two[EC_AT:],
                x_in[X_E2 + EC_AT :],
            ]
        )
    )
    e_halo, ez = call(
        expand_kernel,
        "expand",
        [VMEM] * 4,
        [rows_of(FB * 64), rows_of(FB * EZ_BLOCK)],
        [scratch(4 * E_ROWS)] + meta_scratch(1),
    )(f_own, e_own, e_two, x_in)
    far_edges, ez = lax.optimization_barrier((n_in[EDGES:META], ez))
    x_late = by_one(far_edges)
    new, fixed, cmid, c2_own = call(
        first_stream_kernel,
        "first_stream",
        [VMEM] * 10,
        [
            rows_of(FB * BLOCK),
            rows_of(FB * R),
            rows_of(CB * BLOCK),
            rows_of(FB * 64 + R),
        ],
        [scratch(32), scratch(HALO), scratch(R)] + meta_scratch(),
    )(post, mask, f_own, e_own, e_two, x_in, n_in, cpost, e_halo, ez)
    post2, f2_own = call(
        second_collision_kernel,
        "second_collision",
        [VMEM] * 9,
        [rows_of(FB * BLOCK), rows_of(F2_ROWS)],
        [scratch(R), scratch(5 * R)] + meta_scratch(),
    )(new, mask, f_own, x_in, n_in, x_late, e_halo, fixed, c2_own)

    x2_in = by_one(f2_own)
    n2_in = odd_even(jnp.concatenate([f2_own, x2_in[EDGES:META]]))
    x2_late = by_one(n2_in[EDGES:META])
    (new2,) = call(
        second_stream_kernel,
        "second_stream",
        [VMEM] * 8,
        [rows_of(FB * BLOCK)],
        [scratch(HALO)] + meta_scratch(1),
    )(post2, mask, f2_own, x2_in, n2_in, e_halo, ez, f_own)
    new2, means = call(
        coarsen_kernel,
        "coarsen",
        [VMEM] * 10,
        [rows_of(FB * BLOCK), rows_of(K_ROWS)],
        [scratch(5 * R)] + meta_scratch(),
    )(new2, f2_own, x2_in, n2_in, x2_late, e_halo, fixed, f_own, x_in, n_in)

    k_two = by_two(means)
    fine_out, cpassed = call(
        tail_kernel,
        "tail",
        [VMEM] * 6,
        [
            jax.ShapeDtypeStruct(fine_cells.shape, jnp.float32),
            rows_of(CB * BLOCK),
        ],
        [scratch(3 * EDGES)] + meta_scratch(1),
    )(f_own, new2, f2_own, x2_in, n2_in, cmid)
    k_two, cpassed = lax.optimization_barrier((k_two, cpassed))
    k_one = by_one(jnp.concatenate([means, k_two]))
    (coarse_out,) = call(
        coarse_last_kernel,
        "coarse_last",
        [VMEM] * 5,
        [jax.ShapeDtypeStruct(coarse_cells.shape, jnp.float32)],
        [scratch(CB * BLOCK), scratch(4 * K_ROWS)] + meta_scratch(1),
    )(f_own, cpassed, means, k_two, k_one)
    return by_direction(fine_out), by_direction(coarse_out)


def solution(mesh):
    rows = P(AXES, None)
    blocks = P(AXES, None, None)
    return jax.shard_map(
        on_device,
        mesh=mesh,
        in_specs=(blocks, blocks, rows, rows, rows, rows, rows),
        out_specs=(blocks, blocks),
        check_vma=False,
    )
```

```python
import jax
import jax.numpy as jnp
from jax import lax
from jax.experimental import pallas as pl
from jax.experimental.pallas import tpu as pltpu
from jax.sharding import PartitionSpec as P

AXES = ("gx", "gy")
VELOCITIES = (
    (0, 0, 0),
    (1, 0, 0),
    (-1, 0, 0),
    (0, 1, 0),
    (0, -1, 0),
    (0, 0, 1),
    (0, 0, -1),
    (1, 1, 0),
    (-1, -1, 0),
    (1, -1, 0),
    (-1, 1, 0),
    (1, 0, 1),
    (-1, 0, -1),
    (1, 0, -1),
    (-1, 0, 1),
    (0, 1, 1),
    (0, -1, -1),
    (0, 1, -1),
    (0, -1, 1),
)
WEIGHTS = (1.0 / 3.0,) + (1.0 / 18.0,) * 6 + (1.0 / 36.0,) * 12
OPPOSITE = (0, 2, 1, 4, 3, 6, 5, 8, 7, 10, 9, 12, 11, 14, 13, 16, 15, 18, 17)
OMEGA_COARSE = 1.6
OMEGA_FINE = 1.0 / (2.0 * (1.0 / 1.6 - 0.5) + 0.5)

XP = (1, 7, 9, 11, 13)
XM = (2, 8, 10, 12, 14)
YP = (3, 7, 10, 15, 17)
YM = (4, 8, 9, 16, 18)
ZP = (5, 11, 14, 15, 18)
ZM = (6, 12, 13, 16, 17)
YP1, YM1 = (3, 15, 17), (4, 16, 18)
YP2, YM2 = (7, 10), (8, 9)
ZP2, ZM2 = (11, 14, 15, 18), (12, 13, 16, 17)


R = 32
FB, CB = 4, 2
FR, CR = FB * R, CB * R
F_ALL, C_ALL = 19 * FR, 19 * CR
PY_AT = FR
ZS = 2 * FR
EDGES = ZS + R
META = EDGES + R
F_ROWS = META + 8
F2_ROWS = META
EC_AT = 6 * R
E_ROWS = EC_AT + 8
C_ROWS = 2 * FR + 8
K_ROWS = 2 * 19 * 8
HALO = 3 * EDGES + 2 * FR
X_E = F_ROWS
X_E2 = X_E + E_ROWS
N_EDGE = F_ROWS
N_EC = N_EDGE + R
M_PARENT, M_CNBR, M_CHILD = 4, 8, 16


def iotas(rows=R):
    row = lax.broadcasted_iota(jnp.int32, (rows, 128), 0)
    lane = lax.broadcasted_iota(jnp.int32, (rows, 128), 1)
    return row, lane


def roll(a, shift, axis):
    if isinstance(shift, int):
        shift = shift % a.shape[axis]
        if shift == 0:
            return a
    return pltpu.roll(a, shift, axis)


def at(ref, start, size=R):
    if not isinstance(start, int):
        start = pl.multiple_of(start, 8)
    return ref[pl.ds(start, size), :]


def put(ref, start, value):
    if not isinstance(start, int):
        start = pl.multiple_of(start, 8)
    ref[pl.ds(start, value.shape[0]), :] = value


def zeros(rows):
    return jnp.zeros((rows, 128), jnp.float32)


def total(terms):
    while len(terms) > 1:
        pairs = [terms[k] + terms[k + 1] for k in range(0, len(terms) - 1, 2)]
        terms = pairs + terms[len(terms) - len(terms) % 2 :]
    return terms[0]


def collide(f, rate):
    rho = total(f)
    mom = []
    for axis in range(3):
        plus = [f[i] for i in range(19) if VELOCITIES[i][axis] == 1]
        minus = [f[i] for i in range(19) if VELOCITIES[i][axis] == -1]
        mom.append(total(plus) - total(minus))
    inv = 1.0 / rho
    u = [m * inv for m in mom]
    base = 1.0 - 1.5 * (u[0] * u[0] + u[1] * u[1] + u[2] * u[2])
    scaled = {w: (rate * w) * rho for w in sorted(set(WEIGHTS))}
    keep = 1.0 - rate
    out = [None] * 19
    out[0] = keep * f[0] + scaled[WEIGHTS[0]] * base
    for i in range(1, 19, 2):
        proj = None
        for axis in range(3):
            c = VELOCITIES[i][axis]
            if c:
                term = u[axis]
                if proj is None:
                    proj = term if c > 0 else -term
                else:
                    proj = proj + term if c > 0 else proj - term
        even = base + 4.5 * (proj * proj)
        odd = 3.0 * proj
        w = scaled[WEIGHTS[i]]
        out[i] = keep * f[i] + w * (even + odd)
        out[i + 1] = keep * f[i + 1] + w * (even - odd)
    return out


def collide_rows(src, dst, rows, rate, mask=None, corner=None):
    def body(v, carry):
        f = [at(src, i * rows + v * 16, 16) for i in range(19)]
        if corner is not None:
            edge = at(corner, v * 16, 16)
            f = [with_corners(f[i], i, edge) for i in range(19)]
        post = collide(f, rate)
        if mask is not None:
            solid = (at(mask, v * 16, 16) & 1) > 0
            post = [jnp.where(solid, f[i], post[i]) for i in range(19)]
        for i in range(19):
            put(dst, i * rows + v * 16, post[i])
        return carry

    lax.fori_loop(0, rows // 16, body, 0)


def upper_of(rows, blocks):
    row, _ = iotas(rows)
    return ((row // blocks) & 1) == 1


def swap_halves(a, blocks):
    if blocks == 4:
        rows = a.shape[0]
        return pltpu.roll(a.reshape(rows // 8, 8, 128), 4, 1).reshape(rows, 128)
    return jnp.where(upper_of(a.shape[0], blocks), roll(a, blocks, 0), roll(a, -blocks, 0))


def pack_x(get, packed, first=0):
    _, lane = iotas(packed.shape[0])
    x = lane & 15
    for j in range(5):
        packed = jnp.where(x == first + j, roll(get(XP[j]), first + j - 15, 1), packed)
        packed = jnp.where(x == first + 5 + j, roll(get(XM[j]), first + 5 + j, 1), packed)
    return packed


def pack_y(get, plus, minus, first, rest, blocks):
    rows = rest.shape[0]
    _, lane = iotas(rows)
    upper = upper_of(rows, blocks)
    group = lane >> 4
    packed = zeros(rows)
    for k in range(len(plus)):
        p = first + k
        one = jnp.where(upper, roll(get(plus[k]), 16 * p - 112, 1), roll(get(minus[k]), 16 * p, 1))
        packed = jnp.where(group == p, one, packed)
    packed = swap_halves(packed, blocks)
    return jnp.where((group >= first) & (group < first + len(plus)), packed, rest)


def pack_edges(get, rows):
    _, lane = iotas(rows)
    upper = upper_of(rows, FB)
    first = jnp.where(upper, roll(get(7), -127, 1), get(8))
    second = jnp.where(upper, roll(get(10), 1 - 112, 1), roll(get(9), 1 - 15, 1))
    return swap_halves(jnp.where(lane == 0, first, second), FB)


def move_x(a, cx, halo):
    _, lane = iotas(a.shape[0])
    x = lane & 15
    if cx == 1:
        return jnp.where(x == 0, halo, roll(a, 1, 1))
    return jnp.where(x == 15, halo, roll(a, -1, 1))


def move_y(a, cy, halo, blocks):
    _, lane = iotas(a.shape[0])
    upper = upper_of(a.shape[0], blocks)
    near = roll(a, 16 * cy, 1)
    if cy == 1:
        return jnp.where(lane < 16, jnp.where(upper, swap_halves(near, blocks), halo), near)
    return jnp.where(lane >= 112, jnp.where(upper, halo, swap_halves(near, blocks)), near)


def move_z_coarse(a, cz, halo8):
    row, _ = iotas(8)
    near = roll(a, 4 * cz, 0)
    if cz == 1:
        return jnp.concatenate([jnp.where(row < 4, halo8, near[:8]), near[8:]], axis=0)
    return jnp.concatenate([near[:-8], jnp.where(row >= 4, halo8, near[-8:])], axis=0)


def send_faces(post, out, coarse, spot):
    for h in range(2):
        rows = h * 64
        get = lambda i: at(post, i * FR + rows, 64)
        put(out, rows, pack_x(get, at(coarse, rows, 64)))
        put(out, PY_AT + rows, pack_y(get, YP, YM, 0, at(coarse, PY_AT + rows, 64), FB))
        put(spot, rows, pack_edges(get, 64))
    _, lane = iotas()
    edges = zeros(R)
    for b in range(FB):
        edges = jnp.where((lane >> 1) == b, roll(spot[pl.ds(b, R, stride=FB), :], 2 * b, 1), edges)
    put(out, EDGES, edges)


def place():
    device = lax.axis_index("gx") * lax.axis_size("gy") + lax.axis_index("gy")
    sign = 1 - 2 * (device & 1)
    return device, sign


def number(meta, row, column):
    return meta[row, column].astype(jnp.int32)


def fetch_meta(pairs, sem):
    copies = [
        pltpu.make_async_copy(ref.at[pl.ds(META, 8)], dst, sem.at[k])
        for k, (ref, dst) in enumerate(pairs)
    ]
    for c in copies:
        c.start()
    return copies


def coarse_first_kernel(
    pop_hbm,
    fine_hbm,
    solid_hbm,
    nbr_hbm,
    parent_hbm,
    cnbr_hbm,
    children_hbm,
    post,
    e_out,
    c_out,
    fine_out,
    solid_out,
    meta_out,
    raw,
    spot,
    nbr,
    parent,
    cnbr,
    children,
    sem,
):
    copies = [
        pltpu.make_async_copy(src, dst, sem.at[k])
        for k, (src, dst) in enumerate(
            (
                (pop_hbm, raw),
                (nbr_hbm, nbr),
                (parent_hbm, parent),
                (cnbr_hbm, cnbr),
                (children_hbm, children),
                (fine_hbm, fine_out),
                (solid_hbm, solid_out),
            )
        )
    ]
    for c in copies:
        c.start()
    copies[0].wait()
    _, lane = iotas()
    row8, lane8 = iotas(8)
    x = lane & 15
    half = lambda i: at(raw, i * CR)
    for qx in range(2):
        packed = zeros(R)
        for j in range(5):
            packed = jnp.where(x == j, roll(half(XP[j]), j - 8 * qx, 1), packed)
            packed = jnp.where(x == 5 + j, roll(half(XM[j]), 5 + j - 8 * qx - 7, 1), packed)
        put(e_out, qx * R, packed)
    low, high = zeros(R), zeros(R)
    for p in range(5):
        low = jnp.where((lane >> 4) == p, roll(half(YP[p]), 16 * p, 1), low)
        high = jnp.where((lane >> 4) == p, roll(half(YM[p]), 16 * p - 112, 1), high)
    put(e_out, 2 * R, low)
    put(e_out, 3 * R, high)
    put(e_out, 4 * R, zeros(2 * R))
    for k in range(5):
        e_out[pl.ds(4 * R + 4 * k, 4), :] = raw[pl.ds(ZP[k] * CR, 4), :]
        e_out[pl.ds(4 * R + 20 + 4 * k, 4), :] = raw[pl.ds(ZM[k] * CR + 28, 4), :]
    corner = zeros(8)
    for c in range(CB):
        for q in range(4):
            for e, (i, yq, xq) in enumerate(((7, 7, 0), (10, 7, 7), (9, 0, 0), (8, 0, 7))):
                to = (c * 4 + q) * 4 + e
                rows = raw[pl.ds(i * CR + (q // 2) * 2 + c, 8, stride=4), :]
                rows = roll(rows, to - (yq * 16 + 8 * (q % 2) + xq), 1)
                corner = jnp.where(lane8 == to, rows, corner)
    put(e_out, EC_AT, corner)

    collide_rows(raw, post, CR, OMEGA_COARSE)
    get = lambda i: at(post, i * CR, CR)
    _, wide = iotas(CR)
    ahead, back = zeros(CR), zeros(CR)
    for j in range(5):
        ahead = jnp.where((wide & 15) == 10 + j, roll(get(XP[j]), 10 + j - 15, 1), ahead)
        back = jnp.where((wide & 15) == 10 + j, roll(get(XM[j]), 10 + j, 1), back)
    for k, packed in enumerate((ahead, back)):
        put(spot, 0, packed)
        for c in range(CB):
            c_out[pl.ds(2 * c + k, R, stride=FB), :] = spot[pl.ds(c, R, stride=CB), :]
    put(spot, 0, pack_y(get, YP1, YM1, 5, zeros(CR), CB))
    for c in range(CB):
        c_out[pl.ds(PY_AT + c, R, stride=FB), :] = spot[pl.ds(c, R, stride=CB), :]
        c_out[pl.ds(PY_AT + 2 + c, R, stride=FB), :] = zeros(R)
    top = roll(at(post, 6 * CR - 8, 8), 4, 0)
    bottom = roll(at(post, 6 * CR, 8), 4, 0)
    put(c_out, 2 * FR, jnp.where(row8 < 4, top, bottom))

    for c in copies[1:]:
        c.wait()
    meta = zeros(8)
    entries = []
    for b in range(FB):
        entries += [(b, k, nbr[b, k]) for k in range(4)]
        entries += [(b, M_PARENT + k, parent[k, b]) for k in range(2)]
    for c in range(CB):
        entries += [(c, M_CNBR + k, cnbr[c, k]) for k in range(6)]
        entries += [(c, M_CHILD + k, children[c, k]) for k in range(4)]
    for b, k, value in entries:
        meta = jnp.where((row8 == b) & (lane8 == k), value.astype(jnp.float32), meta)
    put(meta_out, 0, meta)


def fine_first_kernel(meta, pop, solid, coarse, post, mask, f_out, spot):
    s = jnp.where(solid[...] > 0, 1, 0)
    bits = s
    none = jnp.zeros_like(s)
    by_z = {0: lambda a: a}
    by_z[1] = lambda a: jnp.concatenate([a[-8:], a[:-8]], axis=0)
    by_z[-1] = lambda a: jnp.concatenate([a[8:], a[:8]], axis=0)
    by_y = {cy: move_y(s, cy, none, FB) for cy in (1, -1)}
    by_y[0] = s
    by_x = {(cx, cy): roll(by_y[cy], cx, 1) for cx in (1, -1) for cy in (-1, 0, 1)}
    for i in range(1, 19):
        cx, cy, cz = VELOCITIES[i]
        moved = by_z[cz](by_x[cx, cy] if cx else by_y[cy])
        bits = bits | (moved << i)
    put(mask, 0, bits)
    collide_rows(pop, post, FR, OMEGA_FINE, mask)
    put(f_out, ZS, at(coarse, 2 * FR, 8))
    put(f_out, ZS + 8, zeros(24))
    put(f_out, META, meta[...])
    send_faces(post, f_out, coarse, spot)


def onehot(rows, cols, source):
    row = lax.broadcasted_iota(jnp.int32, (rows, cols), 0)
    col = lax.broadcasted_iota(jnp.int32, (rows, cols), 1)
    return jnp.where(row == source(col), 1.0, 0.0).astype(jnp.bfloat16)


def exact_dot(a, b):
    result = None
    for _ in range(3):
        part = a.astype(jnp.bfloat16)
        a = a - part.astype(jnp.float32)
        term = jnp.dot(part, b, preferred_element_type=jnp.float32)
        result = term if result is None else result + term
    return result


def expand_kernel(f_own, e_own, e_two, x_in, e_halo, ez, gathered, meta, sem):
    device, _ = place()
    (fetch,) = fetch_meta(((f_own, meta),), sem)
    put(gathered, 0, e_own[...])
    put(gathered, E_ROWS, x_in[X_E : X_E + E_ROWS, :])
    put(gathered, 2 * E_ROWS, e_two[...])
    put(gathered, 3 * E_ROWS, x_in[X_E2 : X_E2 + E_ROWS, :])
    row, lane = iotas(16)
    x = lane & 15
    spread_x = onehot(128, 256, lambda m: ((m >> 7) * 4 + ((m & 127) >> 5)) * 16 + (m & 15))
    fetch.wait()
    for b in range(FB):
        p, q = number(meta, b, M_PARENT), number(meta, b, M_PARENT + 1)
        qy, qx = q >> 1, q & 1
        base = (((p >> 1) ^ device) & 3) * E_ROWS + qy * 2 + (p & 1)
        ex = exact_dot(gathered[pl.ds(base + qx * R, 8, stride=4), :], spread_x)
        spread_y = onehot(128, 128, lambda m: (m >> 4) * 16 + 8 * qx + ((m & 15) >> 1))
        ey = exact_dot(
            jnp.concatenate(
                [gathered[pl.ds(base + (2 + k) * R, 8, stride=4), :] for k in range(2)], axis=0
            ),
            spread_y,
        )
        for k in range(2):
            for yh in range(2):
                rows = pl.ds(8 * k + 4 * yh + b, 8, stride=16)
                e_halo[rows, :] = ex[:, 128 * yh : 128 * yh + 128]
                rows = pl.ds(PY_AT + 8 * k + 4 * yh + b, 8, stride=16)
                e_halo[rows, :] = ey[8 * yh : 8 * yh + 8]
        spread_z = onehot(
            128,
            256,
            lambda m: ((m >> 7) * 4 + ((m & 127) >> 5)) * 16 + 8 * qx + ((m & 15) >> 1),
        )
        ezs = exact_dot(gathered[pl.ds(base + 4 * R, 16, stride=4), :], spread_z)
        a0, a1 = ezs[:, :128], ezs[:, 128:]
        moves = {}
        moves[0, 0] = (a0, a1)
        moves[1, 0] = tuple(jnp.where(x == 0, a, roll(a, 1, 1)) for a in (a0, a1))
        moves[-1, 0] = tuple(jnp.where(x == 15, a, roll(a, -1, 1)) for a in (a0, a1))
        moves[0, 1] = (
            jnp.where(lane < 16, a0, roll(a0, 16, 1)),
            jnp.where(lane < 16, roll(a0, 16, 1), roll(a1, 16, 1)),
        )
        moves[0, -1] = (
            jnp.where(lane >= 112, roll(a1, -16, 1), roll(a0, -16, 1)),
            jnp.where(lane >= 112, a1, roll(a1, -16, 1)),
        )
        out = [a0, a1]
        for k, i in enumerate(ZP + ZM):
            moved = moves[VELOCITIES[i][:2]]
            out = [jnp.where(row == k, moved[h], out[h]) for h in range(2)]
        for h in range(2):
            ez[pl.ds(4 * h + b, 8, stride=8), :] = out[h][:8]
            ez[pl.ds(64 + 4 * h + b, 2, stride=8), :] = out[h][8:10]


def gather_halo(own, x_in, n_in, halo):
    for k, ref in enumerate((n_in, own, x_in)):
        put(halo, k * EDGES, ref[0:EDGES, :])


def gather_faces(meta, device, sign, e_halo, halo, faces):
    put(halo, 3 * EDGES, e_halo[...])
    for k in range(4):
        for b in range(FB):
            n = number(meta, b, k)
            safe = jnp.maximum(n, 0)
            which = jnp.clip(((safe >> 2) - device) * sign + 1, 0, 2)
            start = jnp.where(n >= 0, which * EDGES + (safe & 3), 3 * EDGES + b)
            start = start + (PY_AT if k >= 2 else 0)
            faces[pl.ds(k * FR + b, R, stride=FB), :] = halo[pl.ds(start, R, stride=FB), :]


def gather_edges(own, x_in, n_in, x_late, relayed, edges):
    for k, ref in enumerate((n_in, own, x_in)):
        put(edges, (k + 1) * R, ref[EDGES : EDGES + R, :])
    put(edges, 0, n_in[pl.ds(relayed, R), :])
    put(edges, 4 * R, x_late[...])


def corners(meta_n, meta_own, meta_x, device, sign, e_halo, edges, fixed, spot):
    row, lane = iotas()
    upper = (row & 1) == 1
    for b in range(FB):
        result = at(fixed, b * R)
        own_rows = e_halo[pl.ds(PY_AT + b, R, stride=FB), :]
        for side in range(2):
            n = number(meta_own, b, 2 + side)
            safe = jnp.maximum(n, 0)
            which = jnp.clip(((safe >> 2) - device) * sign + 1, 0, 2)
            row_n = safe & 3
            for end in range(2):
                i = ((7, 10), (9, 8))[side][end]
                p = (YP, YM)[side].index(i)
                edge_col = ((0, 1), (1, 0))[side][end]
                to = 112 * side + 15 * end
                m = jnp.where(
                    which == 0,
                    meta_n[row_n, end],
                    jnp.where(which == 1, meta_own[row_n, end], meta_x[row_n, end]),
                ).astype(jnp.int32)
                m_safe = jnp.maximum(m, 0)
                slot = jnp.clip(((m_safe >> 2) - device) * sign + 2, 0, 4)
                shift = (to - (2 * (m_safe & 3) + edge_col)) & 127
                sent = roll(at(edges, slot * R), shift, 1)
                own = roll(own_rows, to - (16 * p + 15 * end), 1)
                value = jnp.where(n < 0, own, sent)
                change = jnp.logical_or(n < 0, m >= 0)
                here = (lane == to) & (upper if side else jnp.logical_not(upper)) & change
                result = jnp.where(here, value, result)
        spot[pl.ds(b, R, stride=FB), :] = result


def with_corners(cells, i, corner):
    if i not in (7, 8, 9, 10):
        return cells
    row, lane = iotas(cells.shape[0])
    column, upper = {7: (0, 0), 10: (15, 0), 9: (112, 1), 8: (127, 1)}[i]
    return jnp.where((lane == column) & (((row // FB) & 1) == upper), corner, cells)


def fixed_corners(meta_n, meta_own, meta_x, device, sign, group, from_n, fixed, spare):
    _, lane = iotas()
    npart = device - sign
    for b in range(FB):
        result = zeros(R)
        for side in range(2):
            safe = jnp.maximum(number(meta_own, b, 2 + side), 0)
            which = jnp.clip(((safe >> 2) - device) * sign + 1, 0, 2)
            row_n = safe & 3
            p, q = (
                jnp.where(
                    which == 0,
                    meta_n[row_n, M_PARENT + k],
                    jnp.where(
                        which == 1, meta_own[row_n, M_PARENT + k], meta_x[row_n, M_PARENT + k]
                    ),
                ).astype(jnp.int32)
                for k in range(2)
            )
            near = ((p >> 1) ^ device) & 3
            far = ((p >> 1) ^ npart) & 3
            quad = jnp.where(which == 0, at(from_n, far * 8, 8), at(group, near * 8, 8))
            base = (2 * b + side) * R
            for k in range(4):
                spare[pl.ds(base + k, 8, stride=4), :] = quad
            rows = at(spare, base)
            for end in range(2):
                to = 112 * side + 15 * end
                source = ((p & 1) * 4 + q) * 4 + 2 * side + end
                result = jnp.where(lane == to, roll(rows, (to - source) & 127, 1), result)
        put(fixed, b * R, result)


def stream_fine(post, mask, faces, ez, dst):
    put(dst, 0, at(post, 0, FR))
    for h in range(2):
        bits = at(mask, h * 64, 64)
        solid = (bits & 1) > 0
        for i in range(1, 19):
            cx, cy, cz = VELOCITIES[i]
            start = max(h * 64 - 8 * cz, 0)
            stop = min(h * 64 + 64 - 8 * cz, FR)
            size = stop - start
            g = at(post, i * FR + start, size)
            if cx == 1:
                g = move_x(g, 1, roll(at(faces, start, size), -XP.index(i), 1))
            elif cx == -1:
                g = move_x(g, -1, roll(at(faces, FR + start, size), 10 - XM.index(i), 1))
            if cy == 1:
                side = roll(at(faces, 2 * FR + start, size), cx - 16 * YP.index(i), 1)
                g = move_y(g, 1, side, FB)
            elif cy == -1:
                side = roll(at(faces, 3 * FR + start, size), 112 + cx - 16 * YM.index(i), 1)
                g = move_y(g, -1, side, FB)
            if size < 64:
                k = ZP.index(i) if cz == 1 else 5 + ZM.index(i)
                layer = at(ez, 8 * k, 8)
                g = jnp.concatenate([layer, g] if cz == 1 else [g, layer], axis=0)
            here = h * 64
            g = jnp.where((bits & (1 << i)) > 0, at(post, OPPOSITE[i] * FR + here, 64), g)
            put(dst, i * FR + here, jnp.where(solid, at(post, i * FR + here, 64), g))


class CoarseSides:
    def __init__(self, meta, device, sign):
        self.has, self.which, self.slot = [], [], []
        for k in range(6):
            index = [number(meta, c, M_CNBR + k) for c in range(CB)]
            safe = [jnp.maximum(n, 0) for n in index]
            self.has.append(index)
            self.which.append(
                [jnp.clip(((n >> 1) - device) * sign + 1, 0, 2) * EDGES for n in safe]
            )
            self.slot.append([n & 1 for n in safe])

    def exists(self, k, rows):
        row, _ = iotas(rows)
        first, second = self.has[k]
        return jnp.where((row & 1) == 0, first, second) >= 0

    def face(self, k, halo, spot):
        for c in range(CB):
            if k < 2:
                start = self.which[k][c] + 2 * self.slot[k][c] + k
            else:
                start = self.which[k][c] + PY_AT + self.slot[k][c]
            spot[pl.ds(k * CR + c, R, stride=CB), :] = halo[pl.ds(start, R, stride=FB), :]

    def layers(self, k, halo, spot, count):
        for c in range(CB):
            for n in range(count):
                start = self.which[k][c] + ZS + 8 * n + 4 * (k - 4) + self.slot[k][c]
                spot[pl.ds(8 * n + 4 * (k - 4) + c, 2, stride=2), :] = halo[
                    pl.ds(start, 2, stride=2), :
                ]


def first_stream_kernel(
    post,
    mask,
    f_own,
    e_own,
    e_two,
    x_in,
    n_in,
    cpost,
    e_halo,
    ez,
    new,
    fixed,
    cmid,
    c_out,
    group,
    halo,
    faces,
    spare,
    cfaces,
    clayers,
    meta_n,
    meta_own,
    meta_x,
    sem,
):
    device, sign = place()
    copies = fetch_meta(((n_in, meta_n), (f_own, meta_own), (x_in, meta_x)), sem)
    put(group, 0, e_own[EC_AT:E_ROWS, :])
    put(group, 8, x_in[X_E + EC_AT : X_E + E_ROWS, :])
    put(group, 16, e_two[EC_AT:E_ROWS, :])
    put(group, 24, x_in[X_E2 + EC_AT : X_E2 + E_ROWS, :])
    gather_halo(f_own, x_in, n_in, halo)
    put(c_out, 0, zeros(2 * FR))
    for c in copies:
        c.wait()
    gather_faces(meta_own, device, sign, e_halo, halo, faces)

    row8, _ = iotas(8)
    sides = CoarseSides(meta_own, device, sign)
    for k in range(4):
        sides.face(k, halo, cfaces)
    for k in (4, 5):
        sides.layers(k, halo, clayers, 1)
    put(cmid, 0, at(cpost, 0, CR))
    for i in range(1, 19):
        cx, cy, cz = VELOCITIES[i]
        a = at(cpost, i * CR, CR)
        k = {1: 0, -1: 1}[cx] if cx else {1: 2, -1: 3}[cy] if cy else {1: 4, -1: 5}[cz]
        if cx:
            column = -10 - XP.index(i) if cx == 1 else 5 - XM.index(i)
            side = roll(at(cfaces, k * CR, CR), column, 1)
            g = move_x(a, cx, jnp.where(sides.exists(k, CR), side, a))
        elif cy:
            column = -16 * (5 + YP1.index(i)) if cy == 1 else 112 - 16 * (5 + YM1.index(i))
            side = roll(at(cfaces, k * CR, CR), column, 1)
            g = move_y(a, cy, jnp.where(sides.exists(k, CR), side, a), CB)
        else:
            own = a[:8] if cz == 1 else a[-8:]
            g = move_z_coarse(a, cz, jnp.where(sides.exists(k, 8), clayers[0:8, :], own))
        put(cmid, i * CR, g)
    put(cfaces, 0, pack_y(lambda i: at(cmid, i * CR, CR), YP2, YM2, 5, zeros(CR), CB))
    for c in range(CB):
        c_out[pl.ds(PY_AT + c, R, stride=FB), :] = cfaces[pl.ds(c, R, stride=CB), :]
    for k in range(4):
        top = roll(at(cmid, (ZP2[k] + 1) * CR - 8, 8), 4, 0)
        bottom = roll(at(cmid, ZM2[k] * CR, 8), 4, 0)
        put(c_out, 2 * FR + 8 * k, jnp.where(row8 < 4, top, bottom))

    fixed_corners(
        meta_n,
        meta_own,
        meta_x,
        device,
        sign,
        group,
        n_in.at[pl.ds(N_EC, 32)],
        fixed,
        spare,
    )
    stream_fine(post, mask, faces, ez, new)


def second_collision_kernel(
    new,
    mask,
    f_own,
    x_in,
    n_in,
    x_late,
    e_halo,
    fixed,
    coarse,
    post,
    f_out,
    spot,
    edges,
    meta_n,
    meta_own,
    meta_x,
    sem,
):
    device, sign = place()
    copies = fetch_meta(((n_in, meta_n), (f_own, meta_own), (x_in, meta_x)), sem)
    gather_edges(f_own, x_in, n_in, x_late, N_EDGE, edges)
    put(f_out, ZS, coarse[pl.ds(2 * FR, R), :])
    for c in copies:
        c.wait()
    corners(meta_n, meta_own, meta_x, device, sign, e_halo, edges, fixed, spot)
    collide_rows(new, post, FR, OMEGA_FINE, mask, spot)
    send_faces(post, f_out, coarse, spot)


def second_stream_kernel(
    post, mask, f_own, x_in, n_in, e_halo, ez, f_first, new, halo, faces, meta, sem
):
    device, sign = place()
    (fetch,) = fetch_meta(((f_first, meta),), sem)
    gather_halo(f_own, x_in, n_in, halo)
    fetch.wait()
    gather_faces(meta, device, sign, e_halo, halo, faces)
    stream_fine(post, mask, faces, ez, new)


def coarsen_kernel(
    new,
    f_own,
    x_in,
    n_in,
    x_late,
    e_halo,
    fixed,
    f_first,
    x_first,
    n_first,
    cornered,
    means,
    spot,
    edges,
    meta_n,
    meta_own,
    meta_x,
    sem,
):
    device, sign = place()
    copies = fetch_meta(((n_first, meta_n), (f_first, meta_own), (x_first, meta_x)), sem)
    gather_edges(f_own, x_in, n_in, x_late, F2_ROWS, edges)
    for c in copies:
        c.wait()
    corners(meta_n, meta_own, meta_x, device, sign, e_halo, edges, fixed, spot)
    for i in range(7, 11):
        put(cornered, (i - 7) * FR, with_corners(at(new, i * FR, FR), i, spot[...]))

    row = lax.broadcasted_iota(jnp.int32, (128, 128), 0)
    col = lax.broadcasted_iota(jnp.int32, (128, 128), 1)
    target = lambda yh, h: (yh * 4 + (row >> 5)) * 16 + ((row & 15) >> 1) + 8 * h
    mats = [
        [jnp.where(col == target(yh, h), 0.125, 0.0).astype(jnp.bfloat16) for yh in range(2)]
        for h in range(2)
    ]
    for pair in range(2):
        for ref, base, first, last in (
            (new, 0, 0, 7),
            (cornered, 7, 7, 11),
            (new, 0, 11, 19),
        ):
            rows = 8 * (last - first)
            total_rows = None
            for h in range(2):
                for yh in range(2):
                    start = (first - base) * FR + 4 * yh + 2 * pair + h
                    z0 = ref[pl.ds(start, rows, stride=16), :]
                    z1 = ref[pl.ds(start + 8, rows, stride=16), :]
                    part = exact_dot(z0 + z1, mats[h][yh])
                    total_rows = part if total_rows is None else total_rows + part
            put(means, pair * 19 * 8 + 8 * first, total_rows)


def tail_kernel(
    f_first,
    new,
    cornered,
    f_own,
    x_in,
    n_in,
    cmid,
    fine_out,
    cpassed,
    halo,
    cfaces,
    clayers,
    meta_own,
    sem,
    out_sem,
):
    device, sign = place()
    (fetch,) = fetch_meta(((f_first, meta_own),), sem)
    pieces = (
        (new, 0, 0, 7 * FR),
        (cornered, 0, 7 * FR, 4 * FR),
        (new, 11 * FR, 11 * FR, 8 * FR),
    )
    outs = [
        pltpu.make_async_copy(
            ref.at[pl.ds(source, rows)], fine_out.at[pl.ds(to, rows)], out_sem.at[k]
        )
        for k, (ref, source, to, rows) in enumerate(pieces)
    ]
    for c in outs:
        c.start()
    gather_halo(f_own, x_in, n_in, halo)
    fetch.wait()
    sides = CoarseSides(meta_own, device, sign)
    for k in (2, 3):
        sides.face(k, halo, cfaces)
    for k in (4, 5):
        sides.layers(k, halo, clayers, 4)
    for i in range(19):
        a = at(cmid, i * CR, CR)
        g = a
        if i in YP2 or i in YM2:
            cy = 1 if i in YP2 else -1
            k = 2 if cy == 1 else 3
            column = -16 * (5 + YP2.index(i)) if cy == 1 else 112 - 16 * (5 + YM2.index(i))
            side = roll(at(cfaces, k * CR, CR), column, 1)
            g = move_y(a, cy, jnp.where(sides.exists(k, CR), side, a), CB)
        elif i in ZP2 or i in ZM2:
            cz = 1 if i in ZP2 else -1
            k = 4 if cz == 1 else 5
            n = (ZP2 if cz == 1 else ZM2).index(i)
            own = a[:8] if cz == 1 else a[-8:]
            side = jnp.where(sides.exists(k, 8), at(clayers, 8 * n, 8), own)
            g = move_z_coarse(a, cz, side)
        put(cpassed, i * CR, g)
    for c in outs:
        c.wait()


def coarse_last_kernel(
    f_first, cpassed, own, two, x_in, coarse_out, gathered, meta, sem
):
    device, _ = place()
    (fetch,) = fetch_meta(((f_first, meta),), sem)
    put(gathered, 0, own[...])
    put(gathered, K_ROWS, x_in[0:K_ROWS, :])
    put(gathered, 2 * K_ROWS, two[...])
    put(gathered, 3 * K_ROWS, x_in[K_ROWS : 2 * K_ROWS, :])
    coarse_out[...] = cpassed[...]
    _, lane = iotas(8)
    x_half = (lane >> 3) & 1
    fetch.wait()
    for c in range(CB):
        for qy in range(2):
            children = [number(meta, c, M_CHILD + 2 * qy + qx) for qx in range(2)]
            starts, shifts = [], []
            for qx in range(2):
                child = jnp.maximum(children[qx], 0)
                slot = ((child >> 2) ^ device) & 3
                starts.append(slot * K_ROWS + ((child & 3) >> 1) * (19 * 8))
                shifts.append((8 * (qx - (child & 1))) & 127)
            index = jnp.where(x_half == 0, children[0], children[1])
            for i in range(19):
                rows = pl.ds(i * CR + 2 * qy + c, 8, stride=4)
                values = [roll(at(gathered, starts[qx] + 8 * i, 8), shifts[qx], 1) for qx in (0, 1)]
                value = jnp.where(x_half == 0, values[0], values[1])
                coarse_out[rows, :] = jnp.where(index >= 0, value, cpassed[rows, :])


VMEM = pl.BlockSpec(memory_space=pltpu.VMEM)
HBM = pl.BlockSpec(memory_space=pltpu.HBM)


def rows_of(n, dtype=jnp.float32):
    return jax.ShapeDtypeStruct((n, 128), dtype)


def scratch(n, dtype=jnp.float32):
    return pltpu.VMEM((n, 128), dtype)


def call(kernel, name, specs, outs, scratches, out_specs=None):
    return pl.pallas_call(
        kernel,
        name=name,
        in_specs=specs,
        out_specs=out_specs or [VMEM] * len(outs),
        out_shape=outs,
        scratch_shapes=scratches,
        cost_estimate=pl.CostEstimate(flops=1 << 20, bytes_accessed=4 << 20, transcendentals=0),
        compiler_params=pltpu.CompilerParams(vmem_limit_bytes=32 * 1024 * 1024),
    )


def meta_scratch(n=3):
    return [pltpu.SMEM((8, 128), jnp.float32)] * n + [pltpu.SemaphoreType.DMA((n,))]


def exchange(rows, devices, partner):
    return lax.ppermute(rows, AXES, [(i, partner(i)) for i in range(devices)])


def as_rows(cells, directions):
    blocks = cells.shape[0]
    cells = cells.reshape(blocks, directions, R, 128)
    return cells.transpose(1, 2, 0, 3).reshape(directions * R * blocks, 128)


def as_cells(rows, blocks):
    return rows.reshape(19, R, blocks, 128).transpose(2, 0, 1, 3).reshape(blocks, 19, R * 128)


def on_device(fine_pop, coarse_pop, fine_nbr, coarse_nbr, parent, children, solid):
    devices = lax.axis_size(AXES)
    by_one = lambda a: exchange(a, devices, lambda i: i ^ 1)
    by_two = lambda a: exchange(a, devices, lambda i: i ^ 2)
    odd_even = lambda a: exchange(a, devices, lambda i: (((i + 1) ^ 1) - 1) % devices)
    parent = parent.T
    small = lambda a: pltpu.SMEM(a.shape, jnp.int32)
    inputs = (
        as_rows(coarse_pop, 19),
        as_rows(fine_pop, 19),
        as_rows(solid, 1),
        fine_nbr,
        parent,
        coarse_nbr,
        children,
    )

    cpost, e_own, c_own, fine_raw, solid_raw, meta = call(
        coarse_first_kernel,
        "coarse_first",
        [HBM] * 7,
        [
            rows_of(C_ALL),
            rows_of(E_ROWS),
            rows_of(C_ROWS),
            rows_of(F_ALL),
            rows_of(FR, jnp.int32),
            rows_of(8),
        ],
        [
            scratch(C_ALL),
            scratch(CR),
            small(fine_nbr),
            small(parent),
            small(coarse_nbr),
            small(children),
            pltpu.SemaphoreType.DMA((7,)),
        ],
    )(*(pltpu.with_memory_space_constraint(a, pltpu.HBM) for a in inputs))
    e_two = by_two(e_own)
    post, mask, f_own = call(
        fine_first_kernel,
        "fine_first",
        [VMEM] * 4,
        [rows_of(F_ALL), rows_of(FR, jnp.int32), rows_of(F_ROWS)],
        [scratch(FR)],
    )(meta, fine_raw, solid_raw, c_own)

    x_in = by_one(jnp.concatenate([f_own, e_own, e_two]))
    n_in = odd_even(
        jnp.concatenate(
            [
                f_own,
                x_in[EDGES:META],
                e_own[EC_AT:],
                x_in[X_E + EC_AT : X_E2],
                e_two[EC_AT:],
                x_in[X_E2 + EC_AT :],
            ]
        )
    )
    e_halo, ez = call(
        expand_kernel,
        "expand",
        [VMEM] * 4,
        [rows_of(2 * FR), rows_of(80)],
        [scratch(4 * E_ROWS)] + meta_scratch(1),
    )(f_own, e_own, e_two, x_in)
    far_edges, ez = lax.optimization_barrier((n_in[EDGES:META], ez))
    x_late = by_one(far_edges)
    new, fixed, cmid, c2_own = call(
        first_stream_kernel,
        "first_stream",
        [VMEM] * 10,
        [rows_of(F_ALL), rows_of(FB * R), rows_of(C_ALL), rows_of(2 * FR + R)],
        [
            scratch(32),
            scratch(HALO),
            scratch(4 * FR),
            scratch(8 * R),
            scratch(4 * CR),
            scratch(8),
        ]
        + meta_scratch(),
    )(post, mask, f_own, e_own, e_two, x_in, n_in, cpost, e_halo, ez)
    post2, f2_own = call(
        second_collision_kernel,
        "second_collision",
        [VMEM] * 9,
        [rows_of(F_ALL), rows_of(F2_ROWS)],
        [scratch(FR), scratch(5 * R)] + meta_scratch(),
    )(new, mask, f_own, x_in, n_in, x_late, e_halo, fixed, c2_own)

    x2_in = by_one(f2_own)
    n2_in = odd_even(jnp.concatenate([f2_own, x2_in[EDGES:META]]))
    x2_late = by_one(n2_in[EDGES:META])
    (new2,) = call(
        second_stream_kernel,
        "second_stream",
        [VMEM] * 8,
        [rows_of(F_ALL)],
        [scratch(HALO), scratch(4 * FR)] + meta_scratch(1),
    )(post2, mask, f2_own, x2_in, n2_in, e_halo, ez, f_own)
    cornered, means = call(
        coarsen_kernel,
        "coarsen",
        [VMEM] * 10,
        [rows_of(4 * FR), rows_of(K_ROWS)],
        [scratch(FR), scratch(5 * R)] + meta_scratch(),
    )(new2, f2_own, x2_in, n2_in, x2_late, e_halo, fixed, f_own, x_in, n_in)

    k_two = by_two(means)
    fine_out, cpassed = call(
        tail_kernel,
        "tail",
        [VMEM] * 7,
        [rows_of(F_ALL), rows_of(C_ALL)],
        [scratch(3 * EDGES), scratch(4 * CR), scratch(R)]
        + meta_scratch(1)
        + [pltpu.SemaphoreType.DMA((3,))],
        [HBM, VMEM],
    )(f_own, new2, cornered, f2_own, x2_in, n2_in, cmid)
    k_two, cpassed = lax.optimization_barrier((k_two, cpassed))
    k_one = by_one(jnp.concatenate([means, k_two]))
    (coarse_out,) = call(
        coarse_last_kernel,
        "coarse_last",
        [VMEM] * 5,
        [rows_of(C_ALL)],
        [scratch(4 * K_ROWS)] + meta_scratch(1),
    )(f_own, cpassed, means, k_two, k_one)
    return as_cells(fine_out, FB), as_cells(coarse_out, CB)


def solution(mesh):
    rows = P(AXES, None)
    blocks = P(AXES, None, None)
    return jax.shard_map(
        on_device,
        mesh=mesh,
        in_specs=(blocks, blocks, rows, rows, rows, rows, rows),
        out_specs=(blocks, blocks),
        check_vma=False,
    )
```

```python
import jax
import jax.numpy as jnp
from jax import lax
from jax.experimental import pallas as pl
from jax.experimental.pallas import tpu as pltpu
from jax.sharding import PartitionSpec as P

AXES = ("gx", "gy")
VELOCITIES = (
    (0, 0, 0),
    (1, 0, 0),
    (-1, 0, 0),
    (0, 1, 0),
    (0, -1, 0),
    (0, 0, 1),
    (0, 0, -1),
    (1, 1, 0),
    (-1, -1, 0),
    (1, -1, 0),
    (-1, 1, 0),
    (1, 0, 1),
    (-1, 0, -1),
    (1, 0, -1),
    (-1, 0, 1),
    (0, 1, 1),
    (0, -1, -1),
    (0, 1, -1),
    (0, -1, 1),
)
WEIGHTS = (1.0 / 3.0,) + (1.0 / 18.0,) * 6 + (1.0 / 36.0,) * 12
OPPOSITE = (0, 2, 1, 4, 3, 6, 5, 8, 7, 10, 9, 12, 11, 14, 13, 16, 15, 18, 17)
OMEGA_COARSE = 1.6
OMEGA_FINE = 1.0 / (2.0 * (1.0 / 1.6 - 0.5) + 0.5)

XP = (1, 7, 9, 11, 13)
XM = (2, 8, 10, 12, 14)
YP = (3, 7, 10, 15, 17)
YM = (4, 8, 9, 16, 18)
ZP = (5, 11, 14, 15, 18)
ZM = (6, 12, 13, 16, 17)
YP1, YM1 = (3, 15, 17), (4, 16, 18)
YP2, YM2 = (7, 10), (8, 9)
ZP2, ZM2 = (11, 14, 15, 18), (12, 13, 16, 17)


R = 32
FB, CB = 4, 2
FR, CR = FB * R, CB * R
F_ALL, C_ALL = 19 * FR, 19 * CR
PY_AT = FR
ZS = 2 * FR
EDGES = ZS + 8
META = EDGES + R
F_ROWS = META + 8
EDGES2 = ZS + R
F2_ROWS = EDGES2 + R
N_EC = F_ROWS
EC_AT = 4 * R + 40
E_ROWS = EC_AT + 8
K_ROWS = 2 * 19 * 8
HALO = 3 * EDGES2 + 2 * FR
X_E = F_ROWS
X_E2 = X_E + E_ROWS
M_PARENT, M_CNBR, M_CHILD = 4, 8, 16


def iotas(rows=R):
    row = lax.broadcasted_iota(jnp.int32, (rows, 128), 0)
    lane = lax.broadcasted_iota(jnp.int32, (rows, 128), 1)
    return row, lane


def roll(a, shift, axis):
    if isinstance(shift, int):
        shift = shift % a.shape[axis]
        if shift == 0:
            return a
    return pltpu.roll(a, shift, axis)


def at(ref, start, size=R):
    if not isinstance(start, int):
        start = pl.multiple_of(start, 8)
    return ref[pl.ds(start, size), :]


def put(ref, start, value):
    if not isinstance(start, int):
        start = pl.multiple_of(start, 8)
    ref[pl.ds(start, value.shape[0]), :] = value


def zeros(rows):
    return jnp.zeros((rows, 128), jnp.float32)


def total(terms):
    while len(terms) > 1:
        pairs = [terms[k] + terms[k + 1] for k in range(0, len(terms) - 1, 2)]
        terms = pairs + terms[len(terms) - len(terms) % 2 :]
    return terms[0]


def collide(f, rate):
    rho = total(f)
    mom = []
    for axis in range(3):
        plus = [f[i] for i in range(19) if VELOCITIES[i][axis] == 1]
        minus = [f[i] for i in range(19) if VELOCITIES[i][axis] == -1]
        mom.append(total(plus) - total(minus))
    inv = 1.0 / rho
    u = [m * inv for m in mom]
    base = 1.0 - 1.5 * (u[0] * u[0] + u[1] * u[1] + u[2] * u[2])
    scaled = {w: (rate * w) * rho for w in sorted(set(WEIGHTS))}
    keep = 1.0 - rate
    out = [None] * 19
    out[0] = keep * f[0] + scaled[WEIGHTS[0]] * base
    for i in range(1, 19, 2):
        proj = None
        for axis in range(3):
            c = VELOCITIES[i][axis]
            if c:
                term = u[axis]
                if proj is None:
                    proj = term if c > 0 else -term
                else:
                    proj = proj + term if c > 0 else proj - term
        even = base + 4.5 * (proj * proj)
        odd = 3.0 * proj
        w = scaled[WEIGHTS[i]]
        out[i] = keep * f[i] + w * (even + odd)
        out[i + 1] = keep * f[i + 1] + w * (even - odd)
    return out


def collide_rows(src, dst, rows, rate, mask=None, corner=None):
    def body(v, carry):
        f = [at(src, i * rows + v * 16, 16) for i in range(19)]
        if corner is not None:
            edge = at(corner, v * 16, 16)
            f = [with_corners(f[i], i, edge) for i in range(19)]
        post = collide(f, rate)
        if mask is not None:
            solid = (at(mask, v * 16, 16) & 1) > 0
            post = [jnp.where(solid, f[i], post[i]) for i in range(19)]
        for i in range(19):
            put(dst, i * rows + v * 16, post[i])
        return carry

    lax.fori_loop(0, rows // 16, body, 0)


def upper_of(rows, blocks):
    row, _ = iotas(rows)
    return ((row // blocks) & 1) == 1


def swap_halves(a, blocks):
    if blocks == 4:
        rows = a.shape[0]
        return pltpu.roll(a.reshape(rows // 8, 8, 128), 4, 1).reshape(rows, 128)
    return jnp.where(upper_of(a.shape[0], blocks), roll(a, blocks, 0), roll(a, -blocks, 0))


def pack_x(get, packed, first=0):
    _, lane = iotas(packed.shape[0])
    x = lane & 15
    for j in range(5):
        packed = jnp.where(x == first + j, roll(get(XP[j]), first + j - 15, 1), packed)
        packed = jnp.where(x == first + 5 + j, roll(get(XM[j]), first + 5 + j, 1), packed)
    return packed


def pack_y(get, plus, minus, first, rest, blocks):
    rows = rest.shape[0]
    _, lane = iotas(rows)
    upper = upper_of(rows, blocks)
    group = lane >> 4
    packed = zeros(rows)
    for k in range(len(plus)):
        p = first + k
        one = jnp.where(upper, roll(get(plus[k]), 16 * p - 112, 1), roll(get(minus[k]), 16 * p, 1))
        packed = jnp.where(group == p, one, packed)
    packed = swap_halves(packed, blocks)
    return jnp.where((group >= first) & (group < first + len(plus)), packed, rest)


def pack_edges(get, rows):
    _, lane = iotas(rows)
    upper = upper_of(rows, FB)
    first = jnp.where(upper, roll(get(7), -127, 1), get(8))
    second = jnp.where(upper, roll(get(10), 1 - 112, 1), roll(get(9), 1 - 15, 1))
    return swap_halves(jnp.where(lane == 0, first, second), FB)


def move_x(a, cx, halo):
    _, lane = iotas(a.shape[0])
    x = lane & 15
    if cx == 1:
        return jnp.where(x == 0, halo, roll(a, 1, 1))
    return jnp.where(x == 15, halo, roll(a, -1, 1))


def move_y(a, cy, halo, blocks):
    _, lane = iotas(a.shape[0])
    upper = upper_of(a.shape[0], blocks)
    near = roll(a, 16 * cy, 1)
    if cy == 1:
        return jnp.where(lane < 16, jnp.where(upper, swap_halves(near, blocks), halo), near)
    return jnp.where(lane >= 112, jnp.where(upper, halo, swap_halves(near, blocks)), near)


def move_z_coarse(a, cz, halo8):
    row, _ = iotas(8)
    near = roll(a, 4 * cz, 0)
    if cz == 1:
        return jnp.concatenate([jnp.where(row < 4, halo8, near[:8]), near[8:]], axis=0)
    return jnp.concatenate([near[:-8], jnp.where(row >= 4, halo8, near[-8:])], axis=0)


def send_faces(post, out, edges, coarse, spot):
    for h in range(2):
        rows = h * 64
        get = lambda i: at(post, i * FR + rows, 64)
        put(out, rows, pack_x(get, at(coarse, rows, 64)))
        put(out, PY_AT + rows, pack_y(get, YP, YM, 0, at(coarse, PY_AT + rows, 64), FB))
        put(spot, rows, pack_edges(get, 64))
    _, lane = iotas()
    device, _ = place()
    first = 8 * (device & 1)
    packed = zeros(R)
    for b in range(FB):
        one = roll(spot[pl.ds(b, R, stride=FB), :], first + 2 * b, 1)
        packed = jnp.where((lane >> 1) == (first >> 1) + b, one, packed)
    put(out, edges, packed)


def place():
    device = lax.axis_index("gx") * lax.axis_size("gy") + lax.axis_index("gy")
    sign = 1 - 2 * (device & 1)
    return device, sign


def number(meta, row, column):
    return meta[row, column].astype(jnp.int32)


def fetch_meta(pairs, sem, start=META):
    copies = [
        pltpu.make_async_copy(ref.at[pl.ds(start, 8)], dst, sem.at[k])
        for k, (ref, dst) in enumerate(pairs)
    ]
    for c in copies:
        c.start()
    return copies


def coarse_first_kernel(
    pop_hbm,
    nbr_hbm,
    parent_hbm,
    cnbr_hbm,
    children_hbm,
    raw,
    e_out,
    meta_out,
    nbr,
    parent,
    cnbr,
    children,
    sem,
):
    copies = [
        pltpu.make_async_copy(src, dst, sem.at[k])
        for k, (src, dst) in enumerate(
            (
                (pop_hbm, raw),
                (nbr_hbm, nbr),
                (parent_hbm, parent),
                (cnbr_hbm, cnbr),
                (children_hbm, children),
            )
        )
    ]
    for c in copies:
        c.start()
    copies[0].wait()
    _, lane = iotas()
    row8, lane8 = iotas(8)
    x = lane & 15
    half = lambda i: at(raw, i * CR)
    for qx in range(2):
        packed = zeros(R)
        for j in range(5):
            packed = jnp.where(x == j, roll(half(XP[j]), j - 8 * qx, 1), packed)
            packed = jnp.where(x == 5 + j, roll(half(XM[j]), 5 + j - 8 * qx - 7, 1), packed)
        put(e_out, qx * R, packed)
    low, high = zeros(R), zeros(R)
    for p in range(5):
        low = jnp.where((lane >> 4) == p, roll(half(YP[p]), 16 * p, 1), low)
        high = jnp.where((lane >> 4) == p, roll(half(YM[p]), 16 * p - 112, 1), high)
    put(e_out, 2 * R, low)
    put(e_out, 3 * R, high)
    for k in range(5):
        e_out[pl.ds(4 * R + 4 * k, 4), :] = raw[pl.ds(ZP[k] * CR, 4), :]
        e_out[pl.ds(4 * R + 20 + 4 * k, 4), :] = raw[pl.ds(ZM[k] * CR + 28, 4), :]
    corner = zeros(8)
    for c in range(CB):
        for q in range(4):
            for e, (i, yq, xq) in enumerate(((7, 7, 0), (10, 7, 7), (9, 0, 0), (8, 0, 7))):
                to = (c * 4 + q) * 4 + e
                rows = raw[pl.ds(i * CR + (q // 2) * 2 + c, 8, stride=4), :]
                rows = roll(rows, to - (yq * 16 + 8 * (q % 2) + xq), 1)
                corner = jnp.where(lane8 == to, rows, corner)
    device, _ = place()
    put(e_out, EC_AT, roll(corner, 32 * (device & 3), 1))

    for c in copies[1:]:
        c.wait()
    meta = zeros(8)
    entries = []
    for b in range(FB):
        entries += [(b, k, nbr[b, k]) for k in range(4)]
        entries += [(b, M_PARENT + k, parent[k, b]) for k in range(2)]
    for c in range(CB):
        entries += [(c, M_CNBR + k, cnbr[c, k]) for k in range(6)]
        entries += [(c, M_CHILD + k, children[c, k]) for k in range(4)]
    for b, k, value in entries:
        meta = jnp.where((row8 == b) & (lane8 == k), value.astype(jnp.float32), meta)
    put(meta_out, 0, meta)


def fine_first_kernel(
    meta,
    raw,
    pop_hbm,
    solid_hbm,
    cpost,
    post,
    mask,
    f_out,
    pop,
    solid,
    coarse,
    spot,
    sem,
):
    copies = [
        pltpu.make_async_copy(pop_hbm, pop, sem.at[0]),
        pltpu.make_async_copy(solid_hbm, solid, sem.at[1]),
    ]
    for c in copies:
        c.start()
    row8, _ = iotas(8)
    collide_rows(raw, cpost, CR, OMEGA_COARSE)
    get = lambda i: at(cpost, i * CR, CR)
    _, wide = iotas(CR)
    ahead, back = zeros(CR), zeros(CR)
    for j in range(5):
        ahead = jnp.where((wide & 15) == 10 + j, roll(get(XP[j]), 10 + j - 15, 1), ahead)
        back = jnp.where((wide & 15) == 10 + j, roll(get(XM[j]), 10 + j, 1), back)
    for k, packed in enumerate((ahead, back)):
        put(spot, 0, packed)
        for c in range(CB):
            coarse[pl.ds(2 * c + k, R, stride=FB), :] = spot[pl.ds(c, R, stride=CB), :]
    put(spot, 0, pack_y(get, YP1, YM1, 5, zeros(CR), CB))
    for c in range(CB):
        coarse[pl.ds(PY_AT + c, R, stride=FB), :] = spot[pl.ds(c, R, stride=CB), :]
        coarse[pl.ds(PY_AT + 2 + c, R, stride=FB), :] = zeros(R)
    top = roll(at(cpost, 6 * CR - 8, 8), 4, 0)
    bottom = roll(at(cpost, 6 * CR, 8), 4, 0)
    put(coarse, 2 * FR, jnp.where(row8 < 4, top, bottom))

    for c in copies:
        c.wait()
    s = jnp.where(solid[...] > 0, 1, 0)
    bits = s
    none = jnp.zeros_like(s)
    by_z = {0: lambda a: a}
    by_z[1] = lambda a: jnp.concatenate([a[-8:], a[:-8]], axis=0)
    by_z[-1] = lambda a: jnp.concatenate([a[8:], a[:8]], axis=0)
    by_y = {cy: move_y(s, cy, none, FB) for cy in (1, -1)}
    by_y[0] = s
    by_x = {(cx, cy): roll(by_y[cy], cx, 1) for cx in (1, -1) for cy in (-1, 0, 1)}
    for i in range(1, 19):
        cx, cy, cz = VELOCITIES[i]
        moved = by_z[cz](by_x[cx, cy] if cx else by_y[cy])
        bits = bits | (moved << i)
    put(mask, 0, bits)
    collide_rows(pop, post, FR, OMEGA_FINE, mask)
    put(f_out, ZS, at(coarse, 2 * FR, 8))
    put(f_out, META, meta[...])
    send_faces(post, f_out, EDGES, coarse, spot)


def onehot(rows, cols, source):
    row = lax.broadcasted_iota(jnp.int32, (rows, cols), 0)
    col = lax.broadcasted_iota(jnp.int32, (rows, cols), 1)
    return jnp.where(row == source(col), 1.0, 0.0).astype(jnp.bfloat16)


def exact_dot(a, b):
    result = None
    for _ in range(3):
        part = a.astype(jnp.bfloat16)
        a = a - part.astype(jnp.float32)
        term = jnp.dot(part, b, preferred_element_type=jnp.float32)
        result = term if result is None else result + term
    return result


def first_local_kernel(
    f_own, e_own, e_two, x_in, post, mask, e_halo, ez, local, gathered, meta, sem
):
    device, _ = place()
    (fetch,) = fetch_meta(((f_own, meta),), sem)
    put(gathered, 0, e_own[...])
    put(gathered, E_ROWS, x_in[X_E : X_E + E_ROWS, :])
    put(gathered, 2 * E_ROWS, e_two[...])
    put(gathered, 3 * E_ROWS, x_in[X_E2 : X_E2 + E_ROWS, :])
    row, lane = iotas(16)
    x = lane & 15
    spread_x = onehot(128, 256, lambda m: ((m >> 7) * 4 + ((m & 127) >> 5)) * 16 + (m & 15))
    fetch.wait()
    for b in range(FB):
        p, q = number(meta, b, M_PARENT), number(meta, b, M_PARENT + 1)
        qy, qx = q >> 1, q & 1
        base = (((p >> 1) ^ device) & 3) * E_ROWS + qy * 2 + (p & 1)
        ex = exact_dot(gathered[pl.ds(base + qx * R, 8, stride=4), :], spread_x)
        spread_y = onehot(128, 128, lambda m: (m >> 4) * 16 + 8 * qx + ((m & 15) >> 1))
        ey = exact_dot(
            jnp.concatenate(
                [gathered[pl.ds(base + (2 + k) * R, 8, stride=4), :] for k in range(2)], axis=0
            ),
            spread_y,
        )
        for k in range(2):
            for yh in range(2):
                rows = pl.ds(8 * k + 4 * yh + b, 8, stride=16)
                e_halo[rows, :] = ex[:, 128 * yh : 128 * yh + 128]
                rows = pl.ds(PY_AT + 8 * k + 4 * yh + b, 8, stride=16)
                e_halo[rows, :] = ey[8 * yh : 8 * yh + 8]
        spread_z = onehot(
            128,
            256,
            lambda m: ((m >> 7) * 4 + ((m & 127) >> 5)) * 16 + 8 * qx + ((m & 15) >> 1),
        )
        ezs = exact_dot(gathered[pl.ds(base + 4 * R, 16, stride=4), :], spread_z)
        a0, a1 = ezs[:, :128], ezs[:, 128:]
        moves = {}
        moves[0, 0] = (a0, a1)
        moves[1, 0] = tuple(jnp.where(x == 0, a, roll(a, 1, 1)) for a in (a0, a1))
        moves[-1, 0] = tuple(jnp.where(x == 15, a, roll(a, -1, 1)) for a in (a0, a1))
        moves[0, 1] = (
            jnp.where(lane < 16, a0, roll(a0, 16, 1)),
            jnp.where(lane < 16, roll(a0, 16, 1), roll(a1, 16, 1)),
        )
        moves[0, -1] = (
            jnp.where(lane >= 112, roll(a1, -16, 1), roll(a0, -16, 1)),
            jnp.where(lane >= 112, a1, roll(a1, -16, 1)),
        )
        out = [a0, a1]
        for k, i in enumerate(ZP + ZM):
            moved = moves[VELOCITIES[i][:2]]
            out = [jnp.where(row == k, moved[h], out[h]) for h in range(2)]
        for h in range(2):
            ez[pl.ds(4 * h + b, 8, stride=8), :] = out[h][:8]
            ez[pl.ds(64 + 4 * h + b, 2, stride=8), :] = out[h][8:10]
    stream_local(post, mask, ez, local)


def second_local_kernel(post, mask, ez, local):
    stream_local(post, mask, ez, local)


def gather_halo(own, x_in, n_in, rows, halo):
    for k, ref in enumerate((n_in, own, x_in)):
        put(halo, k * EDGES2, ref[0:rows, :])


def gather_faces(meta, device, sign, e_halo, halo, faces):
    put(halo, 3 * EDGES2, e_halo[...])
    for k in range(4):
        for b in range(FB):
            n = number(meta, b, k)
            safe = jnp.maximum(n, 0)
            which = jnp.clip(((safe >> 2) - device) * sign + 1, 0, 2)
            start = jnp.where(n >= 0, which * EDGES2 + (safe & 3), 3 * EDGES2 + b)
            start = start + (PY_AT if k >= 2 else 0)
            faces[pl.ds(k * FR + b, R, stride=FB), :] = halo[pl.ds(start, R, stride=FB), :]


def plan_corners(meta_n, meta_own, meta_x, device, sign, e_halo, group, from_n, fixed, spare):
    _, lane = iotas()
    for k in range(4):
        spare[pl.ds(k, 8, stride=4), :] = group
        spare[pl.ds(R + k, 8, stride=4), :] = from_n
    near_rows, far_rows = spare[0:R, :], spare[R : 2 * R, :]
    row8, lane8 = iotas(8)
    plan = zeros(8)

    def pick(which, row, column):
        return jnp.where(
            which == 0,
            meta_n[row, column],
            jnp.where(which == 1, meta_own[row, column], meta_x[row, column]),
        ).astype(jnp.int32)

    for b in range(FB):
        result = zeros(R)
        own_rows = e_halo[pl.ds(PY_AT + b, R, stride=FB), :]
        for side in range(2):
            n = number(meta_own, b, 2 + side)
            safe = jnp.maximum(n, 0)
            which = jnp.clip(((safe >> 2) - device) * sign + 1, 0, 2)
            p, q = (pick(which, safe & 3, M_PARENT + k) for k in range(2))
            rows = jnp.where(which == 0, far_rows, near_rows)
            for end in range(2):
                i = ((7, 10), (9, 8))[side][end]
                own_column = 16 * (YP, YM)[side].index(i) + 15 * end
                edge_column = ((0, 1), (1, 0))[side][end]
                to = 112 * side + 15 * end
                source = 32 * ((p >> 1) & 3) + ((p & 1) * 4 + q) * 4 + 2 * side + end
                value = jnp.where(
                    n < 0, roll(own_rows, to - own_column, 1), roll(rows, (to - source) & 127, 1)
                )
                result = jnp.where(lane == to, value, result)
                m = pick(which, safe & 3, end)
                there = jnp.maximum(m, 0) >> 2
                far = (there - device) * sign
                pair = jnp.where(far >= 2, 2, jnp.where(far < 0, 1, 0))
                column = 16 * pair + 8 * (there & 1) + 2 * (m & 3) + edge_column
                shift = jnp.where((n >= 0) & (m >= 0), (to - column) & 127, -1)
                spot = (row8 == b) & (lane8 == 2 * side + end)
                plan = jnp.where(spot, shift.astype(jnp.float32), plan)
        put(fixed, b * R, result)
    return plan


def corners(plan, own, x_in, n_in, x_late, at_row, fixed, spot):
    row, lane = iotas()
    upper = (row & 1) == 1
    table = at(own, at_row) + at(x_in, at_row)
    table = table + roll(at(n_in, at_row), 16, 1) + roll(x_late[...], 32, 1)
    for b in range(FB):
        result = at(fixed, b * R)
        for side in range(2):
            for end in range(2):
                to = 112 * side + 15 * end
                shift = number(plan, b, 2 * side + end)
                value = roll(table, shift & 127, 1)
                here = (lane == to) & (upper if side else jnp.logical_not(upper)) & (shift >= 0)
                result = jnp.where(here, value, result)
        spot[pl.ds(b, R, stride=FB), :] = result


def with_corners(cells, i, corner):
    if i not in (7, 8, 9, 10):
        return cells
    row, lane = iotas(cells.shape[0])
    column, upper = {7: (0, 0), 10: (15, 0), 9: (112, 1), 8: (127, 1)}[i]
    return jnp.where((lane == column) & (((row // FB) & 1) == upper), corner, cells)


def stream_local(post, mask, ez, dst):
    put(dst, 0, at(post, 0, FR))
    for h in range(2):
        bits = at(mask, h * 64, 64)
        solid = (bits & 1) > 0
        for i in range(1, 19):
            cx, cy, cz = VELOCITIES[i]
            start = max(h * 64 - 8 * cz, 0)
            stop = min(h * 64 + 64 - 8 * cz, FR)
            size = stop - start
            g = at(post, i * FR + start, size)
            if cx:
                g = roll(g, cx, 1)
            if cy:
                _, lane = iotas(size)
                g = roll(g, 16 * cy, 1)
                g = jnp.where(lane < 16 if cy == 1 else lane >= 112, swap_halves(g, FB), g)
            if size < 64:
                k = ZP.index(i) if cz == 1 else 5 + ZM.index(i)
                layer = at(ez, 8 * k, 8)
                g = jnp.concatenate([layer, g] if cz == 1 else [g, layer], axis=0)
            here = h * 64
            g = jnp.where((bits & (1 << i)) > 0, at(post, OPPOSITE[i] * FR + here, 64), g)
            put(dst, i * FR + here, jnp.where(solid, at(post, i * FR + here, 64), g))


def stream_sides(local, faces, dst):
    for i in range(19):
        cx, cy, cz = VELOCITIES[i]
        for h in range(2):
            here = h * 64
            g = at(local, i * FR + here, 64)
            start = max(here - 8 * cz, 0)
            stop = min(here + 64 - 8 * cz, FR)
            size = stop - start
            if not (cx or cy):
                put(dst, i * FR + here, g)
                continue
            layer = None
            if size < 64:
                layer = g[:8] if cz == 1 else g[-8:]
                g = g[8:] if cz == 1 else g[:-8]
            _, lane = iotas(size)
            if cx:
                face, column = (0, -XP.index(i)) if cx == 1 else (FR, 10 - XM.index(i))
                side = roll(at(faces, face + start, size), column, 1)
                if cy:
                    side = roll(side, 16 * cy, 1)
                    edge = lane < 16 if cy == 1 else lane >= 112
                    side = jnp.where(edge, swap_halves(side, FB), side)
                g = jnp.where((lane & 15) == (0 if cx == 1 else 15), side, g)
            if cy:
                upper = upper_of(size, FB)
                if cy == 1:
                    side = roll(at(faces, 2 * FR + start, size), cx - 16 * YP.index(i), 1)
                    g = jnp.where((lane < 16) & jnp.logical_not(upper), side, g)
                else:
                    side = roll(at(faces, 3 * FR + start, size), 112 + cx - 16 * YM.index(i), 1)
                    g = jnp.where((lane >= 112) & upper, side, g)
            if layer is not None:
                g = jnp.concatenate([layer, g] if cz == 1 else [g, layer], axis=0)
            put(dst, i * FR + here, g)


class CoarseSides:
    def __init__(self, meta, device, sign):
        self.has, self.which, self.slot = [], [], []
        for k in range(6):
            index = [number(meta, c, M_CNBR + k) for c in range(CB)]
            safe = [jnp.maximum(n, 0) for n in index]
            self.has.append(index)
            self.which.append(
                [jnp.clip(((n >> 1) - device) * sign + 1, 0, 2) * EDGES2 for n in safe]
            )
            self.slot.append([n & 1 for n in safe])

    def exists(self, k, rows):
        row, _ = iotas(rows)
        first, second = self.has[k]
        return jnp.where((row & 1) == 0, first, second) >= 0

    def face(self, k, halo, spot):
        for c in range(CB):
            if k < 2:
                start = self.which[k][c] + 2 * self.slot[k][c] + k
            else:
                start = self.which[k][c] + PY_AT + self.slot[k][c]
            spot[pl.ds(k * CR + c, R, stride=CB), :] = halo[pl.ds(start, R, stride=FB), :]

    def layers(self, k, halo, spot, count):
        for c in range(CB):
            for n in range(count):
                start = self.which[k][c] + ZS + 8 * n + 4 * (k - 4) + self.slot[k][c]
                spot[pl.ds(8 * n + 4 * (k - 4) + c, 2, stride=2), :] = halo[
                    pl.ds(start, 2, stride=2), :
                ]


def first_sides_kernel(
    local,
    f_own,
    x_in,
    n_in,
    group,
    cpost,
    e_halo,
    new,
    fixed,
    plan,
    cmid,
    c_out,
    halo,
    faces,
    spare,
    cfaces,
    clayers,
    meta_n,
    meta_own,
    meta_x,
    sem,
):
    device, sign = place()
    copies = fetch_meta(((n_in, meta_n), (f_own, meta_own), (x_in, meta_x)), sem)
    gather_halo(f_own, x_in, n_in, EDGES, halo)
    put(c_out, 0, zeros(2 * FR))
    for c in copies:
        c.wait()
    gather_faces(meta_own, device, sign, e_halo, halo, faces)

    row8, _ = iotas(8)
    sides = CoarseSides(meta_own, device, sign)
    for k in range(4):
        sides.face(k, halo, cfaces)
    for k in (4, 5):
        sides.layers(k, halo, clayers, 1)
    put(cmid, 0, at(cpost, 0, CR))
    for i in range(1, 19):
        cx, cy, cz = VELOCITIES[i]
        a = at(cpost, i * CR, CR)
        k = {1: 0, -1: 1}[cx] if cx else {1: 2, -1: 3}[cy] if cy else {1: 4, -1: 5}[cz]
        if cx:
            column = -10 - XP.index(i) if cx == 1 else 5 - XM.index(i)
            side = roll(at(cfaces, k * CR, CR), column, 1)
            g = move_x(a, cx, jnp.where(sides.exists(k, CR), side, a))
        elif cy:
            column = -16 * (5 + YP1.index(i)) if cy == 1 else 112 - 16 * (5 + YM1.index(i))
            side = roll(at(cfaces, k * CR, CR), column, 1)
            g = move_y(a, cy, jnp.where(sides.exists(k, CR), side, a), CB)
        else:
            own = a[:8] if cz == 1 else a[-8:]
            g = move_z_coarse(a, cz, jnp.where(sides.exists(k, 8), clayers[0:8, :], own))
        put(cmid, i * CR, g)
    put(cfaces, 0, pack_y(lambda i: at(cmid, i * CR, CR), YP2, YM2, 5, zeros(CR), CB))
    for c in range(CB):
        c_out[pl.ds(PY_AT + c, R, stride=FB), :] = cfaces[pl.ds(c, R, stride=CB), :]
    for k in range(4):
        top = roll(at(cmid, (ZP2[k] + 1) * CR - 8, 8), 4, 0)
        bottom = roll(at(cmid, ZM2[k] * CR, 8), 4, 0)
        put(c_out, 2 * FR + 8 * k, jnp.where(row8 < 4, top, bottom))

    from_n = at(n_in, N_EC, 8)
    plan[...] = plan_corners(
        meta_n, meta_own, meta_x, device, sign, e_halo, group[...], from_n, fixed, spare
    )
    stream_sides(local, faces, new)


def second_collision_kernel(
    new, mask, f_own, x_in, n_in, x_late, fixed, plan, coarse, post, f_out, spot, plan_s, sem
):
    (fetch,) = fetch_meta(((plan, plan_s),), sem, 0)
    put(f_out, ZS, coarse[pl.ds(2 * FR, R), :])
    fetch.wait()
    corners(plan_s, f_own, x_in, n_in, x_late, EDGES, fixed, spot)
    collide_rows(new, post, FR, OMEGA_FINE, mask, spot)
    send_faces(post, f_out, EDGES2, coarse, spot)


def second_sides_kernel(
    local, f_own, x_in, n_in, e_halo, f_first, new, halo, faces, meta, sem
):
    device, sign = place()
    (fetch,) = fetch_meta(((f_first, meta),), sem)
    gather_halo(f_own, x_in, n_in, EDGES2, halo)
    fetch.wait()
    gather_faces(meta, device, sign, e_halo, halo, faces)
    stream_sides(local, faces, new)


def coarsen_kernel(
    new, f_own, x_in, n_in, x_late, fixed, plan, cornered, means, spot, plan_s, sem
):
    (fetch,) = fetch_meta(((plan, plan_s),), sem, 0)
    fetch.wait()
    corners(plan_s, f_own, x_in, n_in, x_late, EDGES2, fixed, spot)
    for i in range(7, 11):
        put(cornered, (i - 7) * FR, with_corners(at(new, i * FR, FR), i, spot[...]))

    row = lax.broadcasted_iota(jnp.int32, (128, 128), 0)
    col = lax.broadcasted_iota(jnp.int32, (128, 128), 1)
    target = lambda yh, h: (yh * 4 + (row >> 5)) * 16 + ((row & 15) >> 1) + 8 * h
    mats = [
        [jnp.where(col == target(yh, h), 0.125, 0.0).astype(jnp.bfloat16) for yh in range(2)]
        for h in range(2)
    ]
    for pair in range(2):
        for ref, base, first, last in (
            (new, 0, 0, 7),
            (cornered, 7, 7, 11),
            (new, 0, 11, 19),
        ):
            rows = 8 * (last - first)
            total_rows = None
            for h in range(2):
                for yh in range(2):
                    start = (first - base) * FR + 4 * yh + 2 * pair + h
                    z0 = ref[pl.ds(start, rows, stride=16), :]
                    z1 = ref[pl.ds(start + 8, rows, stride=16), :]
                    part = exact_dot(z0 + z1, mats[h][yh])
                    total_rows = part if total_rows is None else total_rows + part
            put(means, pair * 19 * 8 + 8 * first, total_rows)


def tail_kernel(
    f_first,
    new,
    cornered,
    f_own,
    x_in,
    n_in,
    cmid,
    fine_out,
    cpassed,
    halo,
    cfaces,
    clayers,
    meta_own,
    sem,
    out_sem,
):
    device, sign = place()
    (fetch,) = fetch_meta(((f_first, meta_own),), sem)
    pieces = (
        (new, 0, 0, 7 * FR),
        (cornered, 0, 7 * FR, 4 * FR),
        (new, 11 * FR, 11 * FR, 8 * FR),
    )
    outs = [
        pltpu.make_async_copy(
            ref.at[pl.ds(source, rows)], fine_out.at[pl.ds(to, rows)], out_sem.at[k]
        )
        for k, (ref, source, to, rows) in enumerate(pieces)
    ]
    for c in outs:
        c.start()
    gather_halo(f_own, x_in, n_in, EDGES2, halo)
    fetch.wait()
    sides = CoarseSides(meta_own, device, sign)
    for k in (2, 3):
        sides.face(k, halo, cfaces)
    for k in (4, 5):
        sides.layers(k, halo, clayers, 4)
    for i in range(19):
        a = at(cmid, i * CR, CR)
        g = a
        if i in YP2 or i in YM2:
            cy = 1 if i in YP2 else -1
            k = 2 if cy == 1 else 3
            column = -16 * (5 + YP2.index(i)) if cy == 1 else 112 - 16 * (5 + YM2.index(i))
            side = roll(at(cfaces, k * CR, CR), column, 1)
            g = move_y(a, cy, jnp.where(sides.exists(k, CR), side, a), CB)
        elif i in ZP2 or i in ZM2:
            cz = 1 if i in ZP2 else -1
            k = 4 if cz == 1 else 5
            n = (ZP2 if cz == 1 else ZM2).index(i)
            own = a[:8] if cz == 1 else a[-8:]
            side = jnp.where(sides.exists(k, 8), at(clayers, 8 * n, 8), own)
            g = move_z_coarse(a, cz, side)
        put(cpassed, i * CR, g)
    for c in outs:
        c.wait()


def coarse_last_kernel(
    f_first, cpassed, own, two, x_in, coarse_out, gathered, meta, sem
):
    device, _ = place()
    (fetch,) = fetch_meta(((f_first, meta),), sem)
    put(gathered, 0, own[...])
    put(gathered, K_ROWS, x_in[0:K_ROWS, :])
    put(gathered, 2 * K_ROWS, two[...])
    put(gathered, 3 * K_ROWS, x_in[K_ROWS : 2 * K_ROWS, :])
    coarse_out[...] = cpassed[...]
    _, lane = iotas(8)
    x_half = (lane >> 3) & 1
    fetch.wait()
    for c in range(CB):
        for qy in range(2):
            children = [number(meta, c, M_CHILD + 2 * qy + qx) for qx in range(2)]
            starts, shifts = [], []
            for qx in range(2):
                child = jnp.maximum(children[qx], 0)
                slot = ((child >> 2) ^ device) & 3
                starts.append(slot * K_ROWS + ((child & 3) >> 1) * (19 * 8))
                shifts.append((8 * (qx - (child & 1))) & 127)
            index = jnp.where(x_half == 0, children[0], children[1])
            for i in range(19):
                rows = pl.ds(i * CR + 2 * qy + c, 8, stride=4)
                values = [roll(at(gathered, starts[qx] + 8 * i, 8), shifts[qx], 1) for qx in (0, 1)]
                value = jnp.where(x_half == 0, values[0], values[1])
                coarse_out[rows, :] = jnp.where(index >= 0, value, cpassed[rows, :])


VMEM = pl.BlockSpec(memory_space=pltpu.VMEM)
HBM = pl.BlockSpec(memory_space=pltpu.HBM)


def rows_of(n, dtype=jnp.float32):
    return jax.ShapeDtypeStruct((n, 128), dtype)


def scratch(n, dtype=jnp.float32):
    return pltpu.VMEM((n, 128), dtype)


def call(kernel, name, specs, outs, scratches, out_specs=None):
    return pl.pallas_call(
        kernel,
        name=name,
        in_specs=specs,
        out_specs=out_specs or [VMEM] * len(outs),
        out_shape=outs,
        scratch_shapes=scratches,
        cost_estimate=pl.CostEstimate(flops=1 << 20, bytes_accessed=4 << 20, transcendentals=0),
        compiler_params=pltpu.CompilerParams(vmem_limit_bytes=32 * 1024 * 1024),
    )


def meta_scratch(n=3):
    return [pltpu.SMEM((8, 128), jnp.float32)] * n + [pltpu.SemaphoreType.DMA((n,))]


def exchange(rows, devices, partner):
    return lax.ppermute(rows, AXES, [(i, partner(i)) for i in range(devices)])


def as_rows(cells, directions):
    blocks = cells.shape[0]
    cells = cells.reshape(blocks, directions, R, 128)
    return cells.transpose(1, 2, 0, 3).reshape(directions * R * blocks, 128)


def as_cells(rows, blocks):
    return rows.reshape(19, R, blocks, 128).transpose(2, 0, 1, 3).reshape(blocks, 19, R * 128)


def on_device(fine_pop, coarse_pop, fine_nbr, coarse_nbr, parent, children, solid):
    devices = lax.axis_size(AXES)
    by_one = lambda a: exchange(a, devices, lambda i: i ^ 1)
    by_two = lambda a: exchange(a, devices, lambda i: i ^ 2)
    odd_even = lambda a: exchange(a, devices, lambda i: (((i + 1) ^ 1) - 1) % devices)
    parent = parent.T
    small = lambda a: pltpu.SMEM(a.shape, jnp.int32)
    in_hbm = lambda a: pltpu.with_memory_space_constraint(a, pltpu.HBM)

    raw, e_own, meta = call(
        coarse_first_kernel,
        "coarse_first",
        [HBM] * 5,
        [rows_of(C_ALL), rows_of(E_ROWS), rows_of(8)],
        [
            small(fine_nbr),
            small(parent),
            small(coarse_nbr),
            small(children),
            pltpu.SemaphoreType.DMA((5,)),
        ],
    )(
        in_hbm(as_rows(coarse_pop, 19)),
        in_hbm(fine_nbr),
        in_hbm(parent),
        in_hbm(coarse_nbr),
        in_hbm(children),
    )
    e_two = by_two(e_own)
    cpost, post, mask, f_own = call(
        fine_first_kernel,
        "fine_first",
        [VMEM, VMEM, HBM, HBM],
        [rows_of(C_ALL), rows_of(F_ALL), rows_of(FR, jnp.int32), rows_of(F_ROWS)],
        [
            scratch(F_ALL),
            scratch(FR, jnp.int32),
            scratch(2 * FR + 8),
            scratch(FR),
            pltpu.SemaphoreType.DMA((2,)),
        ],
    )(meta, raw, in_hbm(as_rows(fine_pop, 19)), in_hbm(as_rows(solid, 1)))

    x_in = by_one(jnp.concatenate([f_own, e_own, e_two]))
    group = (
        e_own[EC_AT:] + x_in[X_E + EC_AT : X_E2] + e_two[EC_AT:] + x_in[X_E2 + EC_AT :]
    )
    n_in = odd_even(
        jnp.concatenate(
            [f_own[:EDGES], f_own[EDGES:META] + x_in[EDGES:META], f_own[META:], group]
        )
    )
    e_halo, ez, local = call(
        first_local_kernel,
        "first_local",
        [VMEM] * 6,
        [rows_of(2 * FR), rows_of(80), rows_of(F_ALL)],
        [scratch(4 * E_ROWS + R)] + meta_scratch(1),
    )(f_own, e_own, e_two, x_in, post, mask)
    far_edges, ez = lax.optimization_barrier((n_in[EDGES:META], ez))
    x_late = by_one(far_edges)
    new, fixed, plan, cmid, c2_own = call(
        first_sides_kernel,
        "first_sides",
        [VMEM] * 7,
        [
            rows_of(F_ALL),
            rows_of(FB * R),
            rows_of(8),
            rows_of(C_ALL),
            rows_of(2 * FR + R),
        ],
        [scratch(HALO), scratch(4 * FR), scratch(2 * R), scratch(4 * CR), scratch(8)]
        + meta_scratch(),
    )(local, f_own, x_in, n_in, group, cpost, e_halo)
    post2, f2_own = call(
        second_collision_kernel,
        "second_collision",
        [VMEM] * 9,
        [rows_of(F_ALL), rows_of(F2_ROWS)],
        [scratch(FR)] + meta_scratch(1),
    )(new, mask, f_own, x_in, n_in, x_late, fixed, plan, c2_own)

    x2_in = by_one(f2_own)
    n2_in = odd_even(
        jnp.concatenate([f2_own[:EDGES2], f2_own[EDGES2:] + x2_in[EDGES2:]])
    )
    (local2,) = call(
        second_local_kernel, "second_local", [VMEM] * 3, [rows_of(F_ALL)], []
    )(post2, mask, ez)
    far_edges2, local2 = lax.optimization_barrier((n2_in[EDGES2:], local2))
    x2_late = by_one(far_edges2)
    (new2,) = call(
        second_sides_kernel,
        "second_sides",
        [VMEM] * 6,
        [rows_of(F_ALL)],
        [scratch(HALO), scratch(4 * FR)] + meta_scratch(1),
    )(local2, f2_own, x2_in, n2_in, e_halo, f_own)
    cornered, means = call(
        coarsen_kernel,
        "coarsen",
        [VMEM] * 7,
        [rows_of(4 * FR), rows_of(K_ROWS)],
        [scratch(FR)] + meta_scratch(1),
    )(new2, f2_own, x2_in, n2_in, x2_late, fixed, plan)

    k_two = by_two(means)
    fine_out, cpassed = call(
        tail_kernel,
        "tail",
        [VMEM] * 7,
        [rows_of(F_ALL), rows_of(C_ALL)],
        [scratch(3 * EDGES2), scratch(4 * CR), scratch(R)]
        + meta_scratch(1)
        + [pltpu.SemaphoreType.DMA((3,))],
        [HBM, VMEM],
    )(f_own, new2, cornered, f2_own, x2_in, n2_in, cmid)
    k_two, cpassed = lax.optimization_barrier((k_two, cpassed))
    k_one = by_one(jnp.concatenate([means, k_two]))
    (coarse_out,) = call(
        coarse_last_kernel,
        "coarse_last",
        [VMEM] * 5,
        [rows_of(C_ALL)],
        [scratch(4 * K_ROWS)] + meta_scratch(1),
    )(f_own, cpassed, means, k_two, k_one)
    return as_cells(fine_out, FB), as_cells(coarse_out, CB)


def solution(mesh):
    rows = P(AXES, None)
    blocks = P(AXES, None, None)
    return jax.shard_map(
        on_device,
        mesh=mesh,
        in_specs=(blocks, blocks, rows, rows, rows, rows, rows),
        out_specs=(blocks, blocks),
        check_vma=False,
    )
```

```python
import jax
import jax.numpy as jnp
from jax import lax
from jax.experimental import pallas as pl
from jax.experimental.pallas import tpu as pltpu
from jax.sharding import PartitionSpec as P

AXES = ("gx", "gy")
VELOCITIES = (
    (0, 0, 0),
    (1, 0, 0),
    (-1, 0, 0),
    (0, 1, 0),
    (0, -1, 0),
    (0, 0, 1),
    (0, 0, -1),
    (1, 1, 0),
    (-1, -1, 0),
    (1, -1, 0),
    (-1, 1, 0),
    (1, 0, 1),
    (-1, 0, -1),
    (1, 0, -1),
    (-1, 0, 1),
    (0, 1, 1),
    (0, -1, -1),
    (0, 1, -1),
    (0, -1, 1),
)
WEIGHTS = (1.0 / 3.0,) + (1.0 / 18.0,) * 6 + (1.0 / 36.0,) * 12
OPPOSITE = (0, 2, 1, 4, 3, 6, 5, 8, 7, 10, 9, 12, 11, 14, 13, 16, 15, 18, 17)
OMEGA_COARSE = 1.6
OMEGA_FINE = 1.0 / (2.0 * (1.0 / 1.6 - 0.5) + 0.5)

XP = (1, 7, 9, 11, 13)
XM = (2, 8, 10, 12, 14)
YP = (3, 7, 10, 15, 17)
YM = (4, 8, 9, 16, 18)
ZP = (5, 11, 14, 15, 18)
ZM = (6, 12, 13, 16, 17)
YP1, YM1 = (3, 15, 17), (4, 16, 18)
YP2, YM2 = (7, 10), (8, 9)
ZP2, ZM2 = (11, 14, 15, 18), (12, 13, 16, 17)


R = 32
FB, CB = 4, 2
FR, CR = FB * R, CB * R
F_ALL, C_ALL = 19 * FR, 19 * CR
PY_AT = FR
ZS = 2 * FR
EDGES = ZS + 8
META = EDGES + R
F_ROWS = META + 8
EDGES2 = ZS + R
F2_ROWS = EDGES2 + R
N_EC = F_ROWS
EC_AT = 4 * R + 40
E_ROWS = EC_AT + 8
K_ROWS = 2 * 19 * 8
S_ROWS = 2 * 32
HALO = 3 * EDGES2 + 2 * FR
X_E = F_ROWS
X_E2 = X_E + E_ROWS
M_PARENT, M_CNBR, M_CHILD = 4, 8, 16


def iotas(rows=R):
    row = lax.broadcasted_iota(jnp.int32, (rows, 128), 0)
    lane = lax.broadcasted_iota(jnp.int32, (rows, 128), 1)
    return row, lane


def roll(a, shift, axis):
    if isinstance(shift, int):
        shift = shift % a.shape[axis]
        if shift == 0:
            return a
    return pltpu.roll(a, shift, axis)


def at(ref, start, size=R):
    if not isinstance(start, int):
        start = pl.multiple_of(start, 8)
    return ref[pl.ds(start, size), :]


def put(ref, start, value):
    if not isinstance(start, int):
        start = pl.multiple_of(start, 8)
    ref[pl.ds(start, value.shape[0]), :] = value


def zeros(rows):
    return jnp.zeros((rows, 128), jnp.float32)


def total(terms):
    while len(terms) > 1:
        pairs = [terms[k] + terms[k + 1] for k in range(0, len(terms) - 1, 2)]
        terms = pairs + terms[len(terms) - len(terms) % 2 :]
    return terms[0]


def collide(f, rate):
    rho = total(f)
    mom = []
    for axis in range(3):
        plus = [f[i] for i in range(19) if VELOCITIES[i][axis] == 1]
        minus = [f[i] for i in range(19) if VELOCITIES[i][axis] == -1]
        mom.append(total(plus) - total(minus))
    inv = 1.0 / rho
    u = [m * inv for m in mom]
    base = 1.0 - 1.5 * (u[0] * u[0] + u[1] * u[1] + u[2] * u[2])
    scaled = {w: (rate * w) * rho for w in sorted(set(WEIGHTS))}
    keep = 1.0 - rate
    out = [None] * 19
    out[0] = keep * f[0] + scaled[WEIGHTS[0]] * base
    for i in range(1, 19, 2):
        proj = None
        for axis in range(3):
            c = VELOCITIES[i][axis]
            if c:
                term = u[axis]
                if proj is None:
                    proj = term if c > 0 else -term
                else:
                    proj = proj + term if c > 0 else proj - term
        even = base + 4.5 * (proj * proj)
        odd = 3.0 * proj
        w = scaled[WEIGHTS[i]]
        out[i] = keep * f[i] + w * (even + odd)
        out[i + 1] = keep * f[i + 1] + w * (even - odd)
    return out


def collide_rows(src, dst, rows, rate, mask=None, corner=None):
    def body(v, carry):
        f = [at(src, i * rows + v * 16, 16) for i in range(19)]
        if corner is not None:
            edge = at(corner, v * 16, 16)
            f = [with_corners(f[i], i, edge) for i in range(19)]
        post = collide(f, rate)
        if mask is not None:
            solid = (at(mask, v * 16, 16) & 1) > 0
            post = [jnp.where(solid, f[i], post[i]) for i in range(19)]
        for i in range(19):
            put(dst, i * rows + v * 16, post[i])
        return carry

    lax.fori_loop(0, rows // 16, body, 0)


def upper_of(rows, blocks):
    row, _ = iotas(rows)
    return ((row // blocks) & 1) == 1


def swap_halves(a, blocks):
    if blocks == 4:
        rows = a.shape[0]
        return pltpu.roll(a.reshape(rows // 8, 8, 128), 4, 1).reshape(rows, 128)
    return jnp.where(upper_of(a.shape[0], blocks), roll(a, blocks, 0), roll(a, -blocks, 0))


def pack_x(get, packed, first=0):
    _, lane = iotas(packed.shape[0])
    x = lane & 15
    for j in range(5):
        packed = jnp.where(x == first + j, roll(get(XP[j]), first + j - 15, 1), packed)
        packed = jnp.where(x == first + 5 + j, roll(get(XM[j]), first + 5 + j, 1), packed)
    return packed


def pack_y(get, plus, minus, first, rest, blocks):
    rows = rest.shape[0]
    _, lane = iotas(rows)
    upper = upper_of(rows, blocks)
    group = lane >> 4
    packed = zeros(rows)
    for k in range(len(plus)):
        p = first + k
        one = jnp.where(upper, roll(get(plus[k]), 16 * p - 112, 1), roll(get(minus[k]), 16 * p, 1))
        packed = jnp.where(group == p, one, packed)
    packed = swap_halves(packed, blocks)
    return jnp.where((group >= first) & (group < first + len(plus)), packed, rest)


def pack_edges(get, rows):
    _, lane = iotas(rows)
    upper = upper_of(rows, FB)
    first = jnp.where(upper, roll(get(7), -127, 1), get(8))
    second = jnp.where(upper, roll(get(10), 1 - 112, 1), roll(get(9), 1 - 15, 1))
    return swap_halves(jnp.where(lane == 0, first, second), FB)


def move_x(a, cx, halo):
    _, lane = iotas(a.shape[0])
    x = lane & 15
    if cx == 1:
        return jnp.where(x == 0, halo, roll(a, 1, 1))
    return jnp.where(x == 15, halo, roll(a, -1, 1))


def move_y(a, cy, halo, blocks):
    _, lane = iotas(a.shape[0])
    upper = upper_of(a.shape[0], blocks)
    near = roll(a, 16 * cy, 1)
    if cy == 1:
        return jnp.where(lane < 16, jnp.where(upper, swap_halves(near, blocks), halo), near)
    return jnp.where(lane >= 112, jnp.where(upper, halo, swap_halves(near, blocks)), near)


def move_z_coarse(a, cz, halo8):
    row, _ = iotas(8)
    near = roll(a, 4 * cz, 0)
    if cz == 1:
        return jnp.concatenate([jnp.where(row < 4, halo8, near[:8]), near[8:]], axis=0)
    return jnp.concatenate([near[:-8], jnp.where(row >= 4, halo8, near[-8:])], axis=0)


def send_faces(post, out, edges, coarse, spot):
    for h in range(2):
        rows = h * 64
        get = lambda i: at(post, i * FR + rows, 64)
        put(out, rows, pack_x(get, at(coarse, rows, 64)))
        put(out, PY_AT + rows, pack_y(get, YP, YM, 0, at(coarse, PY_AT + rows, 64), FB))
        put(spot, rows, pack_edges(get, 64))
    _, lane = iotas()
    device, _ = place()
    first = 8 * (device & 1)
    packed = zeros(R)
    for b in range(FB):
        one = roll(spot[pl.ds(b, R, stride=FB), :], first + 2 * b, 1)
        packed = jnp.where((lane >> 1) == (first >> 1) + b, one, packed)
    put(out, edges, packed)


def place():
    device = lax.axis_index("gx") * lax.axis_size("gy") + lax.axis_index("gy")
    sign = 1 - 2 * (device & 1)
    return device, sign


def number(meta, row, column):
    return meta[row, column].astype(jnp.int32)


def fetch_meta(pairs, sem, start=META):
    copies = [
        pltpu.make_async_copy(ref.at[pl.ds(start, 8)], dst, sem.at[k])
        for k, (ref, dst) in enumerate(pairs)
    ]
    for c in copies:
        c.start()
    return copies


def coarse_first_kernel(
    pop_hbm,
    nbr_hbm,
    parent_hbm,
    cnbr_hbm,
    children_hbm,
    raw,
    e_out,
    meta_out,
    nbr,
    parent,
    cnbr,
    children,
    sem,
):
    copies = [
        pltpu.make_async_copy(src, dst, sem.at[k])
        for k, (src, dst) in enumerate(
            (
                (pop_hbm, raw),
                (nbr_hbm, nbr),
                (parent_hbm, parent),
                (cnbr_hbm, cnbr),
                (children_hbm, children),
            )
        )
    ]
    for c in copies:
        c.start()
    copies[0].wait()
    _, lane = iotas()
    row8, lane8 = iotas(8)
    x = lane & 15
    half = lambda i: at(raw, i * CR)
    for qx in range(2):
        packed = zeros(R)
        for j in range(5):
            packed = jnp.where(x == j, roll(half(XP[j]), j - 8 * qx, 1), packed)
            packed = jnp.where(x == 5 + j, roll(half(XM[j]), 5 + j - 8 * qx - 7, 1), packed)
        put(e_out, qx * R, packed)
    low, high = zeros(R), zeros(R)
    for p in range(5):
        low = jnp.where((lane >> 4) == p, roll(half(YP[p]), 16 * p, 1), low)
        high = jnp.where((lane >> 4) == p, roll(half(YM[p]), 16 * p - 112, 1), high)
    put(e_out, 2 * R, low)
    put(e_out, 3 * R, high)
    for k in range(5):
        e_out[pl.ds(4 * R + 4 * k, 4), :] = raw[pl.ds(ZP[k] * CR, 4), :]
        e_out[pl.ds(4 * R + 20 + 4 * k, 4), :] = raw[pl.ds(ZM[k] * CR + 28, 4), :]
    corner = zeros(8)
    for c in range(CB):
        for q in range(4):
            for e, (i, yq, xq) in enumerate(((7, 7, 0), (10, 7, 7), (9, 0, 0), (8, 0, 7))):
                to = (c * 4 + q) * 4 + e
                rows = raw[pl.ds(i * CR + (q // 2) * 2 + c, 8, stride=4), :]
                rows = roll(rows, to - (yq * 16 + 8 * (q % 2) + xq), 1)
                corner = jnp.where(lane8 == to, rows, corner)
    device, _ = place()
    put(e_out, EC_AT, roll(corner, 32 * (device & 3), 1))

    for c in copies[1:]:
        c.wait()
    meta = zeros(8)
    entries = []
    for b in range(FB):
        entries += [(b, k, nbr[b, k]) for k in range(4)]
        entries += [(b, M_PARENT + k, parent[k, b]) for k in range(2)]
    for c in range(CB):
        entries += [(c, M_CNBR + k, cnbr[c, k]) for k in range(6)]
        entries += [(c, M_CHILD + k, children[c, k]) for k in range(4)]
    for b, k, value in entries:
        meta = jnp.where((row8 == b) & (lane8 == k), value.astype(jnp.float32), meta)
    put(meta_out, 0, meta)


def fine_first_kernel(
    meta,
    raw,
    pop_hbm,
    solid_hbm,
    cpost,
    post,
    mask,
    f_out,
    pop,
    solid,
    coarse,
    spot,
    sem,
):
    copies = [
        pltpu.make_async_copy(pop_hbm, pop, sem.at[0]),
        pltpu.make_async_copy(solid_hbm, solid, sem.at[1]),
    ]
    for c in copies:
        c.start()
    row8, _ = iotas(8)
    collide_rows(raw, cpost, CR, OMEGA_COARSE)
    get = lambda i: at(cpost, i * CR, CR)
    _, wide = iotas(CR)
    ahead, back = zeros(CR), zeros(CR)
    for j in range(5):
        ahead = jnp.where((wide & 15) == 10 + j, roll(get(XP[j]), 10 + j - 15, 1), ahead)
        back = jnp.where((wide & 15) == 10 + j, roll(get(XM[j]), 10 + j, 1), back)
    for k, packed in enumerate((ahead, back)):
        put(spot, 0, packed)
        for c in range(CB):
            coarse[pl.ds(2 * c + k, R, stride=FB), :] = spot[pl.ds(c, R, stride=CB), :]
    put(spot, 0, pack_y(get, YP1, YM1, 5, zeros(CR), CB))
    for c in range(CB):
        coarse[pl.ds(PY_AT + c, R, stride=FB), :] = spot[pl.ds(c, R, stride=CB), :]
        coarse[pl.ds(PY_AT + 2 + c, R, stride=FB), :] = zeros(R)
    top = roll(at(cpost, 6 * CR - 8, 8), 4, 0)
    bottom = roll(at(cpost, 6 * CR, 8), 4, 0)
    put(coarse, 2 * FR, jnp.where(row8 < 4, top, bottom))

    for c in copies:
        c.wait()
    s = jnp.where(solid[...] > 0, 1, 0)
    bits = s
    none = jnp.zeros_like(s)
    by_z = {0: lambda a: a}
    by_z[1] = lambda a: jnp.concatenate([a[-8:], a[:-8]], axis=0)
    by_z[-1] = lambda a: jnp.concatenate([a[8:], a[:8]], axis=0)
    by_y = {cy: move_y(s, cy, none, FB) for cy in (1, -1)}
    by_y[0] = s
    by_x = {(cx, cy): roll(by_y[cy], cx, 1) for cx in (1, -1) for cy in (-1, 0, 1)}
    for i in range(1, 19):
        cx, cy, cz = VELOCITIES[i]
        moved = by_z[cz](by_x[cx, cy] if cx else by_y[cy])
        bits = bits | (moved << i)
    put(mask, 0, bits)
    collide_rows(pop, post, FR, OMEGA_FINE, mask)
    put(f_out, ZS, at(coarse, 2 * FR, 8))
    put(f_out, META, meta[...])
    send_faces(post, f_out, EDGES, coarse, spot)


def onehot(rows, cols, source):
    row = lax.broadcasted_iota(jnp.int32, (rows, cols), 0)
    col = lax.broadcasted_iota(jnp.int32, (rows, cols), 1)
    return jnp.where(row == source(col), 1.0, 0.0).astype(jnp.bfloat16)


def exact_dot(a, b):
    result = None
    for _ in range(3):
        part = a.astype(jnp.bfloat16)
        a = a - part.astype(jnp.float32)
        term = jnp.dot(part, b, preferred_element_type=jnp.float32)
        result = term if result is None else result + term
    return result


def first_local_kernel(
    f_own, e_own, e_two, x_in, post, mask, e_halo, ez, local, gathered, meta, sem
):
    device, _ = place()
    (fetch,) = fetch_meta(((f_own, meta),), sem)
    put(gathered, 0, e_own[...])
    put(gathered, E_ROWS, x_in[X_E : X_E + E_ROWS, :])
    put(gathered, 2 * E_ROWS, e_two[...])
    put(gathered, 3 * E_ROWS, x_in[X_E2 : X_E2 + E_ROWS, :])
    row, lane = iotas(16)
    x = lane & 15
    spread_x = onehot(128, 256, lambda m: ((m >> 7) * 4 + ((m & 127) >> 5)) * 16 + (m & 15))
    fetch.wait()
    for b in range(FB):
        p, q = number(meta, b, M_PARENT), number(meta, b, M_PARENT + 1)
        qy, qx = q >> 1, q & 1
        base = (((p >> 1) ^ device) & 3) * E_ROWS + qy * 2 + (p & 1)
        ex = exact_dot(gathered[pl.ds(base + qx * R, 8, stride=4), :], spread_x)
        spread_y = onehot(128, 128, lambda m: (m >> 4) * 16 + 8 * qx + ((m & 15) >> 1))
        ey = exact_dot(
            jnp.concatenate(
                [gathered[pl.ds(base + (2 + k) * R, 8, stride=4), :] for k in range(2)], axis=0
            ),
            spread_y,
        )
        for k in range(2):
            for yh in range(2):
                rows = pl.ds(8 * k + 4 * yh + b, 8, stride=16)
                e_halo[rows, :] = ex[:, 128 * yh : 128 * yh + 128]
                rows = pl.ds(PY_AT + 8 * k + 4 * yh + b, 8, stride=16)
                e_halo[rows, :] = ey[8 * yh : 8 * yh + 8]
        spread_z = onehot(
            128,
            256,
            lambda m: ((m >> 7) * 4 + ((m & 127) >> 5)) * 16 + 8 * qx + ((m & 15) >> 1),
        )
        ezs = exact_dot(gathered[pl.ds(base + 4 * R, 16, stride=4), :], spread_z)
        a0, a1 = ezs[:, :128], ezs[:, 128:]
        moves = {}
        moves[0, 0] = (a0, a1)
        moves[1, 0] = tuple(jnp.where(x == 0, a, roll(a, 1, 1)) for a in (a0, a1))
        moves[-1, 0] = tuple(jnp.where(x == 15, a, roll(a, -1, 1)) for a in (a0, a1))
        moves[0, 1] = (
            jnp.where(lane < 16, a0, roll(a0, 16, 1)),
            jnp.where(lane < 16, roll(a0, 16, 1), roll(a1, 16, 1)),
        )
        moves[0, -1] = (
            jnp.where(lane >= 112, roll(a1, -16, 1), roll(a0, -16, 1)),
            jnp.where(lane >= 112, a1, roll(a1, -16, 1)),
        )
        out = [a0, a1]
        for k, i in enumerate(ZP + ZM):
            moved = moves[VELOCITIES[i][:2]]
            out = [jnp.where(row == k, moved[h], out[h]) for h in range(2)]
        for h in range(2):
            ez[pl.ds(4 * h + b, 8, stride=8), :] = out[h][:8]
            ez[pl.ds(64 + 4 * h + b, 2, stride=8), :] = out[h][8:10]
    stream_local(post, mask, ez, local)


def coarse_means(pieces, means):
    row = lax.broadcasted_iota(jnp.int32, (128, 128), 0)
    col = lax.broadcasted_iota(jnp.int32, (128, 128), 1)
    target = lambda yh, h: (yh * 4 + (row >> 5)) * 16 + ((row & 15) >> 1) + 8 * h
    mats = [
        [jnp.where(col == target(yh, h), 0.125, 0.0).astype(jnp.bfloat16) for yh in range(2)]
        for h in range(2)
    ]
    for pair in range(2):
        for ref, base, first, last in pieces:
            rows = 8 * (last - first)
            total_rows = None
            for h in range(2):
                for yh in range(2):
                    start = (first - base) * FR + 4 * yh + 2 * pair + h
                    z0 = ref[pl.ds(start, rows, stride=16), :]
                    z1 = ref[pl.ds(start + 8, rows, stride=16), :]
                    part = exact_dot(z0 + z1, mats[h][yh])
                    total_rows = part if total_rows is None else total_rows + part
            put(means, pair * 19 * 8 + 8 * first, total_rows)


def pack_side_means(means, out):
    _, lane = iotas(8)
    x = lane & 15
    for pair in range(2):
        get = lambda i: at(means, pair * 19 * 8 + 8 * i, 8)
        packed = [zeros(8) for _ in range(4)]
        for j in range(5):
            for h in range(2):
                to = 2 * j + h
                packed[0] = jnp.where(x == to, roll(get(XP[j]), to - 8 * h, 1), packed[0])
                packed[1] = jnp.where(x == to, roll(get(XM[j]), to - 8 * h - 7, 1), packed[1])
            group = (lane >> 4) == j
            packed[2] = jnp.where(group, roll(get(YP[j]), 16 * j, 1), packed[2])
            packed[3] = jnp.where(group, roll(get(YM[j]), 16 * j - 112, 1), packed[3])
        for k in range(4):
            put(out, pair * 32 + 8 * k, packed[k])


def second_local_kernel(post, mask, ez, local, means):
    stream_local(post, mask, ez, local)
    coarse_means(((local, 0, 0, 19),), means)


def gather_halo(own, x_in, n_in, rows, halo):
    for k, ref in enumerate((n_in, own, x_in)):
        put(halo, k * EDGES2, ref[0:rows, :])


def gather_faces(meta, device, sign, e_halo, halo, faces):
    put(halo, 3 * EDGES2, e_halo[...])
    for k in range(4):
        for b in range(FB):
            n = number(meta, b, k)
            safe = jnp.maximum(n, 0)
            which = jnp.clip(((safe >> 2) - device) * sign + 1, 0, 2)
            start = jnp.where(n >= 0, which * EDGES2 + (safe & 3), 3 * EDGES2 + b)
            start = start + (PY_AT if k >= 2 else 0)
            faces[pl.ds(k * FR + b, R, stride=FB), :] = halo[pl.ds(start, R, stride=FB), :]


def plan_corners(meta_n, meta_own, meta_x, device, sign, e_halo, group, from_n, fixed, spare):
    _, lane = iotas()
    for k in range(4):
        spare[pl.ds(k, 8, stride=4), :] = group
        spare[pl.ds(R + k, 8, stride=4), :] = from_n
    near_rows, far_rows = spare[0:R, :], spare[R : 2 * R, :]
    row8, lane8 = iotas(8)
    plan = zeros(8)

    def pick(which, row, column):
        return jnp.where(
            which == 0,
            meta_n[row, column],
            jnp.where(which == 1, meta_own[row, column], meta_x[row, column]),
        ).astype(jnp.int32)

    for b in range(FB):
        result = zeros(R)
        own_rows = e_halo[pl.ds(PY_AT + b, R, stride=FB), :]
        for side in range(2):
            n = number(meta_own, b, 2 + side)
            safe = jnp.maximum(n, 0)
            which = jnp.clip(((safe >> 2) - device) * sign + 1, 0, 2)
            p, q = (pick(which, safe & 3, M_PARENT + k) for k in range(2))
            rows = jnp.where(which == 0, far_rows, near_rows)
            for end in range(2):
                i = ((7, 10), (9, 8))[side][end]
                own_column = 16 * (YP, YM)[side].index(i) + 15 * end
                edge_column = ((0, 1), (1, 0))[side][end]
                to = 112 * side + 15 * end
                source = 32 * ((p >> 1) & 3) + ((p & 1) * 4 + q) * 4 + 2 * side + end
                value = jnp.where(
                    n < 0, roll(own_rows, to - own_column, 1), roll(rows, (to - source) & 127, 1)
                )
                result = jnp.where(lane == to, value, result)
                m = pick(which, safe & 3, end)
                there = jnp.maximum(m, 0) >> 2
                far = (there - device) * sign
                pair = jnp.where(far >= 2, 2, jnp.where(far < 0, 1, 0))
                column = 16 * pair + 8 * (there & 1) + 2 * (m & 3) + edge_column
                shift = jnp.where((n >= 0) & (m >= 0), (to - column) & 127, -1)
                spot = (row8 == b) & (lane8 == 2 * side + end)
                plan = jnp.where(spot, shift.astype(jnp.float32), plan)
        put(fixed, b * R, result)
    return plan


def corners(plan, own, x_in, n_in, x_late, at_row, fixed, spot):
    row, lane = iotas()
    upper = (row & 1) == 1
    table = at(own, at_row) + at(x_in, at_row)
    table = table + roll(at(n_in, at_row), 16, 1) + roll(x_late[...], 32, 1)
    for b in range(FB):
        result = at(fixed, b * R)
        for side in range(2):
            for end in range(2):
                to = 112 * side + 15 * end
                shift = number(plan, b, 2 * side + end)
                value = roll(table, shift & 127, 1)
                here = (lane == to) & (upper if side else jnp.logical_not(upper)) & (shift >= 0)
                result = jnp.where(here, value, result)
        spot[pl.ds(b, R, stride=FB), :] = result


def with_corners(cells, i, corner):
    if i not in (7, 8, 9, 10):
        return cells
    row, lane = iotas(cells.shape[0])
    column, upper = {7: (0, 0), 10: (15, 0), 9: (112, 1), 8: (127, 1)}[i]
    return jnp.where((lane == column) & (((row // FB) & 1) == upper), corner, cells)


def stream_local(post, mask, ez, dst):
    put(dst, 0, at(post, 0, FR))
    for h in range(2):
        bits = at(mask, h * 64, 64)
        solid = (bits & 1) > 0
        for i in range(1, 19):
            cx, cy, cz = VELOCITIES[i]
            start = max(h * 64 - 8 * cz, 0)
            stop = min(h * 64 + 64 - 8 * cz, FR)
            size = stop - start
            g = at(post, i * FR + start, size)
            if cx:
                g = roll(g, cx, 1)
            if cy:
                _, lane = iotas(size)
                g = roll(g, 16 * cy, 1)
                g = jnp.where(lane < 16 if cy == 1 else lane >= 112, swap_halves(g, FB), g)
            if size < 64:
                k = ZP.index(i) if cz == 1 else 5 + ZM.index(i)
                layer = at(ez, 8 * k, 8)
                g = jnp.concatenate([layer, g] if cz == 1 else [g, layer], axis=0)
            here = h * 64
            g = jnp.where((bits & (1 << i)) > 0, at(post, OPPOSITE[i] * FR + here, 64), g)
            put(dst, i * FR + here, jnp.where(solid, at(post, i * FR + here, 64), g))


def stream_sides(local, faces, dst):
    for i in range(19):
        cx, cy, cz = VELOCITIES[i]
        for h in range(2):
            here = h * 64
            g = at(local, i * FR + here, 64)
            start = max(here - 8 * cz, 0)
            stop = min(here + 64 - 8 * cz, FR)
            size = stop - start
            if not (cx or cy):
                put(dst, i * FR + here, g)
                continue
            layer = None
            if size < 64:
                layer = g[:8] if cz == 1 else g[-8:]
                g = g[8:] if cz == 1 else g[:-8]
            _, lane = iotas(size)
            if cx:
                face, column = (0, -XP.index(i)) if cx == 1 else (FR, 10 - XM.index(i))
                side = roll(at(faces, face + start, size), column, 1)
                if cy:
                    side = roll(side, 16 * cy, 1)
                    edge = lane < 16 if cy == 1 else lane >= 112
                    side = jnp.where(edge, swap_halves(side, FB), side)
                g = jnp.where((lane & 15) == (0 if cx == 1 else 15), side, g)
            if cy:
                upper = upper_of(size, FB)
                if cy == 1:
                    side = roll(at(faces, 2 * FR + start, size), cx - 16 * YP.index(i), 1)
                    g = jnp.where((lane < 16) & jnp.logical_not(upper), side, g)
                else:
                    side = roll(at(faces, 3 * FR + start, size), 112 + cx - 16 * YM.index(i), 1)
                    g = jnp.where((lane >= 112) & upper, side, g)
            if layer is not None:
                g = jnp.concatenate([layer, g] if cz == 1 else [g, layer], axis=0)
            put(dst, i * FR + here, g)


class CoarseSides:
    def __init__(self, meta, device, sign):
        self.has, self.which, self.slot = [], [], []
        for k in range(6):
            index = [number(meta, c, M_CNBR + k) for c in range(CB)]
            safe = [jnp.maximum(n, 0) for n in index]
            self.has.append(index)
            self.which.append(
                [jnp.clip(((n >> 1) - device) * sign + 1, 0, 2) * EDGES2 for n in safe]
            )
            self.slot.append([n & 1 for n in safe])

    def exists(self, k, rows):
        row, _ = iotas(rows)
        first, second = self.has[k]
        return jnp.where((row & 1) == 0, first, second) >= 0

    def face(self, k, halo, spot):
        for c in range(CB):
            if k < 2:
                start = self.which[k][c] + 2 * self.slot[k][c] + k
            else:
                start = self.which[k][c] + PY_AT + self.slot[k][c]
            spot[pl.ds(k * CR + c, R, stride=CB), :] = halo[pl.ds(start, R, stride=FB), :]

    def layers(self, k, halo, spot, count):
        for c in range(CB):
            for n in range(count):
                start = self.which[k][c] + ZS + 8 * n + 4 * (k - 4) + self.slot[k][c]
                spot[pl.ds(8 * n + 4 * (k - 4) + c, 2, stride=2), :] = halo[
                    pl.ds(start, 2, stride=2), :
                ]


def first_sides_kernel(
    local,
    f_own,
    x_in,
    n_in,
    group,
    cpost,
    e_halo,
    new,
    fixed,
    plan,
    cmid,
    c_out,
    halo,
    faces,
    spare,
    cfaces,
    clayers,
    meta_n,
    meta_own,
    meta_x,
    sem,
):
    device, sign = place()
    copies = fetch_meta(((n_in, meta_n), (f_own, meta_own), (x_in, meta_x)), sem)
    gather_halo(f_own, x_in, n_in, EDGES, halo)
    put(c_out, 0, zeros(2 * FR))
    for c in copies:
        c.wait()
    gather_faces(meta_own, device, sign, e_halo, halo, faces)

    row8, _ = iotas(8)
    sides = CoarseSides(meta_own, device, sign)
    for k in range(4):
        sides.face(k, halo, cfaces)
    for k in (4, 5):
        sides.layers(k, halo, clayers, 1)
    put(cmid, 0, at(cpost, 0, CR))
    for i in range(1, 19):
        cx, cy, cz = VELOCITIES[i]
        a = at(cpost, i * CR, CR)
        k = {1: 0, -1: 1}[cx] if cx else {1: 2, -1: 3}[cy] if cy else {1: 4, -1: 5}[cz]
        if cx:
            column = -10 - XP.index(i) if cx == 1 else 5 - XM.index(i)
            side = roll(at(cfaces, k * CR, CR), column, 1)
            g = move_x(a, cx, jnp.where(sides.exists(k, CR), side, a))
        elif cy:
            column = -16 * (5 + YP1.index(i)) if cy == 1 else 112 - 16 * (5 + YM1.index(i))
            side = roll(at(cfaces, k * CR, CR), column, 1)
            g = move_y(a, cy, jnp.where(sides.exists(k, CR), side, a), CB)
        else:
            own = a[:8] if cz == 1 else a[-8:]
            g = move_z_coarse(a, cz, jnp.where(sides.exists(k, 8), clayers[0:8, :], own))
        put(cmid, i * CR, g)
    put(cfaces, 0, pack_y(lambda i: at(cmid, i * CR, CR), YP2, YM2, 5, zeros(CR), CB))
    for c in range(CB):
        c_out[pl.ds(PY_AT + c, R, stride=FB), :] = cfaces[pl.ds(c, R, stride=CB), :]
    for k in range(4):
        top = roll(at(cmid, (ZP2[k] + 1) * CR - 8, 8), 4, 0)
        bottom = roll(at(cmid, ZM2[k] * CR, 8), 4, 0)
        put(c_out, 2 * FR + 8 * k, jnp.where(row8 < 4, top, bottom))

    from_n = at(n_in, N_EC, 8)
    plan[...] = plan_corners(
        meta_n, meta_own, meta_x, device, sign, e_halo, group[...], from_n, fixed, spare
    )
    stream_sides(local, faces, new)


def second_collision_kernel(
    new, mask, f_own, x_in, n_in, x_late, fixed, plan, coarse, post, f_out, spot, plan_s, sem
):
    (fetch,) = fetch_meta(((plan, plan_s),), sem, 0)
    put(f_out, ZS, coarse[pl.ds(2 * FR, R), :])
    fetch.wait()
    corners(plan_s, f_own, x_in, n_in, x_late, EDGES, fixed, spot)
    collide_rows(new, post, FR, OMEGA_FINE, mask, spot)
    send_faces(post, f_out, EDGES2, coarse, spot)


def second_sides_kernel(
    local, f_own, x_in, n_in, e_halo, f_first, new, halo, faces, meta, sem
):
    device, sign = place()
    (fetch,) = fetch_meta(((f_first, meta),), sem)
    gather_halo(f_own, x_in, n_in, EDGES2, halo)
    fetch.wait()
    gather_faces(meta, device, sign, e_halo, halo, faces)
    stream_sides(local, faces, new)


def coarsen_kernel(
    new,
    f_own,
    x_in,
    n_in,
    x_late,
    fixed,
    plan,
    cornered,
    side_means,
    means,
    spot,
    plan_s,
    sem,
):
    (fetch,) = fetch_meta(((plan, plan_s),), sem, 0)
    fetch.wait()
    corners(plan_s, f_own, x_in, n_in, x_late, EDGES2, fixed, spot)
    for i in range(7, 11):
        put(cornered, (i - 7) * FR, with_corners(at(new, i * FR, FR), i, spot[...]))

    coarse_means(((new, 0, 0, 7), (cornered, 7, 7, 11), (new, 0, 11, 19)), means)
    pack_side_means(means, side_means)


def tail_kernel(
    f_first,
    new,
    cornered,
    f_own,
    x_in,
    n_in,
    cmid,
    fine_out,
    cpassed,
    halo,
    cfaces,
    clayers,
    meta_own,
    sem,
    out_sem,
):
    device, sign = place()
    (fetch,) = fetch_meta(((f_first, meta_own),), sem)
    pieces = (
        (new, 0, 0, 7 * FR),
        (cornered, 0, 7 * FR, 4 * FR),
        (new, 11 * FR, 11 * FR, 8 * FR),
    )
    outs = [
        pltpu.make_async_copy(
            ref.at[pl.ds(source, rows)], fine_out.at[pl.ds(to, rows)], out_sem.at[k]
        )
        for k, (ref, source, to, rows) in enumerate(pieces)
    ]
    for c in outs:
        c.start()
    gather_halo(f_own, x_in, n_in, EDGES2, halo)
    fetch.wait()
    sides = CoarseSides(meta_own, device, sign)
    for k in (2, 3):
        sides.face(k, halo, cfaces)
    for k in (4, 5):
        sides.layers(k, halo, clayers, 4)
    for i in range(19):
        a = at(cmid, i * CR, CR)
        g = a
        if i in YP2 or i in YM2:
            cy = 1 if i in YP2 else -1
            k = 2 if cy == 1 else 3
            column = -16 * (5 + YP2.index(i)) if cy == 1 else 112 - 16 * (5 + YM2.index(i))
            side = roll(at(cfaces, k * CR, CR), column, 1)
            g = move_y(a, cy, jnp.where(sides.exists(k, CR), side, a), CB)
        elif i in ZP2 or i in ZM2:
            cz = 1 if i in ZP2 else -1
            k = 4 if cz == 1 else 5
            n = (ZP2 if cz == 1 else ZM2).index(i)
            own = a[:8] if cz == 1 else a[-8:]
            side = jnp.where(sides.exists(k, 8), at(clayers, 8 * n, 8), own)
            g = move_z_coarse(a, cz, side)
        put(cpassed, i * CR, g)
    for c in outs:
        c.wait()


def coarse_last_kernel(
    f_first,
    cpassed,
    own,
    two,
    x_in,
    own_sides,
    two_sides,
    x_sides,
    coarse_out,
    gathered,
    sides,
    meta,
    sem,
):
    device, _ = place()
    (fetch,) = fetch_meta(((f_first, meta),), sem)
    put(gathered, 0, own[...])
    put(gathered, K_ROWS, x_in[0:K_ROWS, :])
    put(gathered, 2 * K_ROWS, two[...])
    put(gathered, 3 * K_ROWS, x_in[K_ROWS : 2 * K_ROWS, :])
    put(sides, 0, own_sides[...])
    put(sides, S_ROWS, x_sides[0:S_ROWS, :])
    put(sides, 2 * S_ROWS, two_sides[...])
    put(sides, 3 * S_ROWS, x_sides[S_ROWS : 2 * S_ROWS, :])
    coarse_out[...] = cpassed[...]
    _, lane = iotas(8)
    x = lane & 15
    x_half = (lane >> 3) & 1
    fetch.wait()
    for c in range(CB):
        for qy in range(2):
            children = [number(meta, c, M_CHILD + 2 * qy + qx) for qx in range(2)]
            found = []
            for qx in range(2):
                child = jnp.maximum(children[qx], 0)
                slot = ((child >> 2) ^ device) & 3
                pair, h = (child & 3) >> 1, child & 1
                start = slot * K_ROWS + pair * (19 * 8)
                layers = [at(sides, slot * S_ROWS + pair * 32 + 8 * k, 8) for k in range(4)]
                values = []
                for i in range(19):
                    value = roll(at(gathered, start + 8 * i, 8), (8 * (qx - h)) & 127, 1)
                    for k, group in enumerate((XP, XM)):
                        if i in group:
                            to = 8 * qx + 7 * k
                            shift = (to - 2 * group.index(i) - h) & 127
                            value = jnp.where(x == to, roll(layers[k], shift, 1), value)
                    for k, group in enumerate((YP, YM)):
                        if i in group:
                            shift = (112 * k + 8 * (qx - h) - 16 * group.index(i)) & 127
                            edge = (lane >> 4) == 7 * k
                            value = jnp.where(edge, roll(layers[2 + k], shift, 1), value)
                    values.append(value)
                found.append(values)
            index = jnp.where(x_half == 0, children[0], children[1])
            for i in range(19):
                rows = pl.ds(i * CR + 2 * qy + c, 8, stride=4)
                value = jnp.where(x_half == 0, found[0][i], found[1][i])
                coarse_out[rows, :] = jnp.where(index >= 0, value, cpassed[rows, :])


VMEM = pl.BlockSpec(memory_space=pltpu.VMEM)
HBM = pl.BlockSpec(memory_space=pltpu.HBM)


def rows_of(n, dtype=jnp.float32):
    return jax.ShapeDtypeStruct((n, 128), dtype)


def scratch(n, dtype=jnp.float32):
    return pltpu.VMEM((n, 128), dtype)


def call(kernel, name, specs, outs, scratches, out_specs=None):
    return pl.pallas_call(
        kernel,
        name=name,
        in_specs=specs,
        out_specs=out_specs or [VMEM] * len(outs),
        out_shape=outs,
        scratch_shapes=scratches,
        cost_estimate=pl.CostEstimate(flops=1 << 20, bytes_accessed=4 << 20, transcendentals=0),
        compiler_params=pltpu.CompilerParams(vmem_limit_bytes=32 * 1024 * 1024),
    )


def meta_scratch(n=3):
    return [pltpu.SMEM((8, 128), jnp.float32)] * n + [pltpu.SemaphoreType.DMA((n,))]


def exchange(rows, devices, partner):
    return lax.ppermute(rows, AXES, [(i, partner(i)) for i in range(devices)])


def as_rows(cells, directions):
    blocks = cells.shape[0]
    cells = cells.reshape(blocks, directions, R, 128)
    return cells.transpose(1, 2, 0, 3).reshape(directions * R * blocks, 128)


def as_cells(rows, blocks):
    return rows.reshape(19, R, blocks, 128).transpose(2, 0, 1, 3).reshape(blocks, 19, R * 128)


def on_device(fine_pop, coarse_pop, fine_nbr, coarse_nbr, parent, children, solid):
    devices = lax.axis_size(AXES)
    by_one = lambda a: exchange(a, devices, lambda i: i ^ 1)
    by_two = lambda a: exchange(a, devices, lambda i: i ^ 2)
    odd_even = lambda a: exchange(a, devices, lambda i: (((i + 1) ^ 1) - 1) % devices)
    parent = parent.T
    small = lambda a: pltpu.SMEM(a.shape, jnp.int32)
    in_hbm = lambda a: pltpu.with_memory_space_constraint(a, pltpu.HBM)

    raw, e_own, meta = call(
        coarse_first_kernel,
        "coarse_first",
        [HBM] * 5,
        [rows_of(C_ALL), rows_of(E_ROWS), rows_of(8)],
        [
            small(fine_nbr),
            small(parent),
            small(coarse_nbr),
            small(children),
            pltpu.SemaphoreType.DMA((5,)),
        ],
    )(
        in_hbm(as_rows(coarse_pop, 19)),
        in_hbm(fine_nbr),
        in_hbm(parent),
        in_hbm(coarse_nbr),
        in_hbm(children),
    )
    e_two = by_two(e_own)
    cpost, post, mask, f_own = call(
        fine_first_kernel,
        "fine_first",
        [VMEM, VMEM, HBM, HBM],
        [rows_of(C_ALL), rows_of(F_ALL), rows_of(FR, jnp.int32), rows_of(F_ROWS)],
        [
            scratch(F_ALL),
            scratch(FR, jnp.int32),
            scratch(2 * FR + 8),
            scratch(FR),
            pltpu.SemaphoreType.DMA((2,)),
        ],
    )(meta, raw, in_hbm(as_rows(fine_pop, 19)), in_hbm(as_rows(solid, 1)))

    x_in = by_one(jnp.concatenate([f_own, e_own, e_two]))
    group = (
        e_own[EC_AT:] + x_in[X_E + EC_AT : X_E2] + e_two[EC_AT:] + x_in[X_E2 + EC_AT :]
    )
    n_in = odd_even(
        jnp.concatenate(
            [f_own[:EDGES], f_own[EDGES:META] + x_in[EDGES:META], f_own[META:], group]
        )
    )
    e_halo, ez, local = call(
        first_local_kernel,
        "first_local",
        [VMEM] * 6,
        [rows_of(2 * FR), rows_of(80), rows_of(F_ALL)],
        [scratch(4 * E_ROWS + R)] + meta_scratch(1),
    )(f_own, e_own, e_two, x_in, post, mask)
    far_edges, ez = lax.optimization_barrier((n_in[EDGES:META], ez))
    x_late = by_one(far_edges)
    new, fixed, plan, cmid, c2_own = call(
        first_sides_kernel,
        "first_sides",
        [VMEM] * 7,
        [
            rows_of(F_ALL),
            rows_of(FB * R),
            rows_of(8),
            rows_of(C_ALL),
            rows_of(2 * FR + R),
        ],
        [scratch(HALO), scratch(4 * FR), scratch(2 * R), scratch(4 * CR), scratch(8)]
        + meta_scratch(),
    )(local, f_own, x_in, n_in, group, cpost, e_halo)
    post2, f2_own = call(
        second_collision_kernel,
        "second_collision",
        [VMEM] * 9,
        [rows_of(F_ALL), rows_of(F2_ROWS)],
        [scratch(FR)] + meta_scratch(1),
    )(new, mask, f_own, x_in, n_in, x_late, fixed, plan, c2_own)

    x2_in = by_one(f2_own)
    n2_in = odd_even(
        jnp.concatenate([f2_own[:EDGES2], f2_own[EDGES2:] + x2_in[EDGES2:]])
    )
    local2, means = call(
        second_local_kernel,
        "second_local",
        [VMEM] * 3,
        [rows_of(F_ALL), rows_of(K_ROWS)],
        [],
    )(post2, mask, ez)
    k_two = by_two(means)
    far_edges2, local2 = lax.optimization_barrier((n2_in[EDGES2:], local2))
    x2_late = by_one(far_edges2)
    (new2,) = call(
        second_sides_kernel,
        "second_sides",
        [VMEM] * 6,
        [rows_of(F_ALL)],
        [scratch(HALO), scratch(4 * FR)] + meta_scratch(1),
    )(local2, f2_own, x2_in, n2_in, e_halo, f_own)
    cornered, sides = call(
        coarsen_kernel,
        "coarsen",
        [VMEM] * 7,
        [rows_of(4 * FR), rows_of(S_ROWS)],
        [scratch(K_ROWS), scratch(FR)] + meta_scratch(1),
    )(new2, f2_own, x2_in, n2_in, x2_late, fixed, plan)

    k_two, sides = lax.optimization_barrier((k_two, sides))
    sides_two = by_two(sides)
    fine_out, cpassed = call(
        tail_kernel,
        "tail",
        [VMEM] * 7,
        [rows_of(F_ALL), rows_of(C_ALL)],
        [scratch(3 * EDGES2), scratch(4 * CR), scratch(R)]
        + meta_scratch(1)
        + [pltpu.SemaphoreType.DMA((3,))],
        [HBM, VMEM],
    )(f_own, new2, cornered, f2_own, x2_in, n2_in, cmid)
    k_one = by_one(jnp.concatenate([means, k_two]))
    sides_two, cpassed, k_one = lax.optimization_barrier((sides_two, cpassed, k_one))
    sides_one = by_one(jnp.concatenate([sides, sides_two]))
    (coarse_out,) = call(
        coarse_last_kernel,
        "coarse_last",
        [VMEM] * 8,
        [rows_of(C_ALL)],
        [scratch(4 * K_ROWS), scratch(4 * S_ROWS)] + meta_scratch(1),
    )(f_own, cpassed, means, k_two, k_one, sides, sides_two, sides_one)
    return as_cells(fine_out, FB), as_cells(coarse_out, CB)


def solution(mesh):
    rows = P(AXES, None)
    blocks = P(AXES, None, None)
    return jax.shard_map(
        on_device,
        mesh=mesh,
        in_specs=(blocks, blocks, rows, rows, rows, rows, rows),
        out_specs=(blocks, blocks),
        check_vma=False,
    )
```

```python
import jax
import jax.numpy as jnp
from jax import lax
from jax.experimental import pallas as pl
from jax.experimental.pallas import tpu as pltpu
from jax.sharding import PartitionSpec as P

AXES = ("gx", "gy")
VELOCITIES = (
    (0, 0, 0),
    (1, 0, 0),
    (-1, 0, 0),
    (0, 1, 0),
    (0, -1, 0),
    (0, 0, 1),
    (0, 0, -1),
    (1, 1, 0),
    (-1, -1, 0),
    (1, -1, 0),
    (-1, 1, 0),
    (1, 0, 1),
    (-1, 0, -1),
    (1, 0, -1),
    (-1, 0, 1),
    (0, 1, 1),
    (0, -1, -1),
    (0, 1, -1),
    (0, -1, 1),
)
WEIGHTS = (1.0 / 3.0,) + (1.0 / 18.0,) * 6 + (1.0 / 36.0,) * 12
OPPOSITE = (0, 2, 1, 4, 3, 6, 5, 8, 7, 10, 9, 12, 11, 14, 13, 16, 15, 18, 17)
OMEGA_COARSE = 1.6
OMEGA_FINE = 1.0 / (2.0 * (1.0 / 1.6 - 0.5) + 0.5)

XP = (1, 7, 9, 11, 13)
XM = (2, 8, 10, 12, 14)
YP = (3, 7, 10, 15, 17)
YM = (4, 8, 9, 16, 18)
ZP = (5, 11, 14, 15, 18)
ZM = (6, 12, 13, 16, 17)
YP1, YM1 = (3, 15, 17), (4, 16, 18)
YP2, YM2 = (7, 10), (8, 9)
ZP2, ZM2 = (11, 14, 15, 18), (12, 13, 16, 17)


R = 32
FB, CB = 4, 2
FR, CR = FB * R, CB * R
F_ALL, C_ALL = 19 * FR, 19 * CR
PY_AT = FR
ZS = 2 * FR
EDGES = ZS + 8
META = EDGES + R
F_ROWS = META + 8
EDGES2 = ZS + R
F2_ROWS = EDGES2 + R
N_EC = F_ROWS
EC_AT = 4 * R + 40
E_ROWS = EC_AT + 8
K_ROWS = 2 * 19 * 8
S_ROWS = 2 * 32
HALO = 3 * EDGES2
X_E = F_ROWS
X_E2 = X_E + E_ROWS
M_PARENT, M_CNBR, M_CHILD = 4, 8, 16


def iotas(rows=R):
    row = lax.broadcasted_iota(jnp.int32, (rows, 128), 0)
    lane = lax.broadcasted_iota(jnp.int32, (rows, 128), 1)
    return row, lane


def roll(a, shift, axis):
    if isinstance(shift, int):
        shift = shift % a.shape[axis]
        if shift == 0:
            return a
    return pltpu.roll(a, shift, axis)


def at(ref, start, size=R):
    if not isinstance(start, int):
        start = pl.multiple_of(start, 8)
    return ref[pl.ds(start, size), :]


def put(ref, start, value):
    if not isinstance(start, int):
        start = pl.multiple_of(start, 8)
    ref[pl.ds(start, value.shape[0]), :] = value


def zeros(rows):
    return jnp.zeros((rows, 128), jnp.float32)


def total(terms):
    while len(terms) > 1:
        pairs = [terms[k] + terms[k + 1] for k in range(0, len(terms) - 1, 2)]
        terms = pairs + terms[len(terms) - len(terms) % 2 :]
    return terms[0]


def collide(f, rate):
    rho = total(f)
    mom = []
    for axis in range(3):
        plus = [f[i] for i in range(19) if VELOCITIES[i][axis] == 1]
        minus = [f[i] for i in range(19) if VELOCITIES[i][axis] == -1]
        mom.append(total(plus) - total(minus))
    inv = 1.0 / rho
    u = [m * inv for m in mom]
    base = 1.0 - 1.5 * (u[0] * u[0] + u[1] * u[1] + u[2] * u[2])
    scaled = {w: (rate * w) * rho for w in sorted(set(WEIGHTS))}
    keep = 1.0 - rate
    out = [None] * 19
    out[0] = keep * f[0] + scaled[WEIGHTS[0]] * base
    for i in range(1, 19, 2):
        proj = None
        for axis in range(3):
            c = VELOCITIES[i][axis]
            if c:
                term = u[axis]
                if proj is None:
                    proj = term if c > 0 else -term
                else:
                    proj = proj + term if c > 0 else proj - term
        even = base + 4.5 * (proj * proj)
        odd = 3.0 * proj
        w = scaled[WEIGHTS[i]]
        out[i] = keep * f[i] + w * (even + odd)
        out[i + 1] = keep * f[i + 1] + w * (even - odd)
    return out


def collide_rows(src, dst, rows, rate, mask=None, corner=None):
    def body(v, carry):
        f = [at(src, i * rows + v * 16, 16) for i in range(19)]
        if corner is not None:
            edge = at(corner, v * 16, 16)
            f = [with_corners(f[i], i, edge) for i in range(19)]
        post = collide(f, rate)
        if mask is not None:
            solid = (at(mask, v * 16, 16) & 1) > 0
            post = [jnp.where(solid, f[i], post[i]) for i in range(19)]
        for i in range(19):
            put(dst, i * rows + v * 16, post[i])
        return carry

    lax.fori_loop(0, rows // 16, body, 0)


def upper_of(rows, blocks):
    row, _ = iotas(rows)
    return ((row // blocks) & 1) == 1


def swap_halves(a, blocks):
    if blocks == 4:
        rows = a.shape[0]
        return pltpu.roll(a.reshape(rows // 8, 8, 128), 4, 1).reshape(rows, 128)
    return jnp.where(upper_of(a.shape[0], blocks), roll(a, blocks, 0), roll(a, -blocks, 0))


def pack_x(get, packed, first=0):
    _, lane = iotas(packed.shape[0])
    x = lane & 15
    for j in range(5):
        packed = jnp.where(x == first + j, roll(get(XP[j]), first + j - 15, 1), packed)
        packed = jnp.where(x == first + 5 + j, roll(get(XM[j]), first + 5 + j, 1), packed)
    return packed


def pack_y(get, plus, minus, first, rest, blocks):
    rows = rest.shape[0]
    _, lane = iotas(rows)
    upper = upper_of(rows, blocks)
    group = lane >> 4
    packed = zeros(rows)
    for k in range(len(plus)):
        p = first + k
        one = jnp.where(upper, roll(get(plus[k]), 16 * p - 112, 1), roll(get(minus[k]), 16 * p, 1))
        packed = jnp.where(group == p, one, packed)
    packed = swap_halves(packed, blocks)
    return jnp.where((group >= first) & (group < first + len(plus)), packed, rest)


def pack_edges(get, rows):
    _, lane = iotas(rows)
    upper = upper_of(rows, FB)
    first = jnp.where(upper, roll(get(7), -127, 1), get(8))
    second = jnp.where(upper, roll(get(10), 1 - 112, 1), roll(get(9), 1 - 15, 1))
    return swap_halves(jnp.where(lane == 0, first, second), FB)


def move_x(a, cx, halo):
    _, lane = iotas(a.shape[0])
    x = lane & 15
    if cx == 1:
        return jnp.where(x == 0, halo, roll(a, 1, 1))
    return jnp.where(x == 15, halo, roll(a, -1, 1))


def move_y(a, cy, halo, blocks):
    _, lane = iotas(a.shape[0])
    upper = upper_of(a.shape[0], blocks)
    near = roll(a, 16 * cy, 1)
    if cy == 1:
        return jnp.where(lane < 16, jnp.where(upper, swap_halves(near, blocks), halo), near)
    return jnp.where(lane >= 112, jnp.where(upper, halo, swap_halves(near, blocks)), near)


def move_z_coarse(a, cz, halo8):
    row, _ = iotas(8)
    near = roll(a, 4 * cz, 0)
    if cz == 1:
        return jnp.concatenate([jnp.where(row < 4, halo8, near[:8]), near[8:]], axis=0)
    return jnp.concatenate([near[:-8], jnp.where(row >= 4, halo8, near[-8:])], axis=0)


def send_faces(post, out, edges, coarse, spot):
    for h in range(2):
        rows = h * 64
        get = lambda i: at(post, i * FR + rows, 64)
        put(out, rows, pack_x(get, at(coarse, rows, 64)))
        put(out, PY_AT + rows, pack_y(get, YP, YM, 0, at(coarse, PY_AT + rows, 64), FB))
        put(spot, rows, pack_edges(get, 64))
    _, lane = iotas()
    device, _ = place()
    first = 8 * (device & 1)
    packed = zeros(R)
    for b in range(FB):
        one = roll(spot[pl.ds(b, R, stride=FB), :], first + 2 * b, 1)
        packed = jnp.where((lane >> 1) == (first >> 1) + b, one, packed)
    put(out, edges, packed)


def place():
    device = lax.axis_index("gx") * lax.axis_size("gy") + lax.axis_index("gy")
    sign = 1 - 2 * (device & 1)
    return device, sign


def number(meta, row, column):
    return meta[row, column].astype(jnp.int32)


def fetch_meta(pairs, sem):
    copies = [
        pltpu.make_async_copy(ref.at[pl.ds(META, 8)], dst, sem.at[k])
        for k, (ref, dst) in enumerate(pairs)
    ]
    for c in copies:
        c.start()
    return copies


def coarse_first_kernel(
    pop_hbm,
    nbr_hbm,
    parent_hbm,
    cnbr_hbm,
    children_hbm,
    raw,
    e_out,
    meta_out,
    nbr,
    parent,
    cnbr,
    children,
    sem,
):
    copies = [
        pltpu.make_async_copy(src, dst, sem.at[k])
        for k, (src, dst) in enumerate(
            (
                (pop_hbm, raw),
                (nbr_hbm, nbr),
                (parent_hbm, parent),
                (cnbr_hbm, cnbr),
                (children_hbm, children),
            )
        )
    ]
    for c in copies:
        c.start()
    copies[0].wait()
    _, lane = iotas()
    row8, lane8 = iotas(8)
    x = lane & 15
    half = lambda i: at(raw, i * CR)
    for qx in range(2):
        packed = zeros(R)
        for j in range(5):
            packed = jnp.where(x == j, roll(half(XP[j]), j - 8 * qx, 1), packed)
            packed = jnp.where(x == 5 + j, roll(half(XM[j]), 5 + j - 8 * qx - 7, 1), packed)
        put(e_out, qx * R, packed)
    low, high = zeros(R), zeros(R)
    for p in range(5):
        low = jnp.where((lane >> 4) == p, roll(half(YP[p]), 16 * p, 1), low)
        high = jnp.where((lane >> 4) == p, roll(half(YM[p]), 16 * p - 112, 1), high)
    put(e_out, 2 * R, low)
    put(e_out, 3 * R, high)
    for k in range(5):
        e_out[pl.ds(4 * R + 4 * k, 4), :] = raw[pl.ds(ZP[k] * CR, 4), :]
        e_out[pl.ds(4 * R + 20 + 4 * k, 4), :] = raw[pl.ds(ZM[k] * CR + 28, 4), :]
    corner = zeros(8)
    for c in range(CB):
        for q in range(4):
            for e, (i, yq, xq) in enumerate(((7, 7, 0), (10, 7, 7), (9, 0, 0), (8, 0, 7))):
                to = (c * 4 + q) * 4 + e
                rows = raw[pl.ds(i * CR + (q // 2) * 2 + c, 8, stride=4), :]
                rows = roll(rows, to - (yq * 16 + 8 * (q % 2) + xq), 1)
                corner = jnp.where(lane8 == to, rows, corner)
    device, _ = place()
    put(e_out, EC_AT, roll(corner, 32 * (device & 3), 1))

    for c in copies[1:]:
        c.wait()
    meta = zeros(8)
    entries = []
    for b in range(FB):
        entries += [(b, k, nbr[b, k]) for k in range(4)]
        entries += [(b, M_PARENT + k, parent[k, b]) for k in range(2)]
    for c in range(CB):
        entries += [(c, M_CNBR + k, cnbr[c, k]) for k in range(6)]
        entries += [(c, M_CHILD + k, children[c, k]) for k in range(4)]
    for b, k, value in entries:
        meta = jnp.where((row8 == b) & (lane8 == k), value.astype(jnp.float32), meta)
    put(meta_out, 0, meta)


def fine_first_kernel(
    meta,
    raw,
    pop_hbm,
    solid_hbm,
    cpost,
    post,
    mask,
    f_out,
    pop,
    solid,
    coarse,
    spot,
    sem,
):
    copies = [
        pltpu.make_async_copy(pop_hbm, pop, sem.at[0]),
        pltpu.make_async_copy(solid_hbm, solid, sem.at[1]),
    ]
    for c in copies:
        c.start()
    row8, _ = iotas(8)
    collide_rows(raw, cpost, CR, OMEGA_COARSE)
    get = lambda i: at(cpost, i * CR, CR)
    _, wide = iotas(CR)
    ahead, back = zeros(CR), zeros(CR)
    for j in range(5):
        ahead = jnp.where((wide & 15) == 10 + j, roll(get(XP[j]), 10 + j - 15, 1), ahead)
        back = jnp.where((wide & 15) == 10 + j, roll(get(XM[j]), 10 + j, 1), back)
    for k, packed in enumerate((ahead, back)):
        put(spot, 0, packed)
        for c in range(CB):
            coarse[pl.ds(2 * c + k, R, stride=FB), :] = spot[pl.ds(c, R, stride=CB), :]
    put(spot, 0, pack_y(get, YP1, YM1, 5, zeros(CR), CB))
    for c in range(CB):
        coarse[pl.ds(PY_AT + c, R, stride=FB), :] = spot[pl.ds(c, R, stride=CB), :]
        coarse[pl.ds(PY_AT + 2 + c, R, stride=FB), :] = zeros(R)
    top = roll(at(cpost, 6 * CR - 8, 8), 4, 0)
    bottom = roll(at(cpost, 6 * CR, 8), 4, 0)
    put(coarse, 2 * FR, jnp.where(row8 < 4, top, bottom))

    for c in copies:
        c.wait()
    s = jnp.where(solid[...] > 0, 1, 0)
    bits = s
    none = jnp.zeros_like(s)
    by_z = {0: lambda a: a}
    by_z[1] = lambda a: jnp.concatenate([a[-8:], a[:-8]], axis=0)
    by_z[-1] = lambda a: jnp.concatenate([a[8:], a[:8]], axis=0)
    by_y = {cy: move_y(s, cy, none, FB) for cy in (1, -1)}
    by_y[0] = s
    by_x = {(cx, cy): roll(by_y[cy], cx, 1) for cx in (1, -1) for cy in (-1, 0, 1)}
    for i in range(1, 19):
        cx, cy, cz = VELOCITIES[i]
        moved = by_z[cz](by_x[cx, cy] if cx else by_y[cy])
        bits = bits | (moved << i)
    put(mask, 0, bits)
    collide_rows(pop, post, FR, OMEGA_FINE, mask)
    put(f_out, ZS, at(coarse, 2 * FR, 8))
    put(f_out, META, meta[...])
    send_faces(post, f_out, EDGES, coarse, spot)


def onehot(rows, cols, source):
    row = lax.broadcasted_iota(jnp.int32, (rows, cols), 0)
    col = lax.broadcasted_iota(jnp.int32, (rows, cols), 1)
    return jnp.where(row == source(col), 1.0, 0.0).astype(jnp.bfloat16)


def exact_dot(a, b):
    result = None
    for _ in range(3):
        part = a.astype(jnp.bfloat16)
        a = a - part.astype(jnp.float32)
        term = jnp.dot(part, b, preferred_element_type=jnp.float32)
        result = term if result is None else result + term
    return result


def first_local_kernel(
    f_own, e_own, e_two, x_in, post, mask, e_halo, ez, local, route, gathered, meta, sem
):
    device, sign = place()
    (fetch,) = fetch_meta(((f_own, meta),), sem)
    put(gathered, 0, e_own[...])
    put(gathered, E_ROWS, x_in[X_E : X_E + E_ROWS, :])
    put(gathered, 2 * E_ROWS, e_two[...])
    put(gathered, 3 * E_ROWS, x_in[X_E2 : X_E2 + E_ROWS, :])
    row, lane = iotas(16)
    x = lane & 15
    spread_x = onehot(128, 256, lambda m: ((m >> 7) * 4 + ((m & 127) >> 5)) * 16 + (m & 15))
    fetch.wait()
    for b in range(FB):
        p, q = number(meta, b, M_PARENT), number(meta, b, M_PARENT + 1)
        qy, qx = q >> 1, q & 1
        base = (((p >> 1) ^ device) & 3) * E_ROWS + qy * 2 + (p & 1)
        ex = exact_dot(gathered[pl.ds(base + qx * R, 8, stride=4), :], spread_x)
        spread_y = onehot(128, 128, lambda m: (m >> 4) * 16 + 8 * qx + ((m & 15) >> 1))
        ey = exact_dot(
            jnp.concatenate(
                [gathered[pl.ds(base + (2 + k) * R, 8, stride=4), :] for k in range(2)], axis=0
            ),
            spread_y,
        )
        for k in range(2):
            for yh in range(2):
                rows = pl.ds(8 * k + 4 * yh + b, 8, stride=16)
                e_halo[rows, :] = ex[:, 128 * yh : 128 * yh + 128]
                rows = pl.ds(PY_AT + 8 * k + 4 * yh + b, 8, stride=16)
                e_halo[rows, :] = ey[8 * yh : 8 * yh + 8]
        spread_z = onehot(
            128,
            256,
            lambda m: ((m >> 7) * 4 + ((m & 127) >> 5)) * 16 + 8 * qx + ((m & 15) >> 1),
        )
        ezs = exact_dot(gathered[pl.ds(base + 4 * R, 16, stride=4), :], spread_z)
        a0, a1 = ezs[:, :128], ezs[:, 128:]
        moves = {}
        moves[0, 0] = (a0, a1)
        moves[1, 0] = tuple(jnp.where(x == 0, a, roll(a, 1, 1)) for a in (a0, a1))
        moves[-1, 0] = tuple(jnp.where(x == 15, a, roll(a, -1, 1)) for a in (a0, a1))
        moves[0, 1] = (
            jnp.where(lane < 16, a0, roll(a0, 16, 1)),
            jnp.where(lane < 16, roll(a0, 16, 1), roll(a1, 16, 1)),
        )
        moves[0, -1] = (
            jnp.where(lane >= 112, roll(a1, -16, 1), roll(a0, -16, 1)),
            jnp.where(lane >= 112, a1, roll(a1, -16, 1)),
        )
        out = [a0, a1]
        for k, i in enumerate(ZP + ZM):
            moved = moves[VELOCITIES[i][:2]]
            out = [jnp.where(row == k, moved[h], out[h]) for h in range(2)]
        for h in range(2):
            ez[pl.ds(4 * h + b, 8, stride=8), :] = out[h][:8]
            ez[pl.ds(64 + 4 * h + b, 2, stride=8), :] = out[h][8:10]
    plan_faces(meta, device, sign, route)
    stream_local(post, mask, ez, local)


def coarse_means(pieces, means):
    row = lax.broadcasted_iota(jnp.int32, (128, 128), 0)
    col = lax.broadcasted_iota(jnp.int32, (128, 128), 1)
    target = lambda yh, h: (yh * 4 + (row >> 5)) * 16 + ((row & 15) >> 1) + 8 * h
    mats = [
        [jnp.where(col == target(yh, h), 0.125, 0.0).astype(jnp.bfloat16) for yh in range(2)]
        for h in range(2)
    ]
    for pair in range(2):
        for ref, base, first, last in pieces:
            rows = 8 * (last - first)
            total_rows = None
            for h in range(2):
                for yh in range(2):
                    start = (first - base) * FR + 4 * yh + 2 * pair + h
                    z0 = ref[pl.ds(start, rows, stride=16), :]
                    z1 = ref[pl.ds(start + 8, rows, stride=16), :]
                    part = exact_dot(z0 + z1, mats[h][yh])
                    total_rows = part if total_rows is None else total_rows + part
            put(means, pair * 19 * 8 + 8 * first, total_rows)


def pack_side_means(means, out):
    _, lane = iotas(8)
    x = lane & 15
    for pair in range(2):
        get = lambda i: at(means, pair * 19 * 8 + 8 * i, 8)
        packed = [zeros(8) for _ in range(4)]
        for j in range(5):
            for h in range(2):
                to = 2 * j + h
                packed[0] = jnp.where(x == to, roll(get(XP[j]), to - 8 * h, 1), packed[0])
                packed[1] = jnp.where(x == to, roll(get(XM[j]), to - 8 * h - 7, 1), packed[1])
            group = (lane >> 4) == j
            packed[2] = jnp.where(group, roll(get(YP[j]), 16 * j, 1), packed[2])
            packed[3] = jnp.where(group, roll(get(YM[j]), 16 * j - 112, 1), packed[3])
        for k in range(4):
            put(out, pair * 32 + 8 * k, packed[k])


def second_local_kernel(post, mask, ez, local, means):
    stream_local(post, mask, ez, local)
    coarse_means(((local, 0, 0, 19),), means)


def gather_halo(own, x_in, n_in, rows, halo):
    for k, ref in enumerate((n_in, own, x_in)):
        put(halo, k * EDGES2, ref[0:rows, :])


def plan_faces(meta, device, sign, route):
    row, _ = iotas(8)
    for k in range(4):
        slot = jnp.zeros((8, 128), jnp.int32)
        source = jnp.zeros((8, 128), jnp.int32)
        for b in range(FB):
            n = number(meta, b, k)
            safe = jnp.maximum(n, 0)
            which = jnp.clip(((safe >> 2) - device) * sign + 1, 0, 2)
            mine = (row & 3) == b
            slot = jnp.where(mine, safe & 3, slot)
            source = jnp.where(mine, jnp.where(n >= 0, which, 3), source)
        put(route, 16 * k, slot + (row & 4))
        put(route, 16 * k + 8, source)


def gather_faces(route, own, x_in, n_in, e_halo, faces):
    for k in range(4):
        rows, source = at(route, 16 * k, 8), at(route, 16 * k + 8, 8)
        first = PY_AT if k >= 2 else 0
        for v in range(0, FR, 8):
            n, o, x = (
                jnp.take_along_axis(at(ref, first + v, 8), rows, axis=0, mode="promise_in_bounds")
                for ref in (n_in, own, x_in)
            )
            side = jnp.where(source == 0, n, jnp.where(source == 1, o, x))
            put(faces, k * FR + v, jnp.where(source == 3, at(e_halo, first + v, 8), side))


def plan_corners(
    meta_n, meta_own, meta_x, device, sign, e_halo, group, from_n, fixed, plan, spare
):
    row, lane = iotas()
    for k in range(4):
        spare[pl.ds(k, 8, stride=4), :] = group
        spare[pl.ds(R + k, 8, stride=4), :] = from_n
    near_rows, far_rows = spare[0:R, :], spare[R : 2 * R, :]

    def pick(which, row, column):
        return jnp.where(
            which == 0,
            meta_n[row, column],
            jnp.where(which == 1, meta_own[row, column], meta_x[row, column]),
        ).astype(jnp.int32)

    for b in range(FB):
        result = zeros(R)
        source_lanes = jnp.full((R, 128), -1, jnp.int32)
        own_rows = e_halo[pl.ds(PY_AT + b, R, stride=FB), :]
        for side in range(2):
            n = number(meta_own, b, 2 + side)
            safe = jnp.maximum(n, 0)
            which = jnp.clip(((safe >> 2) - device) * sign + 1, 0, 2)
            p, q = (pick(which, safe & 3, M_PARENT + k) for k in range(2))
            rows = jnp.where(which == 0, far_rows, near_rows)
            for end in range(2):
                i = ((7, 10), (9, 8))[side][end]
                own_column = 16 * (YP, YM)[side].index(i) + 15 * end
                edge_column = ((0, 1), (1, 0))[side][end]
                to = 112 * side + 15 * end
                source = 32 * ((p >> 1) & 3) + ((p & 1) * 4 + q) * 4 + 2 * side + end
                value = jnp.where(
                    n < 0, roll(own_rows, to - own_column, 1), roll(rows, (to - source) & 127, 1)
                )
                result = jnp.where(lane == to, value, result)
                m = pick(which, safe & 3, end)
                there = jnp.maximum(m, 0) >> 2
                far = (there - device) * sign
                pair = jnp.where(far >= 2, 2, jnp.where(far < 0, 1, 0))
                column = 16 * pair + 8 * (there & 1) + 2 * (m & 3) + edge_column
                column = jnp.where((n >= 0) & (m >= 0), column, -1)
                here = (lane == to) & ((row & 1) == side)
                source_lanes = jnp.where(here, column, source_lanes)
        fixed[pl.ds(b, R, stride=FB), :] = result
        plan[pl.ds(b, R, stride=FB), :] = source_lanes


def corners(plan, own, x_in, n_in, x_late, at_row, fixed, spot):
    table = at(own, at_row) + at(x_in, at_row)
    table = table + roll(at(n_in, at_row), 16, 1) + roll(x_late[...], 32, 1)
    for b in range(FB):
        spot[pl.ds(b, R, stride=FB), :] = table
    for v in range(0, FR, 8):
        lanes = at(plan, v, 8)
        sent = jnp.take_along_axis(
            at(spot, v, 8), jnp.maximum(lanes, 0), axis=1, mode="promise_in_bounds"
        )
        put(spot, v, jnp.where(lanes >= 0, sent, at(fixed, v, 8)))


def with_corners(cells, i, corner):
    if i not in (7, 8, 9, 10):
        return cells
    row, lane = iotas(cells.shape[0])
    column, upper = {7: (0, 0), 10: (15, 0), 9: (112, 1), 8: (127, 1)}[i]
    return jnp.where((lane == column) & (((row // FB) & 1) == upper), corner, cells)


def stream_local(post, mask, ez, dst):
    put(dst, 0, at(post, 0, FR))
    for h in range(2):
        bits = at(mask, h * 64, 64)
        solid = (bits & 1) > 0
        for i in range(1, 19):
            cx, cy, cz = VELOCITIES[i]
            start = max(h * 64 - 8 * cz, 0)
            stop = min(h * 64 + 64 - 8 * cz, FR)
            size = stop - start
            g = at(post, i * FR + start, size)
            if cx:
                g = roll(g, cx, 1)
            if cy:
                _, lane = iotas(size)
                g = roll(g, 16 * cy, 1)
                g = jnp.where(lane < 16 if cy == 1 else lane >= 112, swap_halves(g, FB), g)
            if size < 64:
                k = ZP.index(i) if cz == 1 else 5 + ZM.index(i)
                layer = at(ez, 8 * k, 8)
                g = jnp.concatenate([layer, g] if cz == 1 else [g, layer], axis=0)
            here = h * 64
            g = jnp.where((bits & (1 << i)) > 0, at(post, OPPOSITE[i] * FR + here, 64), g)
            put(dst, i * FR + here, jnp.where(solid, at(post, i * FR + here, 64), g))


def stream_sides(local, faces, dst):
    for i in range(19):
        cx, cy, cz = VELOCITIES[i]
        for h in range(2):
            here = h * 64
            g = at(local, i * FR + here, 64)
            start = max(here - 8 * cz, 0)
            stop = min(here + 64 - 8 * cz, FR)
            size = stop - start
            if not (cx or cy):
                put(dst, i * FR + here, g)
                continue
            layer = None
            if size < 64:
                layer = g[:8] if cz == 1 else g[-8:]
                g = g[8:] if cz == 1 else g[:-8]
            _, lane = iotas(size)
            if cx:
                face, column = (0, -XP.index(i)) if cx == 1 else (FR, 10 - XM.index(i))
                side = roll(at(faces, face + start, size), column, 1)
                if cy:
                    side = roll(side, 16 * cy, 1)
                    edge = lane < 16 if cy == 1 else lane >= 112
                    side = jnp.where(edge, swap_halves(side, FB), side)
                g = jnp.where((lane & 15) == (0 if cx == 1 else 15), side, g)
            if cy:
                upper = upper_of(size, FB)
                if cy == 1:
                    side = roll(at(faces, 2 * FR + start, size), cx - 16 * YP.index(i), 1)
                    g = jnp.where((lane < 16) & jnp.logical_not(upper), side, g)
                else:
                    side = roll(at(faces, 3 * FR + start, size), 112 + cx - 16 * YM.index(i), 1)
                    g = jnp.where((lane >= 112) & upper, side, g)
            if layer is not None:
                g = jnp.concatenate([layer, g] if cz == 1 else [g, layer], axis=0)
            put(dst, i * FR + here, g)


class CoarseSides:
    def __init__(self, meta, device, sign):
        self.has, self.which, self.slot = [], [], []
        for k in range(6):
            index = [number(meta, c, M_CNBR + k) for c in range(CB)]
            safe = [jnp.maximum(n, 0) for n in index]
            self.has.append(index)
            self.which.append(
                [jnp.clip(((n >> 1) - device) * sign + 1, 0, 2) * EDGES2 for n in safe]
            )
            self.slot.append([n & 1 for n in safe])

    def exists(self, k, rows):
        row, _ = iotas(rows)
        first, second = self.has[k]
        return jnp.where((row & 1) == 0, first, second) >= 0

    def face(self, k, halo, spot):
        for c in range(CB):
            if k < 2:
                start = self.which[k][c] + 2 * self.slot[k][c] + k
            else:
                start = self.which[k][c] + PY_AT + self.slot[k][c]
            spot[pl.ds(k * CR + c, R, stride=CB), :] = halo[pl.ds(start, R, stride=FB), :]

    def layers(self, k, halo, spot, count):
        for c in range(CB):
            for n in range(count):
                start = self.which[k][c] + ZS + 8 * n + 4 * (k - 4) + self.slot[k][c]
                spot[pl.ds(8 * n + 4 * (k - 4) + c, 2, stride=2), :] = halo[
                    pl.ds(start, 2, stride=2), :
                ]


def first_sides_kernel(
    local,
    f_own,
    x_in,
    n_in,
    group,
    cpost,
    e_halo,
    route,
    new,
    fixed,
    plan,
    cmid,
    c_out,
    halo,
    faces,
    spare,
    cfaces,
    clayers,
    meta_n,
    meta_own,
    meta_x,
    sem,
):
    device, sign = place()
    copies = fetch_meta(((n_in, meta_n), (f_own, meta_own), (x_in, meta_x)), sem)
    gather_halo(f_own, x_in, n_in, EDGES, halo)
    put(c_out, 0, zeros(2 * FR))
    gather_faces(route, f_own, x_in, n_in, e_halo, faces)
    stream_sides(local, faces, new)
    for c in copies:
        c.wait()

    row8, _ = iotas(8)
    sides = CoarseSides(meta_own, device, sign)
    for k in range(4):
        sides.face(k, halo, cfaces)
    for k in (4, 5):
        sides.layers(k, halo, clayers, 1)
    put(cmid, 0, at(cpost, 0, CR))
    for i in range(1, 19):
        cx, cy, cz = VELOCITIES[i]
        a = at(cpost, i * CR, CR)
        k = {1: 0, -1: 1}[cx] if cx else {1: 2, -1: 3}[cy] if cy else {1: 4, -1: 5}[cz]
        if cx:
            column = -10 - XP.index(i) if cx == 1 else 5 - XM.index(i)
            side = roll(at(cfaces, k * CR, CR), column, 1)
            g = move_x(a, cx, jnp.where(sides.exists(k, CR), side, a))
        elif cy:
            column = -16 * (5 + YP1.index(i)) if cy == 1 else 112 - 16 * (5 + YM1.index(i))
            side = roll(at(cfaces, k * CR, CR), column, 1)
            g = move_y(a, cy, jnp.where(sides.exists(k, CR), side, a), CB)
        else:
            own = a[:8] if cz == 1 else a[-8:]
            g = move_z_coarse(a, cz, jnp.where(sides.exists(k, 8), clayers[0:8, :], own))
        put(cmid, i * CR, g)
    put(cfaces, 0, pack_y(lambda i: at(cmid, i * CR, CR), YP2, YM2, 5, zeros(CR), CB))
    for c in range(CB):
        c_out[pl.ds(PY_AT + c, R, stride=FB), :] = cfaces[pl.ds(c, R, stride=CB), :]
    for k in range(4):
        top = roll(at(cmid, (ZP2[k] + 1) * CR - 8, 8), 4, 0)
        bottom = roll(at(cmid, ZM2[k] * CR, 8), 4, 0)
        put(c_out, 2 * FR + 8 * k, jnp.where(row8 < 4, top, bottom))

    from_n = at(n_in, N_EC, 8)
    plan_corners(
        meta_n, meta_own, meta_x, device, sign, e_halo, group[...], from_n, fixed, plan, spare
    )


def second_collision_kernel(
    new, mask, f_own, x_in, n_in, x_late, fixed, plan, coarse, post, f_out, spot
):
    put(f_out, ZS, coarse[pl.ds(2 * FR, R), :])
    corners(plan, f_own, x_in, n_in, x_late, EDGES, fixed, spot)
    collide_rows(new, post, FR, OMEGA_FINE, mask, spot)
    send_faces(post, f_out, EDGES2, coarse, spot)


def second_sides_kernel(local, f_own, x_in, n_in, e_halo, route, new, faces):
    gather_faces(route, f_own, x_in, n_in, e_halo, faces)
    stream_sides(local, faces, new)


def coarsen_kernel(
    new,
    f_own,
    x_in,
    n_in,
    x_late,
    fixed,
    plan,
    cornered,
    side_means,
    means,
    spot,
):
    corners(plan, f_own, x_in, n_in, x_late, EDGES2, fixed, spot)
    for i in range(7, 11):
        put(cornered, (i - 7) * FR, with_corners(at(new, i * FR, FR), i, spot[...]))

    coarse_means(((new, 0, 0, 7), (cornered, 7, 7, 11), (new, 0, 11, 19)), means)
    pack_side_means(means, side_means)


def tail_kernel(
    f_first,
    new,
    cornered,
    f_own,
    x_in,
    n_in,
    cmid,
    fine_out,
    cpassed,
    halo,
    cfaces,
    clayers,
    meta_own,
    sem,
    out_sem,
):
    device, sign = place()
    (fetch,) = fetch_meta(((f_first, meta_own),), sem)
    pieces = (
        (new, 0, 0, 7 * FR),
        (cornered, 0, 7 * FR, 4 * FR),
        (new, 11 * FR, 11 * FR, 8 * FR),
    )
    outs = [
        pltpu.make_async_copy(
            ref.at[pl.ds(source, rows)], fine_out.at[pl.ds(to, rows)], out_sem.at[k]
        )
        for k, (ref, source, to, rows) in enumerate(pieces)
    ]
    for c in outs:
        c.start()
    gather_halo(f_own, x_in, n_in, EDGES2, halo)
    fetch.wait()
    sides = CoarseSides(meta_own, device, sign)
    for k in (2, 3):
        sides.face(k, halo, cfaces)
    for k in (4, 5):
        sides.layers(k, halo, clayers, 4)
    for i in range(19):
        a = at(cmid, i * CR, CR)
        g = a
        if i in YP2 or i in YM2:
            cy = 1 if i in YP2 else -1
            k = 2 if cy == 1 else 3
            column = -16 * (5 + YP2.index(i)) if cy == 1 else 112 - 16 * (5 + YM2.index(i))
            side = roll(at(cfaces, k * CR, CR), column, 1)
            g = move_y(a, cy, jnp.where(sides.exists(k, CR), side, a), CB)
        elif i in ZP2 or i in ZM2:
            cz = 1 if i in ZP2 else -1
            k = 4 if cz == 1 else 5
            n = (ZP2 if cz == 1 else ZM2).index(i)
            own = a[:8] if cz == 1 else a[-8:]
            side = jnp.where(sides.exists(k, 8), at(clayers, 8 * n, 8), own)
            g = move_z_coarse(a, cz, side)
        put(cpassed, i * CR, g)
    for c in outs:
        c.wait()


def coarse_last_kernel(
    f_first,
    cpassed,
    own,
    two,
    x_in,
    own_sides,
    two_sides,
    x_sides,
    coarse_out,
    gathered,
    sides,
    meta,
    sem,
):
    device, _ = place()
    (fetch,) = fetch_meta(((f_first, meta),), sem)
    put(gathered, 0, own[...])
    put(gathered, K_ROWS, x_in[0:K_ROWS, :])
    put(gathered, 2 * K_ROWS, two[...])
    put(gathered, 3 * K_ROWS, x_in[K_ROWS : 2 * K_ROWS, :])
    put(sides, 0, own_sides[...])
    put(sides, S_ROWS, x_sides[0:S_ROWS, :])
    put(sides, 2 * S_ROWS, two_sides[...])
    put(sides, 3 * S_ROWS, x_sides[S_ROWS : 2 * S_ROWS, :])
    coarse_out[...] = cpassed[...]
    _, lane = iotas(8)
    x = lane & 15
    x_half = (lane >> 3) & 1
    fetch.wait()
    for c in range(CB):
        for qy in range(2):
            children = [number(meta, c, M_CHILD + 2 * qy + qx) for qx in range(2)]
            found = []
            for qx in range(2):
                child = jnp.maximum(children[qx], 0)
                slot = ((child >> 2) ^ device) & 3
                pair, h = (child & 3) >> 1, child & 1
                start = slot * K_ROWS + pair * (19 * 8)
                layers = [at(sides, slot * S_ROWS + pair * 32 + 8 * k, 8) for k in range(4)]
                values = []
                for i in range(19):
                    value = roll(at(gathered, start + 8 * i, 8), (8 * (qx - h)) & 127, 1)
                    for k, group in enumerate((XP, XM)):
                        if i in group:
                            to = 8 * qx + 7 * k
                            shift = (to - 2 * group.index(i) - h) & 127
                            value = jnp.where(x == to, roll(layers[k], shift, 1), value)
                    for k, group in enumerate((YP, YM)):
                        if i in group:
                            shift = (112 * k + 8 * (qx - h) - 16 * group.index(i)) & 127
                            edge = (lane >> 4) == 7 * k
                            value = jnp.where(edge, roll(layers[2 + k], shift, 1), value)
                    values.append(value)
                found.append(values)
            index = jnp.where(x_half == 0, children[0], children[1])
            for i in range(19):
                rows = pl.ds(i * CR + 2 * qy + c, 8, stride=4)
                value = jnp.where(x_half == 0, found[0][i], found[1][i])
                coarse_out[rows, :] = jnp.where(index >= 0, value, cpassed[rows, :])


VMEM = pl.BlockSpec(memory_space=pltpu.VMEM)
HBM = pl.BlockSpec(memory_space=pltpu.HBM)


def rows_of(n, dtype=jnp.float32):
    return jax.ShapeDtypeStruct((n, 128), dtype)


def scratch(n, dtype=jnp.float32):
    return pltpu.VMEM((n, 128), dtype)


def call(kernel, name, specs, outs, scratches, out_specs=None):
    return pl.pallas_call(
        kernel,
        name=name,
        in_specs=specs,
        out_specs=out_specs or [VMEM] * len(outs),
        out_shape=outs,
        scratch_shapes=scratches,
        cost_estimate=pl.CostEstimate(flops=1 << 20, bytes_accessed=4 << 20, transcendentals=0),
        compiler_params=pltpu.CompilerParams(vmem_limit_bytes=32 * 1024 * 1024),
    )


def meta_scratch(n=3):
    return [pltpu.SMEM((8, 128), jnp.float32)] * n + [pltpu.SemaphoreType.DMA((n,))]


def exchange(rows, devices, partner):
    return lax.ppermute(rows, AXES, [(i, partner(i)) for i in range(devices)])


def as_rows(cells, directions):
    blocks = cells.shape[0]
    cells = cells.reshape(blocks, directions, R, 128)
    return cells.transpose(1, 2, 0, 3).reshape(directions * R * blocks, 128)


def as_cells(rows, blocks):
    return rows.reshape(19, R, blocks, 128).transpose(2, 0, 1, 3).reshape(blocks, 19, R * 128)


def on_device(fine_pop, coarse_pop, fine_nbr, coarse_nbr, parent, children, solid):
    devices = lax.axis_size(AXES)
    by_one = lambda a: exchange(a, devices, lambda i: i ^ 1)
    by_two = lambda a: exchange(a, devices, lambda i: i ^ 2)
    odd_even = lambda a: exchange(a, devices, lambda i: (((i + 1) ^ 1) - 1) % devices)
    parent = parent.T
    small = lambda a: pltpu.SMEM(a.shape, jnp.int32)
    in_hbm = lambda a: pltpu.with_memory_space_constraint(a, pltpu.HBM)

    raw, e_own, meta = call(
        coarse_first_kernel,
        "coarse_first",
        [HBM] * 5,
        [rows_of(C_ALL), rows_of(E_ROWS), rows_of(8)],
        [
            small(fine_nbr),
            small(parent),
            small(coarse_nbr),
            small(children),
            pltpu.SemaphoreType.DMA((5,)),
        ],
    )(
        in_hbm(as_rows(coarse_pop, 19)),
        in_hbm(fine_nbr),
        in_hbm(parent),
        in_hbm(coarse_nbr),
        in_hbm(children),
    )
    e_two = by_two(e_own)
    cpost, post, mask, f_own = call(
        fine_first_kernel,
        "fine_first",
        [VMEM, VMEM, HBM, HBM],
        [rows_of(C_ALL), rows_of(F_ALL), rows_of(FR, jnp.int32), rows_of(F_ROWS)],
        [
            scratch(F_ALL),
            scratch(FR, jnp.int32),
            scratch(2 * FR + 8),
            scratch(FR),
            pltpu.SemaphoreType.DMA((2,)),
        ],
    )(meta, raw, in_hbm(as_rows(fine_pop, 19)), in_hbm(as_rows(solid, 1)))

    x_in = by_one(jnp.concatenate([f_own, e_own, e_two]))
    group = (
        e_own[EC_AT:] + x_in[X_E + EC_AT : X_E2] + e_two[EC_AT:] + x_in[X_E2 + EC_AT :]
    )
    n_in = odd_even(
        jnp.concatenate(
            [f_own[:EDGES], f_own[EDGES:META] + x_in[EDGES:META], f_own[META:], group]
        )
    )
    e_halo, ez, local, route = call(
        first_local_kernel,
        "first_local",
        [VMEM] * 6,
        [rows_of(2 * FR), rows_of(80), rows_of(F_ALL), rows_of(64, jnp.int32)],
        [scratch(4 * E_ROWS + R)] + meta_scratch(1),
    )(f_own, e_own, e_two, x_in, post, mask)
    far_edges, ez = lax.optimization_barrier((n_in[EDGES:META], ez))
    x_late = by_one(far_edges)
    new, fixed, plan, cmid, c2_own = call(
        first_sides_kernel,
        "first_sides",
        [VMEM] * 8,
        [
            rows_of(F_ALL),
            rows_of(FR),
            rows_of(FR, jnp.int32),
            rows_of(C_ALL),
            rows_of(2 * FR + R),
        ],
        [scratch(HALO), scratch(4 * FR), scratch(2 * R), scratch(4 * CR), scratch(8)]
        + meta_scratch(),
    )(local, f_own, x_in, n_in, group, cpost, e_halo, route)
    post2, f2_own = call(
        second_collision_kernel,
        "second_collision",
        [VMEM] * 9,
        [rows_of(F_ALL), rows_of(F2_ROWS)],
        [scratch(FR)],
    )(new, mask, f_own, x_in, n_in, x_late, fixed, plan, c2_own)

    x2_in = by_one(f2_own)
    n2_in = odd_even(
        jnp.concatenate([f2_own[:EDGES2], f2_own[EDGES2:] + x2_in[EDGES2:]])
    )
    local2, means = call(
        second_local_kernel,
        "second_local",
        [VMEM] * 3,
        [rows_of(F_ALL), rows_of(K_ROWS)],
        [],
    )(post2, mask, ez)
    k_two = by_two(means)
    far_edges2, local2 = lax.optimization_barrier((n2_in[EDGES2:], local2))
    x2_late = by_one(far_edges2)
    (new2,) = call(
        second_sides_kernel,
        "second_sides",
        [VMEM] * 6,
        [rows_of(F_ALL)],
        [scratch(4 * FR)],
    )(local2, f2_own, x2_in, n2_in, e_halo, route)
    cornered, sides = call(
        coarsen_kernel,
        "coarsen",
        [VMEM] * 7,
        [rows_of(4 * FR), rows_of(S_ROWS)],
        [scratch(K_ROWS), scratch(FR)],
    )(new2, f2_own, x2_in, n2_in, x2_late, fixed, plan)

    k_two, sides = lax.optimization_barrier((k_two, sides))
    sides_two = by_two(sides)
    fine_out, cpassed = call(
        tail_kernel,
        "tail",
        [VMEM] * 7,
        [rows_of(F_ALL), rows_of(C_ALL)],
        [scratch(3 * EDGES2), scratch(4 * CR), scratch(R)]
        + meta_scratch(1)
        + [pltpu.SemaphoreType.DMA((3,))],
        [HBM, VMEM],
    )(f_own, new2, cornered, f2_own, x2_in, n2_in, cmid)
    k_one = by_one(jnp.concatenate([means, k_two]))
    sides_two, cpassed, k_one = lax.optimization_barrier((sides_two, cpassed, k_one))
    sides_one = by_one(jnp.concatenate([sides, sides_two]))
    (coarse_out,) = call(
        coarse_last_kernel,
        "coarse_last",
        [VMEM] * 8,
        [rows_of(C_ALL)],
        [scratch(4 * K_ROWS), scratch(4 * S_ROWS)] + meta_scratch(1),
    )(f_own, cpassed, means, k_two, k_one, sides, sides_two, sides_one)
    return as_cells(fine_out, FB), as_cells(coarse_out, CB)


def solution(mesh):
    rows = P(AXES, None)
    blocks = P(AXES, None, None)
    return jax.shard_map(
        on_device,
        mesh=mesh,
        in_specs=(blocks, blocks, rows, rows, rows, rows, rows),
        out_specs=(blocks, blocks),
        check_vma=False,
    )
```

```python
import jax
import jax.numpy as jnp
from jax import lax
from jax.experimental import pallas as pl
from jax.experimental.pallas import tpu as pltpu
from jax.sharding import PartitionSpec as P

AXES = ("gx", "gy")
VELOCITIES = (
    (0, 0, 0),
    (1, 0, 0),
    (-1, 0, 0),
    (0, 1, 0),
    (0, -1, 0),
    (0, 0, 1),
    (0, 0, -1),
    (1, 1, 0),
    (-1, -1, 0),
    (1, -1, 0),
    (-1, 1, 0),
    (1, 0, 1),
    (-1, 0, -1),
    (1, 0, -1),
    (-1, 0, 1),
    (0, 1, 1),
    (0, -1, -1),
    (0, 1, -1),
    (0, -1, 1),
)
WEIGHTS = (1.0 / 3.0,) + (1.0 / 18.0,) * 6 + (1.0 / 36.0,) * 12
OPPOSITE = (0, 2, 1, 4, 3, 6, 5, 8, 7, 10, 9, 12, 11, 14, 13, 16, 15, 18, 17)
OMEGA_COARSE = 1.6
OMEGA_FINE = 1.0 / (2.0 * (1.0 / 1.6 - 0.5) + 0.5)

XP = (1, 7, 9, 11, 13)
XM = (2, 8, 10, 12, 14)
YP = (3, 7, 10, 15, 17)
YM = (4, 8, 9, 16, 18)
ZP = (5, 11, 14, 15, 18)
ZM = (6, 12, 13, 16, 17)
YP1, YM1 = (3, 15, 17), (4, 16, 18)
YP2, YM2 = (7, 10), (8, 9)
ZP2, ZM2 = (11, 14, 15, 18), (12, 13, 16, 17)


R = 32
FB, CB = 4, 2
FR, CR = FB * R, CB * R
F_ALL, C_ALL = 19 * FR, 19 * CR
PY_AT = FR
ZS = 2 * FR
EDGES = ZS + 8
META = EDGES + R
F_ROWS = META + 8
EDGES2 = ZS + R
F2_ROWS = EDGES2 + R
N_EC = F_ROWS
EC_AT = 4 * R + 40
E_ROWS = EC_AT + 8
K_ROWS = 2 * 19 * 8
S_ROWS = 2 * 32
HALO = 3 * EDGES2
X_E = F_ROWS
X_E2 = X_E + E_ROWS
M_PARENT, M_CNBR, M_CHILD = 4, 8, 16


def iotas(rows=R):
    row = lax.broadcasted_iota(jnp.int32, (rows, 128), 0)
    lane = lax.broadcasted_iota(jnp.int32, (rows, 128), 1)
    return row, lane


def roll(a, shift, axis):
    if isinstance(shift, int):
        shift = shift % a.shape[axis]
        if shift == 0:
            return a
    return pltpu.roll(a, shift, axis)


def at(ref, start, size=R):
    if not isinstance(start, int):
        start = pl.multiple_of(start, 8)
    return ref[pl.ds(start, size), :]


def put(ref, start, value):
    if not isinstance(start, int):
        start = pl.multiple_of(start, 8)
    ref[pl.ds(start, value.shape[0]), :] = value


def zeros(rows):
    return jnp.zeros((rows, 128), jnp.float32)


def total(terms):
    while len(terms) > 1:
        pairs = [terms[k] + terms[k + 1] for k in range(0, len(terms) - 1, 2)]
        terms = pairs + terms[len(terms) - len(terms) % 2 :]
    return terms[0]


def collide(f, rate):
    rho = total(f)
    mom = []
    for axis in range(3):
        plus = [f[i] for i in range(19) if VELOCITIES[i][axis] == 1]
        minus = [f[i] for i in range(19) if VELOCITIES[i][axis] == -1]
        mom.append(total(plus) - total(minus))
    inv = 1.0 / rho
    u = [m * inv for m in mom]
    base = 1.0 - 1.5 * (u[0] * u[0] + u[1] * u[1] + u[2] * u[2])
    scaled = {w: (rate * w) * rho for w in sorted(set(WEIGHTS))}
    keep = 1.0 - rate
    out = [None] * 19
    out[0] = keep * f[0] + scaled[WEIGHTS[0]] * base
    for i in range(1, 19, 2):
        proj = None
        for axis in range(3):
            c = VELOCITIES[i][axis]
            if c:
                term = u[axis]
                if proj is None:
                    proj = term if c > 0 else -term
                else:
                    proj = proj + term if c > 0 else proj - term
        even = base + 4.5 * (proj * proj)
        odd = 3.0 * proj
        w = scaled[WEIGHTS[i]]
        out[i] = keep * f[i] + w * (even + odd)
        out[i + 1] = keep * f[i + 1] + w * (even - odd)
    return out


def collide_rows(src, dst, rows, rate, mask=None, corner=None):
    def body(v, carry):
        f = [at(src, i * rows + v * 16, 16) for i in range(19)]
        if corner is not None:
            edge = at(corner, v * 16, 16)
            f = [with_corners(f[i], i, edge) for i in range(19)]
        post = collide(f, rate)
        if mask is not None:
            solid = (at(mask, v * 16, 16) & 1) > 0
            post = [jnp.where(solid, f[i], post[i]) for i in range(19)]
        for i in range(19):
            put(dst, i * rows + v * 16, post[i])
        return carry

    lax.fori_loop(0, rows // 16, body, 0)


def upper_of(rows, blocks):
    row, _ = iotas(rows)
    return ((row // blocks) & 1) == 1


def swap_halves(a, blocks):
    if blocks == 4:
        rows = a.shape[0]
        return pltpu.roll(a.reshape(rows // 8, 8, 128), 4, 1).reshape(rows, 128)
    return jnp.where(upper_of(a.shape[0], blocks), roll(a, blocks, 0), roll(a, -blocks, 0))


def pack_x(get, packed, first=0):
    _, lane = iotas(packed.shape[0])
    x = lane & 15
    for j in range(5):
        packed = jnp.where(x == first + j, roll(get(XP[j]), first + j - 15, 1), packed)
        packed = jnp.where(x == first + 5 + j, roll(get(XM[j]), first + 5 + j, 1), packed)
    return packed


def pack_y(get, plus, minus, first, rest, blocks):
    rows = rest.shape[0]
    _, lane = iotas(rows)
    upper = upper_of(rows, blocks)
    group = lane >> 4
    packed = zeros(rows)
    for k in range(len(plus)):
        p = first + k
        one = jnp.where(upper, roll(get(plus[k]), 16 * p - 112, 1), roll(get(minus[k]), 16 * p, 1))
        packed = jnp.where(group == p, one, packed)
    packed = swap_halves(packed, blocks)
    return jnp.where((group >= first) & (group < first + len(plus)), packed, rest)


def pack_edges(get, rows):
    _, lane = iotas(rows)
    upper = upper_of(rows, FB)
    first = jnp.where(upper, roll(get(7), -127, 1), get(8))
    second = jnp.where(upper, roll(get(10), 1 - 112, 1), roll(get(9), 1 - 15, 1))
    return swap_halves(jnp.where(lane == 0, first, second), FB)


def move_x(a, cx, halo):
    _, lane = iotas(a.shape[0])
    x = lane & 15
    if cx == 1:
        return jnp.where(x == 0, halo, roll(a, 1, 1))
    return jnp.where(x == 15, halo, roll(a, -1, 1))


def move_y(a, cy, halo, blocks):
    _, lane = iotas(a.shape[0])
    upper = upper_of(a.shape[0], blocks)
    near = roll(a, 16 * cy, 1)
    if cy == 1:
        return jnp.where(lane < 16, jnp.where(upper, swap_halves(near, blocks), halo), near)
    return jnp.where(lane >= 112, jnp.where(upper, halo, swap_halves(near, blocks)), near)


def move_z_coarse(a, cz, halo8):
    row, _ = iotas(8)
    near = roll(a, 4 * cz, 0)
    if cz == 1:
        return jnp.concatenate([jnp.where(row < 4, halo8, near[:8]), near[8:]], axis=0)
    return jnp.concatenate([near[:-8], jnp.where(row >= 4, halo8, near[-8:])], axis=0)


def send_faces(post, out, edges, coarse, spot):
    for h in range(2):
        rows = h * 64
        get = lambda i: at(post, i * FR + rows, 64)
        put(out, rows, pack_x(get, at(coarse, rows, 64)))
        put(out, PY_AT + rows, pack_y(get, YP, YM, 0, at(coarse, PY_AT + rows, 64), FB))
        put(spot, rows, pack_edges(get, 64))
    _, lane = iotas()
    device, _ = place()
    first = 8 * (device & 1)
    packed = zeros(R)
    for b in range(FB):
        one = roll(spot[pl.ds(b, R, stride=FB), :], first + 2 * b, 1)
        packed = jnp.where((lane >> 1) == (first >> 1) + b, one, packed)
    put(out, edges, packed)


def place():
    device = lax.axis_index("gx") * lax.axis_size("gy") + lax.axis_index("gy")
    sign = 1 - 2 * (device & 1)
    return device, sign


def number(meta, row, column):
    return meta[row, column].astype(jnp.int32)


def fetch_meta(pairs, sem):
    copies = [
        pltpu.make_async_copy(ref.at[pl.ds(META, 8)], dst, sem.at[k])
        for k, (ref, dst) in enumerate(pairs)
    ]
    for c in copies:
        c.start()
    return copies


def coarse_first_kernel(
    pop_hbm,
    nbr_hbm,
    parent_hbm,
    cnbr_hbm,
    children_hbm,
    raw,
    e_out,
    meta_out,
    nbr,
    parent,
    cnbr,
    children,
    sem,
):
    copies = [
        pltpu.make_async_copy(src, dst, sem.at[k])
        for k, (src, dst) in enumerate(
            (
                (pop_hbm, raw),
                (nbr_hbm, nbr),
                (parent_hbm, parent),
                (cnbr_hbm, cnbr),
                (children_hbm, children),
            )
        )
    ]
    for c in copies:
        c.start()
    copies[0].wait()
    _, lane = iotas()
    row8, lane8 = iotas(8)
    x = lane & 15
    half = lambda i: at(raw, i * CR)
    for qx in range(2):
        packed = zeros(R)
        for j in range(5):
            packed = jnp.where(x == j, roll(half(XP[j]), j - 8 * qx, 1), packed)
            packed = jnp.where(x == 5 + j, roll(half(XM[j]), 5 + j - 8 * qx - 7, 1), packed)
        put(e_out, qx * R, packed)
    low, high = zeros(R), zeros(R)
    for p in range(5):
        low = jnp.where((lane >> 4) == p, roll(half(YP[p]), 16 * p, 1), low)
        high = jnp.where((lane >> 4) == p, roll(half(YM[p]), 16 * p - 112, 1), high)
    put(e_out, 2 * R, low)
    put(e_out, 3 * R, high)
    for k in range(5):
        e_out[pl.ds(4 * R + 4 * k, 4), :] = raw[pl.ds(ZP[k] * CR, 4), :]
        e_out[pl.ds(4 * R + 20 + 4 * k, 4), :] = raw[pl.ds(ZM[k] * CR + 28, 4), :]
    corner = zeros(8)
    for c in range(CB):
        for q in range(4):
            for e, (i, yq, xq) in enumerate(((7, 7, 0), (10, 7, 7), (9, 0, 0), (8, 0, 7))):
                to = (c * 4 + q) * 4 + e
                rows = raw[pl.ds(i * CR + (q // 2) * 2 + c, 8, stride=4), :]
                rows = roll(rows, to - (yq * 16 + 8 * (q % 2) + xq), 1)
                corner = jnp.where(lane8 == to, rows, corner)
    device, _ = place()
    put(e_out, EC_AT, roll(corner, 32 * (device & 3), 1))

    for c in copies[1:]:
        c.wait()
    meta = zeros(8)
    entries = []
    for b in range(FB):
        entries += [(b, k, nbr[b, k]) for k in range(4)]
        entries += [(b, M_PARENT + k, parent[k, b]) for k in range(2)]
    for c in range(CB):
        entries += [(c, M_CNBR + k, cnbr[c, k]) for k in range(6)]
        entries += [(c, M_CHILD + k, children[c, k]) for k in range(4)]
    for b, k, value in entries:
        meta = jnp.where((row8 == b) & (lane8 == k), value.astype(jnp.float32), meta)
    put(meta_out, 0, meta)


def fine_first_kernel(
    meta,
    raw,
    pop_hbm,
    solid_hbm,
    cpost,
    post,
    mask,
    f_out,
    pop,
    solid,
    coarse,
    spot,
    sem,
):
    copies = [
        pltpu.make_async_copy(pop_hbm, pop, sem.at[0]),
        pltpu.make_async_copy(solid_hbm, solid, sem.at[1]),
    ]
    for c in copies:
        c.start()
    row8, _ = iotas(8)
    collide_rows(raw, cpost, CR, OMEGA_COARSE)
    get = lambda i: at(cpost, i * CR, CR)
    _, wide = iotas(CR)
    ahead, back = zeros(CR), zeros(CR)
    for j in range(5):
        ahead = jnp.where((wide & 15) == 10 + j, roll(get(XP[j]), 10 + j - 15, 1), ahead)
        back = jnp.where((wide & 15) == 10 + j, roll(get(XM[j]), 10 + j, 1), back)
    for k, packed in enumerate((ahead, back)):
        put(spot, 0, packed)
        for c in range(CB):
            coarse[pl.ds(2 * c + k, R, stride=FB), :] = spot[pl.ds(c, R, stride=CB), :]
    put(spot, 0, pack_y(get, YP1, YM1, 5, zeros(CR), CB))
    for c in range(CB):
        coarse[pl.ds(PY_AT + c, R, stride=FB), :] = spot[pl.ds(c, R, stride=CB), :]
        coarse[pl.ds(PY_AT + 2 + c, R, stride=FB), :] = zeros(R)
    top = roll(at(cpost, 6 * CR - 8, 8), 4, 0)
    bottom = roll(at(cpost, 6 * CR, 8), 4, 0)
    put(coarse, 2 * FR, jnp.where(row8 < 4, top, bottom))

    for c in copies:
        c.wait()
    s = jnp.where(solid[...] > 0, 1, 0)
    bits = s
    none = jnp.zeros_like(s)
    by_z = {0: lambda a: a}
    by_z[1] = lambda a: jnp.concatenate([a[-8:], a[:-8]], axis=0)
    by_z[-1] = lambda a: jnp.concatenate([a[8:], a[:8]], axis=0)
    by_y = {cy: move_y(s, cy, none, FB) for cy in (1, -1)}
    by_y[0] = s
    by_x = {(cx, cy): roll(by_y[cy], cx, 1) for cx in (1, -1) for cy in (-1, 0, 1)}
    for i in range(1, 19):
        cx, cy, cz = VELOCITIES[i]
        moved = by_z[cz](by_x[cx, cy] if cx else by_y[cy])
        bits = bits | (moved << i)
    put(mask, 0, bits)
    collide_rows(pop, post, FR, OMEGA_FINE, mask)
    put(f_out, ZS, at(coarse, 2 * FR, 8))
    put(f_out, META, meta[...])
    send_faces(post, f_out, EDGES, coarse, spot)


def onehot(rows, cols, source):
    row = lax.broadcasted_iota(jnp.int32, (rows, cols), 0)
    col = lax.broadcasted_iota(jnp.int32, (rows, cols), 1)
    return jnp.where(row == source(col), 1.0, 0.0).astype(jnp.bfloat16)


def exact_dot(a, b):
    result = None
    for _ in range(3):
        part = a.astype(jnp.bfloat16)
        a = a - part.astype(jnp.float32)
        term = jnp.dot(part, b, preferred_element_type=jnp.float32)
        result = term if result is None else result + term
    return result


def first_local_kernel(
    f_own, e_own, e_two, x_in, post, mask, e_halo, ez, local, route, gathered, meta, sem
):
    device, sign = place()
    (fetch,) = fetch_meta(((f_own, meta),), sem)
    put(gathered, 0, e_own[...])
    put(gathered, E_ROWS, x_in[X_E : X_E + E_ROWS, :])
    put(gathered, 2 * E_ROWS, e_two[...])
    put(gathered, 3 * E_ROWS, x_in[X_E2 : X_E2 + E_ROWS, :])
    row, lane = iotas(16)
    x = lane & 15
    spread_x = onehot(128, 256, lambda m: ((m >> 7) * 4 + ((m & 127) >> 5)) * 16 + (m & 15))
    fetch.wait()
    for b in range(FB):
        p, q = number(meta, b, M_PARENT), number(meta, b, M_PARENT + 1)
        qy, qx = q >> 1, q & 1
        base = (((p >> 1) ^ device) & 3) * E_ROWS + qy * 2 + (p & 1)
        ex = exact_dot(gathered[pl.ds(base + qx * R, 8, stride=4), :], spread_x)
        spread_y = onehot(128, 128, lambda m: (m >> 4) * 16 + 8 * qx + ((m & 15) >> 1))
        ey = exact_dot(
            jnp.concatenate(
                [gathered[pl.ds(base + (2 + k) * R, 8, stride=4), :] for k in range(2)], axis=0
            ),
            spread_y,
        )
        for k in range(2):
            for yh in range(2):
                rows = pl.ds(8 * k + 4 * yh + b, 8, stride=16)
                e_halo[rows, :] = ex[:, 128 * yh : 128 * yh + 128]
                rows = pl.ds(PY_AT + 8 * k + 4 * yh + b, 8, stride=16)
                e_halo[rows, :] = ey[8 * yh : 8 * yh + 8]
        spread_z = onehot(
            128,
            256,
            lambda m: ((m >> 7) * 4 + ((m & 127) >> 5)) * 16 + 8 * qx + ((m & 15) >> 1),
        )
        ezs = exact_dot(gathered[pl.ds(base + 4 * R, 16, stride=4), :], spread_z)
        a0, a1 = ezs[:, :128], ezs[:, 128:]
        moves = {}
        moves[0, 0] = (a0, a1)
        moves[1, 0] = tuple(jnp.where(x == 0, a, roll(a, 1, 1)) for a in (a0, a1))
        moves[-1, 0] = tuple(jnp.where(x == 15, a, roll(a, -1, 1)) for a in (a0, a1))
        moves[0, 1] = (
            jnp.where(lane < 16, a0, roll(a0, 16, 1)),
            jnp.where(lane < 16, roll(a0, 16, 1), roll(a1, 16, 1)),
        )
        moves[0, -1] = (
            jnp.where(lane >= 112, roll(a1, -16, 1), roll(a0, -16, 1)),
            jnp.where(lane >= 112, a1, roll(a1, -16, 1)),
        )
        out = [a0, a1]
        for k, i in enumerate(ZP + ZM):
            moved = moves[VELOCITIES[i][:2]]
            out = [jnp.where(row == k, moved[h], out[h]) for h in range(2)]
        for h in range(2):
            ez[pl.ds(4 * h + b, 8, stride=8), :] = out[h][:8]
            ez[pl.ds(64 + 4 * h + b, 2, stride=8), :] = out[h][8:10]
    plan_faces(meta, device, sign, route)
    stream_local(post, mask, ez, local)


def coarse_means(pieces, means):
    row = lax.broadcasted_iota(jnp.int32, (128, 128), 0)
    col = lax.broadcasted_iota(jnp.int32, (128, 128), 1)
    target = lambda yh, h: (yh * 4 + (row >> 5)) * 16 + ((row & 15) >> 1) + 8 * h
    mats = [
        [jnp.where(col == target(yh, h), 0.125, 0.0).astype(jnp.bfloat16) for yh in range(2)]
        for h in range(2)
    ]
    for pair in range(2):
        for ref, base, first, last in pieces:
            rows = 8 * (last - first)
            total_rows = None
            for h in range(2):
                for yh in range(2):
                    start = (first - base) * FR + 4 * yh + 2 * pair + h
                    z0 = ref[pl.ds(start, rows, stride=16), :]
                    z1 = ref[pl.ds(start + 8, rows, stride=16), :]
                    part = exact_dot(z0 + z1, mats[h][yh])
                    total_rows = part if total_rows is None else total_rows + part
            put(means, pair * 19 * 8 + 8 * first, total_rows)


def pack_side_means(means, out):
    _, lane = iotas(8)
    x = lane & 15
    for pair in range(2):
        get = lambda i: at(means, pair * 19 * 8 + 8 * i, 8)
        packed = [zeros(8) for _ in range(4)]
        for j in range(5):
            for h in range(2):
                to = 2 * j + h
                packed[0] = jnp.where(x == to, roll(get(XP[j]), to - 8 * h, 1), packed[0])
                packed[1] = jnp.where(x == to, roll(get(XM[j]), to - 8 * h - 7, 1), packed[1])
            group = (lane >> 4) == j
            packed[2] = jnp.where(group, roll(get(YP[j]), 16 * j, 1), packed[2])
            packed[3] = jnp.where(group, roll(get(YM[j]), 16 * j - 112, 1), packed[3])
        for k in range(4):
            put(out, pair * 32 + 8 * k, packed[k])


def second_local_kernel(post, mask, ez, local, means):
    stream_local(post, mask, ez, local)
    coarse_means(((local, 0, 0, 19),), means)


def gather_halo(own, x_in, n_in, rows, halo):
    for k, ref in enumerate((n_in, own, x_in)):
        put(halo, k * EDGES2, ref[0:rows, :])


def plan_faces(meta, device, sign, route):
    row, _ = iotas(8)
    for k in range(4):
        slot = jnp.zeros((8, 128), jnp.int32)
        source = jnp.zeros((8, 128), jnp.int32)
        for b in range(FB):
            n = number(meta, b, k)
            safe = jnp.maximum(n, 0)
            which = jnp.clip(((safe >> 2) - device) * sign + 1, 0, 2)
            mine = (row & 3) == b
            slot = jnp.where(mine, safe & 3, slot)
            source = jnp.where(mine, jnp.where(n >= 0, which, 3), source)
        put(route, 16 * k, slot + (row & 4))
        put(route, 16 * k + 8, source)


def gather_faces(route, own, x_in, n_in, e_halo, faces):
    for k in range(4):
        rows, source = at(route, 16 * k, 8), at(route, 16 * k + 8, 8)
        first = PY_AT if k >= 2 else 0
        for v in range(0, FR, 8):
            n, o, x = (
                jnp.take_along_axis(at(ref, first + v, 8), rows, axis=0, mode="promise_in_bounds")
                for ref in (n_in, own, x_in)
            )
            side = jnp.where(source == 0, n, jnp.where(source == 1, o, x))
            put(faces, k * FR + v, jnp.where(source == 3, at(e_halo, first + v, 8), side))


def plan_corners(
    meta_n, meta_own, meta_x, device, sign, e_halo, group, from_n, fixed, plan, spare
):
    row, lane = iotas()
    for k in range(4):
        spare[pl.ds(k, 8, stride=4), :] = group
        spare[pl.ds(R + k, 8, stride=4), :] = from_n
    near_rows, far_rows = spare[0:R, :], spare[R : 2 * R, :]

    def pick(which, row, column):
        return jnp.where(
            which == 0,
            meta_n[row, column],
            jnp.where(which == 1, meta_own[row, column], meta_x[row, column]),
        ).astype(jnp.int32)

    for b in range(FB):
        result = zeros(R)
        source_lanes = jnp.full((R, 128), -1, jnp.int32)
        own_rows = e_halo[pl.ds(PY_AT + b, R, stride=FB), :]
        for side in range(2):
            n = number(meta_own, b, 2 + side)
            safe = jnp.maximum(n, 0)
            which = jnp.clip(((safe >> 2) - device) * sign + 1, 0, 2)
            p, q = (pick(which, safe & 3, M_PARENT + k) for k in range(2))
            rows = jnp.where(which == 0, far_rows, near_rows)
            for end in range(2):
                i = ((7, 10), (9, 8))[side][end]
                own_column = 16 * (YP, YM)[side].index(i) + 15 * end
                edge_column = ((0, 1), (1, 0))[side][end]
                to = 112 * side + 15 * end
                source = 32 * ((p >> 1) & 3) + ((p & 1) * 4 + q) * 4 + 2 * side + end
                value = jnp.where(
                    n < 0, roll(own_rows, to - own_column, 1), roll(rows, (to - source) & 127, 1)
                )
                result = jnp.where(lane == to, value, result)
                m = pick(which, safe & 3, end)
                there = jnp.maximum(m, 0) >> 2
                far = (there - device) * sign
                pair = jnp.where(far >= 2, 2, jnp.where(far < 0, 1, 0))
                column = 16 * pair + 8 * (there & 1) + 2 * (m & 3) + edge_column
                column = jnp.where((n >= 0) & (m >= 0), column, -1)
                here = (lane == to) & ((row & 1) == side)
                source_lanes = jnp.where(here, column, source_lanes)
        fixed[pl.ds(b, R, stride=FB), :] = result
        plan[pl.ds(b, R, stride=FB), :] = source_lanes


def corners(plan, own, x_in, n_in, x_late, at_row, fixed, spot):
    table = at(own, at_row) + at(x_in, at_row)
    table = table + roll(at(n_in, at_row), 16, 1) + roll(x_late[...], 32, 1)
    for b in range(FB):
        spot[pl.ds(b, R, stride=FB), :] = table
    for v in range(0, FR, 8):
        lanes = at(plan, v, 8)
        sent = jnp.take_along_axis(
            at(spot, v, 8), jnp.maximum(lanes, 0), axis=1, mode="promise_in_bounds"
        )
        put(spot, v, jnp.where(lanes >= 0, sent, at(fixed, v, 8)))


def with_corners(cells, i, corner):
    if i not in (7, 8, 9, 10):
        return cells
    row, lane = iotas(cells.shape[0])
    column, upper = {7: (0, 0), 10: (15, 0), 9: (112, 1), 8: (127, 1)}[i]
    return jnp.where((lane == column) & (((row // FB) & 1) == upper), corner, cells)


def stream_local(post, mask, ez, dst):
    put(dst, 0, at(post, 0, FR))
    for h in range(2):
        bits = at(mask, h * 64, 64)
        solid = (bits & 1) > 0
        for i in range(1, 19):
            cx, cy, cz = VELOCITIES[i]
            start = max(h * 64 - 8 * cz, 0)
            stop = min(h * 64 + 64 - 8 * cz, FR)
            size = stop - start
            g = at(post, i * FR + start, size)
            if cx:
                g = roll(g, cx, 1)
            if cy:
                _, lane = iotas(size)
                g = roll(g, 16 * cy, 1)
                g = jnp.where(lane < 16 if cy == 1 else lane >= 112, swap_halves(g, FB), g)
            if size < 64:
                k = ZP.index(i) if cz == 1 else 5 + ZM.index(i)
                layer = at(ez, 8 * k, 8)
                g = jnp.concatenate([layer, g] if cz == 1 else [g, layer], axis=0)
            here = h * 64
            g = jnp.where((bits & (1 << i)) > 0, at(post, OPPOSITE[i] * FR + here, 64), g)
            put(dst, i * FR + here, jnp.where(solid, at(post, i * FR + here, 64), g))


def stream_sides(local, faces, dst):
    for i in range(19):
        cx, cy, cz = VELOCITIES[i]
        for h in range(2):
            here = h * 64
            g = at(local, i * FR + here, 64)
            start = max(here - 8 * cz, 0)
            stop = min(here + 64 - 8 * cz, FR)
            size = stop - start
            if not (cx or cy):
                put(dst, i * FR + here, g)
                continue
            layer = None
            if size < 64:
                layer = g[:8] if cz == 1 else g[-8:]
                g = g[8:] if cz == 1 else g[:-8]
            _, lane = iotas(size)
            if cx:
                face, column = (0, -XP.index(i)) if cx == 1 else (FR, 10 - XM.index(i))
                side = roll(at(faces, face + start, size), column, 1)
                if cy:
                    side = roll(side, 16 * cy, 1)
                    edge = lane < 16 if cy == 1 else lane >= 112
                    side = jnp.where(edge, swap_halves(side, FB), side)
                g = jnp.where((lane & 15) == (0 if cx == 1 else 15), side, g)
            if cy:
                upper = upper_of(size, FB)
                if cy == 1:
                    side = roll(at(faces, 2 * FR + start, size), cx - 16 * YP.index(i), 1)
                    g = jnp.where((lane < 16) & jnp.logical_not(upper), side, g)
                else:
                    side = roll(at(faces, 3 * FR + start, size), 112 + cx - 16 * YM.index(i), 1)
                    g = jnp.where((lane >= 112) & upper, side, g)
            if layer is not None:
                g = jnp.concatenate([layer, g] if cz == 1 else [g, layer], axis=0)
            put(dst, i * FR + here, g)


class CoarseSides:
    def __init__(self, meta, device, sign):
        self.has, self.which, self.slot = [], [], []
        for k in range(6):
            index = [number(meta, c, M_CNBR + k) for c in range(CB)]
            safe = [jnp.maximum(n, 0) for n in index]
            self.has.append(index)
            self.which.append(
                [jnp.clip(((n >> 1) - device) * sign + 1, 0, 2) * EDGES2 for n in safe]
            )
            self.slot.append([n & 1 for n in safe])

    def exists(self, k, rows):
        row, _ = iotas(rows)
        first, second = self.has[k]
        return jnp.where((row & 1) == 0, first, second) >= 0

    def face(self, k, halo, spot):
        for c in range(CB):
            if k < 2:
                start = self.which[k][c] + 2 * self.slot[k][c] + k
            else:
                start = self.which[k][c] + PY_AT + self.slot[k][c]
            spot[pl.ds(k * CR + c, R, stride=CB), :] = halo[pl.ds(start, R, stride=FB), :]

    def layers(self, k, halo, spot, count):
        for c in range(CB):
            for n in range(count):
                start = self.which[k][c] + ZS + 8 * n + 4 * (k - 4) + self.slot[k][c]
                spot[pl.ds(8 * n + 4 * (k - 4) + c, 2, stride=2), :] = halo[
                    pl.ds(start, 2, stride=2), :
                ]


def first_sides_kernel(
    local,
    f_own,
    x_in,
    n_in,
    group,
    cpost,
    e_halo,
    route,
    new,
    fixed,
    plan,
    cmid,
    c_out,
    halo,
    faces,
    spare,
    cfaces,
    clayers,
    meta_n,
    meta_own,
    meta_x,
    sem,
):
    device, sign = place()
    copies = fetch_meta(((n_in, meta_n), (f_own, meta_own), (x_in, meta_x)), sem)
    gather_halo(f_own, x_in, n_in, EDGES, halo)
    put(c_out, 0, zeros(2 * FR))
    gather_faces(route, f_own, x_in, n_in, e_halo, faces)
    stream_sides(local, faces, new)
    for c in copies:
        c.wait()

    row8, _ = iotas(8)
    sides = CoarseSides(meta_own, device, sign)
    for k in range(4):
        sides.face(k, halo, cfaces)
    for k in (4, 5):
        sides.layers(k, halo, clayers, 1)
    put(cmid, 0, at(cpost, 0, CR))
    for i in range(1, 19):
        cx, cy, cz = VELOCITIES[i]
        a = at(cpost, i * CR, CR)
        k = {1: 0, -1: 1}[cx] if cx else {1: 2, -1: 3}[cy] if cy else {1: 4, -1: 5}[cz]
        if cx:
            column = -10 - XP.index(i) if cx == 1 else 5 - XM.index(i)
            side = roll(at(cfaces, k * CR, CR), column, 1)
            g = move_x(a, cx, jnp.where(sides.exists(k, CR), side, a))
        elif cy:
            column = -16 * (5 + YP1.index(i)) if cy == 1 else 112 - 16 * (5 + YM1.index(i))
            side = roll(at(cfaces, k * CR, CR), column, 1)
            g = move_y(a, cy, jnp.where(sides.exists(k, CR), side, a), CB)
        else:
            own = a[:8] if cz == 1 else a[-8:]
            g = move_z_coarse(a, cz, jnp.where(sides.exists(k, 8), clayers[0:8, :], own))
        put(cmid, i * CR, g)
    put(cfaces, 0, pack_y(lambda i: at(cmid, i * CR, CR), YP2, YM2, 5, zeros(CR), CB))
    for c in range(CB):
        c_out[pl.ds(PY_AT + c, R, stride=FB), :] = cfaces[pl.ds(c, R, stride=CB), :]
    for k in range(4):
        top = roll(at(cmid, (ZP2[k] + 1) * CR - 8, 8), 4, 0)
        bottom = roll(at(cmid, ZM2[k] * CR, 8), 4, 0)
        put(c_out, 2 * FR + 8 * k, jnp.where(row8 < 4, top, bottom))

    from_n = at(n_in, N_EC, 8)
    plan_corners(
        meta_n, meta_own, meta_x, device, sign, e_halo, group[...], from_n, fixed, plan, spare
    )


def second_collision_kernel(
    new, mask, f_own, x_in, n_in, x_late, fixed, plan, coarse, post, f_out, spot
):
    put(f_out, ZS, coarse[pl.ds(2 * FR, R), :])
    corners(plan, f_own, x_in, n_in, x_late, EDGES, fixed, spot)
    collide_rows(new, post, FR, OMEGA_FINE, mask, spot)
    send_faces(post, f_out, EDGES2, coarse, spot)


def second_sides_kernel(local, f_own, x_in, n_in, e_halo, route, new, faces):
    gather_faces(route, f_own, x_in, n_in, e_halo, faces)
    stream_sides(local, faces, new)


def coarsen_kernel(
    new,
    f_own,
    x_in,
    n_in,
    x_late,
    fixed,
    plan,
    cornered,
    side_means,
    means,
    spot,
):
    corners(plan, f_own, x_in, n_in, x_late, EDGES2, fixed, spot)
    for i in range(7, 11):
        put(cornered, (i - 7) * FR, with_corners(at(new, i * FR, FR), i, spot[...]))

    coarse_means(((new, 0, 0, 7), (cornered, 7, 7, 11), (new, 0, 11, 19)), means)
    pack_side_means(means, side_means)


def tail_kernel(
    f_first,
    new,
    cornered,
    f_own,
    x_in,
    n_in,
    cmid,
    fine_out,
    cpassed,
    halo,
    cfaces,
    clayers,
    meta_own,
    sem,
    out_sem,
):
    device, sign = place()
    (fetch,) = fetch_meta(((f_first, meta_own),), sem)
    pieces = (
        (new, 0, 0, 7 * FR),
        (cornered, 0, 7 * FR, 4 * FR),
        (new, 11 * FR, 11 * FR, 8 * FR),
    )
    outs = [
        pltpu.make_async_copy(
            ref.at[pl.ds(source, rows)], fine_out.at[pl.ds(to, rows)], out_sem.at[k]
        )
        for k, (ref, source, to, rows) in enumerate(pieces)
    ]
    for c in outs:
        c.start()
    gather_halo(f_own, x_in, n_in, EDGES2, halo)
    fetch.wait()
    sides = CoarseSides(meta_own, device, sign)
    for k in (2, 3):
        sides.face(k, halo, cfaces)
    for k in (4, 5):
        sides.layers(k, halo, clayers, 4)
    for i in range(19):
        a = at(cmid, i * CR, CR)
        g = a
        if i in YP2 or i in YM2:
            cy = 1 if i in YP2 else -1
            k = 2 if cy == 1 else 3
            column = -16 * (5 + YP2.index(i)) if cy == 1 else 112 - 16 * (5 + YM2.index(i))
            side = roll(at(cfaces, k * CR, CR), column, 1)
            g = move_y(a, cy, jnp.where(sides.exists(k, CR), side, a), CB)
        elif i in ZP2 or i in ZM2:
            cz = 1 if i in ZP2 else -1
            k = 4 if cz == 1 else 5
            n = (ZP2 if cz == 1 else ZM2).index(i)
            own = a[:8] if cz == 1 else a[-8:]
            side = jnp.where(sides.exists(k, 8), at(clayers, 8 * n, 8), own)
            g = move_z_coarse(a, cz, side)
        put(cpassed, i * CR, g)
    for c in outs:
        c.wait()


def merge_kernel(f_first, cpassed, own, two, x_in, merged, gathered, meta, sem):
    device, _ = place()
    (fetch,) = fetch_meta(((f_first, meta),), sem)
    put(gathered, 0, own[...])
    put(gathered, K_ROWS, x_in[0:K_ROWS, :])
    put(gathered, 2 * K_ROWS, two[...])
    put(gathered, 3 * K_ROWS, x_in[K_ROWS : 2 * K_ROWS, :])
    merged[...] = cpassed[...]
    _, lane = iotas(8)
    x_half = (lane >> 3) & 1
    fetch.wait()
    for c in range(CB):
        for qy in range(2):
            children = [number(meta, c, M_CHILD + 2 * qy + qx) for qx in range(2)]
            starts, shifts = [], []
            for qx in range(2):
                child = jnp.maximum(children[qx], 0)
                slot = ((child >> 2) ^ device) & 3
                starts.append(slot * K_ROWS + ((child & 3) >> 1) * (19 * 8))
                shifts.append((8 * (qx - (child & 1))) & 127)
            index = jnp.where(x_half == 0, children[0], children[1])
            for i in range(19):
                rows = pl.ds(i * CR + 2 * qy + c, 8, stride=4)
                values = [
                    roll(at(gathered, starts[qx] + 8 * i, 8), shifts[qx], 1) for qx in range(2)
                ]
                value = jnp.where(x_half == 0, values[0], values[1])
                merged[rows, :] = jnp.where(index >= 0, value, cpassed[rows, :])


def coarse_last_kernel(f_first, merged, own, two, x_in, coarse_out, sides, meta, sem):
    device, _ = place()
    (fetch,) = fetch_meta(((f_first, meta),), sem)
    put(sides, 0, own[...])
    put(sides, S_ROWS, x_in[0:S_ROWS, :])
    put(sides, 2 * S_ROWS, two[...])
    put(sides, 3 * S_ROWS, x_in[S_ROWS : 2 * S_ROWS, :])
    coarse_out[...] = merged[...]
    _, lane = iotas(8)
    x = lane & 15
    x_half = (lane >> 3) & 1
    fetch.wait()
    for c in range(CB):
        for qy in range(2):
            changes = {i: [] for i in range(19)}
            for qx in range(2):
                index = number(meta, c, M_CHILD + 2 * qy + qx)
                child = jnp.maximum(index, 0)
                slot = ((child >> 2) ^ device) & 3
                pair, h = (child & 3) >> 1, child & 1
                layers = [at(sides, slot * S_ROWS + pair * 32 + 8 * k, 8) for k in range(4)]
                for k in range(2):
                    to = 8 * qx + 7 * k
                    here = (x == to) & (index >= 0)
                    for n, i in enumerate((XP, XM)[k]):
                        changes[i].append((here, roll(layers[k], (to - 2 * n - h) & 127, 1)))
                    here = ((lane >> 4) == 7 * k) & (x_half == qx) & (index >= 0)
                    for n, i in enumerate((YP, YM)[k]):
                        shift = (112 * k + 8 * (qx - h) - 16 * n) & 127
                        changes[i].append((here, roll(layers[2 + k], shift, 1)))
            for i in range(19):
                if changes[i]:
                    rows = pl.ds(i * CR + 2 * qy + c, 8, stride=4)
                    value = merged[rows, :]
                    for here, change in changes[i]:
                        value = jnp.where(here, change, value)
                    coarse_out[rows, :] = value


VMEM = pl.BlockSpec(memory_space=pltpu.VMEM)
HBM = pl.BlockSpec(memory_space=pltpu.HBM)


def rows_of(n, dtype=jnp.float32):
    return jax.ShapeDtypeStruct((n, 128), dtype)


def scratch(n, dtype=jnp.float32):
    return pltpu.VMEM((n, 128), dtype)


def call(kernel, name, specs, outs, scratches, out_specs=None):
    return pl.pallas_call(
        kernel,
        name=name,
        in_specs=specs,
        out_specs=out_specs or [VMEM] * len(outs),
        out_shape=outs,
        scratch_shapes=scratches,
        cost_estimate=pl.CostEstimate(flops=1 << 20, bytes_accessed=4 << 20, transcendentals=0),
        compiler_params=pltpu.CompilerParams(vmem_limit_bytes=32 * 1024 * 1024),
    )


def meta_scratch(n=3):
    return [pltpu.SMEM((8, 128), jnp.float32)] * n + [pltpu.SemaphoreType.DMA((n,))]


def exchange(rows, devices, partner):
    return lax.ppermute(rows, AXES, [(i, partner(i)) for i in range(devices)])


def as_rows(cells, directions):
    blocks = cells.shape[0]
    cells = cells.reshape(blocks, directions, R, 128)
    return cells.transpose(1, 2, 0, 3).reshape(directions * R * blocks, 128)


def as_cells(rows, blocks):
    return rows.reshape(19, R, blocks, 128).transpose(2, 0, 1, 3).reshape(blocks, 19, R * 128)


def on_device(fine_pop, coarse_pop, fine_nbr, coarse_nbr, parent, children, solid):
    devices = lax.axis_size(AXES)
    by_one = lambda a: exchange(a, devices, lambda i: i ^ 1)
    by_two = lambda a: exchange(a, devices, lambda i: i ^ 2)
    odd_even = lambda a: exchange(a, devices, lambda i: (((i + 1) ^ 1) - 1) % devices)
    parent = parent.T
    small = lambda a: pltpu.SMEM(a.shape, jnp.int32)
    in_hbm = lambda a: pltpu.with_memory_space_constraint(a, pltpu.HBM)

    raw, e_own, meta = call(
        coarse_first_kernel,
        "coarse_first",
        [HBM] * 5,
        [rows_of(C_ALL), rows_of(E_ROWS), rows_of(8)],
        [
            small(fine_nbr),
            small(parent),
            small(coarse_nbr),
            small(children),
            pltpu.SemaphoreType.DMA((5,)),
        ],
    )(
        in_hbm(as_rows(coarse_pop, 19)),
        in_hbm(fine_nbr),
        in_hbm(parent),
        in_hbm(coarse_nbr),
        in_hbm(children),
    )
    e_two = by_two(e_own)
    cpost, post, mask, f_own = call(
        fine_first_kernel,
        "fine_first",
        [VMEM, VMEM, HBM, HBM],
        [rows_of(C_ALL), rows_of(F_ALL), rows_of(FR, jnp.int32), rows_of(F_ROWS)],
        [
            scratch(F_ALL),
            scratch(FR, jnp.int32),
            scratch(2 * FR + 8),
            scratch(FR),
            pltpu.SemaphoreType.DMA((2,)),
        ],
    )(meta, raw, in_hbm(as_rows(fine_pop, 19)), in_hbm(as_rows(solid, 1)))

    x_in = by_one(jnp.concatenate([f_own, e_own, e_two]))
    group = (
        e_own[EC_AT:] + x_in[X_E + EC_AT : X_E2] + e_two[EC_AT:] + x_in[X_E2 + EC_AT :]
    )
    n_in = odd_even(
        jnp.concatenate(
            [f_own[:EDGES], f_own[EDGES:META] + x_in[EDGES:META], f_own[META:], group]
        )
    )
    e_halo, ez, local, route = call(
        first_local_kernel,
        "first_local",
        [VMEM] * 6,
        [rows_of(2 * FR), rows_of(80), rows_of(F_ALL), rows_of(64, jnp.int32)],
        [scratch(4 * E_ROWS + R)] + meta_scratch(1),
    )(f_own, e_own, e_two, x_in, post, mask)
    far_edges, ez = lax.optimization_barrier((n_in[EDGES:META], ez))
    x_late = by_one(far_edges)
    new, fixed, plan, cmid, c2_own = call(
        first_sides_kernel,
        "first_sides",
        [VMEM] * 8,
        [
            rows_of(F_ALL),
            rows_of(FR),
            rows_of(FR, jnp.int32),
            rows_of(C_ALL),
            rows_of(2 * FR + R),
        ],
        [scratch(HALO), scratch(4 * FR), scratch(2 * R), scratch(4 * CR), scratch(8)]
        + meta_scratch(),
    )(local, f_own, x_in, n_in, group, cpost, e_halo, route)
    post2, f2_own = call(
        second_collision_kernel,
        "second_collision",
        [VMEM] * 9,
        [rows_of(F_ALL), rows_of(F2_ROWS)],
        [scratch(FR)],
    )(new, mask, f_own, x_in, n_in, x_late, fixed, plan, c2_own)

    x2_in = by_one(f2_own)
    n2_in = odd_even(
        jnp.concatenate([f2_own[:EDGES2], f2_own[EDGES2:] + x2_in[EDGES2:]])
    )
    local2, means = call(
        second_local_kernel,
        "second_local",
        [VMEM] * 3,
        [rows_of(F_ALL), rows_of(K_ROWS)],
        [],
    )(post2, mask, ez)
    k_two = by_two(means)
    far_edges2, local2 = lax.optimization_barrier((n2_in[EDGES2:], local2))
    x2_late = by_one(far_edges2)
    (new2,) = call(
        second_sides_kernel,
        "second_sides",
        [VMEM] * 6,
        [rows_of(F_ALL)],
        [scratch(4 * FR)],
    )(local2, f2_own, x2_in, n2_in, e_halo, route)
    cornered, sides = call(
        coarsen_kernel,
        "coarsen",
        [VMEM] * 7,
        [rows_of(4 * FR), rows_of(S_ROWS)],
        [scratch(K_ROWS), scratch(FR)],
    )(new2, f2_own, x2_in, n2_in, x2_late, fixed, plan)

    k_two, sides = lax.optimization_barrier((k_two, sides))
    sides_two = by_two(sides)
    fine_out, cpassed = call(
        tail_kernel,
        "tail",
        [VMEM] * 7,
        [rows_of(F_ALL), rows_of(C_ALL)],
        [scratch(3 * EDGES2), scratch(4 * CR), scratch(R)]
        + meta_scratch(1)
        + [pltpu.SemaphoreType.DMA((3,))],
        [HBM, VMEM],
    )(f_own, new2, cornered, f2_own, x2_in, n2_in, cmid)
    k_one = by_one(jnp.concatenate([means, k_two]))
    (merged,) = call(
        merge_kernel,
        "merge",
        [VMEM] * 5,
        [rows_of(C_ALL)],
        [scratch(4 * K_ROWS)] + meta_scratch(1),
    )(f_own, cpassed, means, k_two, k_one)
    sides_two, merged = lax.optimization_barrier((sides_two, merged))
    sides_one = by_one(jnp.concatenate([sides, sides_two]))
    (coarse_out,) = call(
        coarse_last_kernel,
        "coarse_last",
        [VMEM] * 5,
        [rows_of(C_ALL)],
        [scratch(4 * S_ROWS)] + meta_scratch(1),
    )(f_own, merged, sides, sides_two, sides_one)
    return as_cells(fine_out, FB), as_cells(coarse_out, CB)


def solution(mesh):
    rows = P(AXES, None)
    blocks = P(AXES, None, None)
    return jax.shard_map(
        on_device,
        mesh=mesh,
        in_specs=(blocks, blocks, rows, rows, rows, rows, rows),
        out_specs=(blocks, blocks),
        check_vma=False,
    )
```
